32 devices in a mesh: ctx: 16 (over z, x, core), head: 2 (over y).
Axes of the slice: x: 2, y: 2, z: 4, core: 2. Of those that a mesh axis runs over, the one named last changes fastest.
Arguments:
- queries: bfloat16 [2, 4096, 1024], P(None, 'ctx', 'head'), may hold values from -64 to 64
- keys: bfloat16 [2, 4096, 1024], P(None, 'ctx', 'head'), may hold values from -4 to 4
- values: bfloat16 [2, 4096, 1024], P(None, 'ctx', 'head'), may hold values from -5 to 5
- gates: bfloat16 [2, 4096, 1024], P(None, 'ctx', 'head'), may hold values from -4 to 4
- token_rates: float32 [4096, 2], P('ctx', 'head'), may hold values from 0.05 to 1
- fast_init: bfloat16 [2, 512, 768], P('head', 'ctx'), may hold values from -0.25 to 0.25
- fast_rate: float32 [2], P('head'), may hold values from 0.3 to 1
- norm_gain: float32 [1024], replicated, may hold values from 0.5 to 1.5
Outputs:
- normed: bfloat16 [2, 4096, 1024], P(None, ('ctx', 'head'))
The draws below stay inside these ranges and needn't reach their ends.
All inputs are finite; a program needn't handle non-finite values.
Results may differ from the reference program's by a relative error of at most 0.02.
Values may be sent and summed in bfloat16 or wider, within the bound.
No kernel may reach another device: no remote copies, remote signals or barrier semaphores. Data moves between devices by JAX's collectives and lax.ppermute only.
A program may use at most 64 MiB of HBM per device.

```python
import math
import jax
import jax.numpy as jnp
from jax import lax

ROWS = 256
HD = 512
FH = 256
WIN = 1024
HEADS = 2
D = 1024
GROUP = 4096


def query_key_pair(key):
    query_draw = jax.random.truncated_normal(jax.random.fold_in(key, 11), -4.0, 4.0, (2, GROUP, D), jnp.float32)
    key_draw = jax.random.truncated_normal(jax.random.fold_in(key, 12), -4.0, 4.0, (2, GROUP, D), jnp.float32)
    return (query_draw, key_draw)


def draw_queries(key, part):
    return query_key_pair(key)[0].astype(jnp.bfloat16)


def draw_keys(key, part):
    return query_key_pair(key)[1].astype(jnp.bfloat16)


def block_scale(key, dims, shards, least, top_value):
    gain = 1.0
    for position, blocks in shards:
        draws = jax.random.uniform(jax.random.fold_in(jax.random.fold_in(key, 6), position), (blocks,), jnp.float32, least / len(shards), top_value / len(shards))
        gain = gain * jnp.repeat(jnp.exp(draws), dims[position] // blocks).reshape((-1,) + (1,) * (len(dims) - 1 - position))
    return gain


def normal_values(rng, shape, scale, limit, pieces=(), kind=jnp.bfloat16):
    entries = scale * jax.random.normal(rng, shape, jnp.float32)
    if pieces:
        entries = entries * block_scale(rng, shape, pieces, -0.22, 0.18)
    return jnp.clip(entries, -limit, limit).astype(kind)


def setup_inputs(seed: int = 0) -> dict:
    splits = jax.random.split(jax.random.key(seed), 9)
    queries = draw_queries(jax.random.fold_in(splits[8], 71), 0)
    keys = draw_keys(jax.random.fold_in(splits[8], 71), 0)
    values = normal_values(splits[2], (2, GROUP, D), 1.0, 5.0, ((1, 16), (2, 2)))
    gates = normal_values(splits[3], (2, GROUP, D), 1.0, 4.0, ((1, 16), (2, 2)))
    token_rates = jnp.clip(jnp.exp(math.log(1.0) - 2.9957323 * jax.random.uniform(splits[4], (GROUP, HEADS), jnp.float32) ** block_scale(splits[4], (GROUP, HEADS), ((0, 16), (1, 2)), -0.2, 0.2)), 0.05, 1.0)
    fast_init = normal_values(splits[5], (HEADS, HD, 3 * FH), HD ** -0.5, 0.25, ((0, 2), (1, 16)))
    fast_rate = jnp.clip(jnp.exp(math.log(1.0) - 1.2039728 * jax.random.uniform(splits[6], (HEADS,), jnp.float32) ** block_scale(splits[6], (HEADS,), ((0, 2),), -0.2, 0.2)), 0.3, 1.0)
    norm_gain = jnp.clip(1.0 + 0.1 * jax.random.normal(splits[7], (D,), jnp.float32), 0.5, 1.5)
    return dict(queries=queries, keys=keys, values=values, gates=gates, token_rates=token_rates, fast_init=fast_init, fast_rate=fast_rate, norm_gain=norm_gain)


A_COEF = 3.4445
B_COEF = -4.775
C_COEF = 2.0315

def window_attention(query_seq, key_seq, value_seq):
    reach = (WIN - 1) // ROWS + 1
    head_dim = query_seq.shape[1]
    blocks = query_seq.shape[0] // ROWS
    query_wide = query_seq.astype(jnp.float32)
    lead = jnp.zeros((reach * ROWS, head_dim), jnp.float32)
    key_padded = jnp.concatenate([lead, key_seq.astype(jnp.float32)], 0)
    value_padded = jnp.concatenate([lead, value_seq.astype(jnp.float32)], 0)
    span = (reach + 1) * ROWS
    row_pos = jnp.arange(ROWS)[:, None]
    rel_pos = (jnp.arange(span) - reach * ROWS)[None, :]
    base_ok = (rel_pos <= row_pos) & (rel_pos > row_pos - WIN)

    def one_block(block_index):
        start = (block_index * ROWS).astype(jnp.int32)
        query_rows = lax.dynamic_slice_in_dim(query_wide, start, ROWS, 0)
        key_rows = lax.dynamic_slice_in_dim(key_padded, start, span, 0)
        value_rows = lax.dynamic_slice_in_dim(value_padded, start, span, 0)
        global_pos = start - reach * ROWS + jnp.arange(span).astype(jnp.int32)
        allowed = base_ok & (global_pos >= 0)[None, :]
        scores = jnp.dot(query_rows, key_rows.T) * head_dim ** (-0.5)
        scores = jnp.where(allowed, scores, -1e+30)
        row_max = lax.optimization_barrier(jnp.max(scores, -1, keepdims=True))
        exp_scores = jnp.where(allowed, jnp.exp(scores - row_max), 0.0)
        row_total = lax.optimization_barrier(jnp.sum(exp_scores, -1, keepdims=True))
        rounded = lax.optimization_barrier(exp_scores.astype(jnp.bfloat16)).astype(jnp.float32)
        return jnp.dot(rounded, value_rows) / row_total
    outs = lax.map(one_block, jnp.arange(blocks, dtype=jnp.int32))
    return outs.reshape(-1, head_dim)

def fast_hidden(inputs, weights):
    block_width = weights.shape[1] // 3
    gate_up = jnp.dot(inputs, weights[:, :2 * block_width], preferred_element_type=jnp.float32)
    gate_part = gate_up[:, :block_width]
    up_part = gate_up[:, block_width:]
    hidden = (jax.nn.silu(gate_part) * up_part).astype(jnp.bfloat16)
    return (gate_part, up_part, hidden)

def fast_apply(inputs, weights):
    block_width = weights.shape[1] // 3
    gate_part, up_part, hidden = fast_hidden(inputs, weights)
    return lax.dot_general(hidden, weights[:, 2 * block_width:], (((1,), (1,)), ((), ())), preferred_element_type=jnp.float32)

def fast_gradient(key_rows, value_rows, rate_rows, weights):
    block_width = weights.shape[1] // 3
    gate_part, up_part, hidden = fast_hidden(key_rows, weights)
    target = (-rate_rows * value_rows.astype(jnp.float32)).astype(jnp.bfloat16)
    out_grad = lax.dot_general(target, hidden, (((0,), (0,)), ((), ())), preferred_element_type=jnp.float32)
    hidden_grad = jnp.dot(target, weights[:, 2 * block_width:], preferred_element_type=jnp.float32)
    sigmoid_g = jax.nn.sigmoid(gate_part)
    gate_grad = hidden_grad * up_part * sigmoid_g * (1.0 + gate_part * (1.0 - sigmoid_g))
    up_grad = hidden_grad * jax.nn.silu(gate_part)
    joined = jnp.concatenate([gate_grad, up_grad], 1).astype(jnp.bfloat16)
    in_grad = lax.dot_general(key_rows, joined, (((0,), (0,)), ((), ())), preferred_element_type=jnp.float32)
    return jnp.concatenate([in_grad, out_grad], 1)

def orthogonalize(gradient):
    rows_count = gradient.shape[0]
    block_width = gradient.shape[1] // 3
    blocks = gradient.reshape(rows_count, 3, block_width)
    block_norms = jnp.sqrt(lax.optimization_barrier(jnp.sum(blocks * blocks, axis=(0, 2))))
    ortho = (blocks / (block_norms[None, :, None] + 1e-06)).astype(jnp.bfloat16)
    for turn_index in range(3):
        ortho_wide = ortho.astype(jnp.float32)
        gram_mat = jnp.einsum('rmf,rmg->mfg', ortho_wide, ortho_wide)
        gram_low = lax.optimization_barrier(gram_mat.astype(jnp.bfloat16)).astype(jnp.float32)
        square = jnp.einsum('mfg,mgh->mfh', gram_low, gram_low)
        mixer_low = lax.optimization_barrier((B_COEF * gram_mat + C_COEF * square).astype(jnp.bfloat16))
        mixer_mat = mixer_low.astype(jnp.float32)
        ortho = (A_COEF * ortho_wide + jnp.einsum('rmf,mfg->rmg', ortho_wide, mixer_mat)).astype(jnp.bfloat16)
    return ortho.reshape(rows_count, 3 * block_width)

def renew(initial, ortho, rate_value):
    anchor = initial.astype(jnp.float32)
    updated = anchor - rate_value * ortho.astype(jnp.float32)
    first_norm = jnp.sqrt(lax.optimization_barrier(jnp.sum(anchor * anchor, 0)))
    updated_norm = jnp.sqrt(lax.optimization_barrier(jnp.sum(updated * updated, 0)))
    return (updated * (first_norm / (updated_norm + 1e-06))).astype(jnp.bfloat16)

def reference(queries, keys, values, gates, token_rates, fast_init, fast_rate, norm_gain):
    query_seq = queries.reshape(2 * GROUP, D)
    key_seq = keys.reshape(2 * GROUP, D)
    value_seq = values.reshape(2 * GROUP, D)
    gate_seq = gates.reshape(2 * GROUP, D)
    outputs = []
    for head_index in range(HEADS):
        low_col = head_index * HD
        high_col = low_col + HD
        window_out = window_attention(query_seq[:, low_col:high_col], key_seq[:, low_col:high_col], value_seq[:, low_col:high_col])
        weights = fast_init[head_index]
        gradient = fast_gradient(keys[0][:, low_col:high_col], values[0][:, low_col:high_col], token_rates[:, head_index:head_index + 1], weights)
        renewed = renew(weights, orthogonalize(gradient), fast_rate[head_index])
        fast_out = jnp.concatenate([fast_apply(queries[0][:, low_col:high_col], weights), fast_apply(queries[1][:, low_col:high_col], renewed)], 0)
        combined = window_out + fast_out
        gate_vals = gate_seq[:, low_col:high_col].astype(jnp.float32)
        outputs.append((combined * jax.nn.silu(gate_vals)).astype(jnp.bfloat16))
    gated_all = jnp.concatenate(outputs, 1).astype(jnp.float32)
    inv_rms = lax.rsqrt(lax.optimization_barrier(jnp.mean(gated_all * gated_all, -1, keepdims=True)) + 1e-06)
    normed = (gated_all * inv_rms * norm_gain).astype(jnp.bfloat16)
    return normed.reshape(2, GROUP, D)
```

```python
import functools

import jax
import jax.numpy as jnp
from jax import lax
from jax.experimental import pallas as pl
from jax.experimental.pallas import tpu as pltpu
from jax.sharding import PartitionSpec as P

WIN = 1024
A_COEF = 3.4445
B_COEF = -4.775
C_COEF = 2.0315
BF = jnp.bfloat16
F32 = jnp.float32
VMEM_LIMIT = 48 * 1024 * 1024


def dot_nn(a, b):
    return lax.dot_general(a, b, (((1,), (0,)), ((), ())), preferred_element_type=F32)


def dot_nt(a, b):
    return lax.dot_general(a, b, (((1,), (1,)), ((), ())), preferred_element_type=F32)


def dot_tn(a, b):
    return lax.dot_general(a, b, (((0,), (0,)), ((), ())), preferred_element_type=F32)


def swapped(value, mask, axis="ctx"):
    count = lax.axis_size(axis)
    return lax.ppermute(value, axis, [(i, i ^ mask) for i in range(count)])


def vmem_spec():
    return pl.BlockSpec(memory_space=pltpu.VMEM)


def call(body, args, outs, scratch=(), cost=None):
    return pl.pallas_call(
        body,
        out_shape=outs,
        in_specs=[pl.BlockSpec(memory_space=pltpu.SMEM)] + [vmem_spec()] * (len(args) - 1),
        out_specs=jax.tree.map(lambda _: vmem_spec(), outs),
        scratch_shapes=list(scratch),
        compiler_params=pltpu.CompilerParams(vmem_limit_bytes=VMEM_LIMIT),
        cost_estimate=cost,
    )(*args)


def cost_of(flops, moved):
    return pl.CostEstimate(flops=int(flops), bytes_accessed=int(moved), transcendentals=0)


def silu(v):
    return v / (1.0 + jnp.exp(-v))


def gradient_body(planes, ids, mine, other, pair_a, pair_b, send, keep, weights, total):
    plane, side = ids[0], ids[1]
    rows = mine.shape[1]
    for m in range(planes):
        base = ((plane ^ m) * 2) * rows
        weights[pl.ds(pl.multiple_of(base + side * rows, rows), rows), :] = mine[m]
        weights[pl.ds(pl.multiple_of(base + (1 - side) * rows, rows), rows), :] = other[m]
    half = weights.shape[1] // 3
    gate_up_w = weights[:, : 2 * half]
    out_w = weights[:, 2 * half :]
    first = None
    for pair in (pair_a, pair_b):
        key_rows, target = pair[0], pair[1]
        gate_up = dot_nn(key_rows, gate_up_w)
        g, u = gate_up[:, :half], gate_up[:, half:]
        dh = dot_nn(target, out_w)
        s = 1.0 / (1.0 + jnp.exp(-g))
        gs = g * s
        hidden = (gs * u).astype(BF)
        dg = dh * u * s * (1.0 + g * (1.0 - s))
        du = dh * gs
        joined = jnp.concatenate([dg, du], 1).astype(BF)
        in_grad = dot_tn(joined, key_rows)
        out_grad = dot_tn(hidden, target)
        first = (in_grad, out_grad) if first is None else (first[0] + in_grad, first[1] + out_grad)
    total[: 2 * half, :] = first[0]
    total[2 * half : 3 * half, :] = first[1]
    if total.shape[0] > 3 * half:
        total[3 * half :, :] = jnp.zeros((total.shape[0] - 3 * half, total.shape[1]), F32)
    part = send.shape[0]
    send[...] = total[pl.ds(pl.multiple_of((1 - side) * part, part), part), :].astype(BF)
    keep[...] = total[pl.ds(pl.multiple_of(side * part, part), part), :]


def side_sum_body(planes, ids, keep, got, *refs):
    outs, total = refs[:planes], refs[planes]
    plane = ids[0]
    total[...] = keep[...] + got[...].astype(F32)
    part = outs[0].shape[0]
    for m in range(planes):
        rows = total[pl.ds(pl.multiple_of((plane ^ m) * part, part), part), :]
        outs[m][...] = rows.astype(outs[m].dtype)


def plane_sum_body(ids, own, *refs):
    total = own[...]
    for ref in refs[:-1]:
        total = total + ref[...].astype(F32)
    refs[-1][...] = total.astype(BF)


def weights_body(planes, ids, mine, other, beside, whole, flipped, norms):
    plane, side, core = ids[0], ids[1], ids[2]
    rows = mine.shape[1]
    half = mine.shape[2] // 3
    for m in range(planes):
        for far in range(2):
            base = ((plane ^ m) * 2 + (side if far == 0 else 1 - side)) * rows
            block_k = (mine, other)[far][m]
            block_c = beside[far * planes + m]
            low = jnp.where(core == 0, block_k, block_c)
            high = jnp.where(core == 0, block_c, block_k)
            where = pl.ds(pl.multiple_of(base, rows), rows)
            for b in range(3):
                whole[where, 2 * b * half : (2 * b + 1) * half] = low[:, b * half : (b + 1) * half]
                whole[where, (2 * b + 1) * half : (2 * b + 2) * half] = high[
                    :, b * half : (b + 1) * half
                ]
    width = whole.shape[1]
    for b in range(3):
        cols = slice(b * width // 3, (b + 1) * width // 3)
        turned = whole[:, cols].astype(F32).T
        flipped[cols, :] = turned
        norms[cols, :] = jnp.sqrt(jnp.sum(turned * turned, 1, keepdims=True))


def window(ids, q, k_own, v_own, first_group, far_pair, full_pairs):
    rows, depth = q.shape
    scale = depth**-0.5
    row = lax.broadcasted_iota(jnp.int32, (rows, rows), 0)
    col = lax.broadcasted_iota(jnp.int32, (rows, rows), 1)
    blocks = [(k_own, v_own, col <= row)]
    far_ok = col > row
    for keys, values, live in [far_pair] + full_pairs:
        allowed = far_ok if keys is far_pair[0] else None
        if first_group:
            alive = jnp.full((rows, rows), live, jnp.int32) != 0
            allowed = alive if allowed is None else allowed & alive
        blocks.append((keys, values, allowed))
    scores = []
    for keys, values, allowed in blocks:
        s = dot_nt(q, keys) * scale
        scores.append(s if allowed is None else jnp.where(allowed, s, -1e30))
    top = jnp.max(scores[0], -1, keepdims=True)
    for s in scores[1:]:
        top = jnp.maximum(top, jnp.max(s, -1, keepdims=True))
    total = None
    out = None
    for s, (keys, values, allowed) in zip(scores, blocks):
        e = jnp.exp(s - top)
        t = jnp.sum(e, -1, keepdims=True)
        o = dot_nn(e.astype(BF), values)
        total = t if total is None else total + t
        out = o if out is None else out + o
    return out / total


def live_flags(ids):
    plane, side, core = ids[0], ids[1], ids[2]
    later = (plane > 0).astype(jnp.int32)
    side_live = jnp.maximum(later, side)
    core_live = jnp.maximum(later, core)
    return later, side_live, core_live


def first_group_body(ids, q, k_own, v_own, far, near, core, gates, whole, out):
    later, side_live, core_live = live_flags(ids)
    pairs = [
        (near[0], near[1], side_live),
        (core[0], core[1], core_live),
        (core[2], core[3], side_live),
    ]
    win = window(ids, q[0], k_own[0], v_own[0], True, (far[0], far[1], later), pairs)
    width = whole.shape[1] // 3
    gate_up = dot_nn(q[0], whole[:, : 2 * width])
    hidden = (silu(gate_up[:, :width]) * gate_up[:, width:]).astype(BF)
    fast = dot_nt(hidden, whole[:, 2 * width :])
    gate = gates[0].astype(F32)
    out[...] = ((win + fast) * silu(gate)).astype(BF)


def second_group_body(ids, q, k_own, v_own, far, near, core, out):
    pairs = [(near[0], near[1], 1), (core[0], core[1], 1), (core[2], core[3], 1)]
    out[...] = window(ids, q[0], k_own[0], v_own[0], False, (far[0], far[1], 1), pairs)


def group_call(body, index, ids, grouped, others, outs, cost):
    def spec(a):
        tail = (0,) * (a.ndim - 1)
        return pl.BlockSpec((1,) + a.shape[1:], lambda i: (index,) + tail)

    def full(a):
        return pl.BlockSpec(a.shape, lambda i, nd=a.ndim: (0,) * nd)

    specs, args = [], []
    for a, is_grouped in grouped:
        specs.append(spec(a) if is_grouped else full(a))
        args.append(a)
    for a in others:
        specs.append(full(a))
        args.append(a)
    return pl.pallas_call(
        body,
        grid=(1,),
        out_shape=outs,
        in_specs=[pl.BlockSpec(memory_space=pltpu.SMEM)] + specs,
        out_specs=pl.BlockSpec(outs.shape, lambda i: (0,) * len(outs.shape)),
        compiler_params=pltpu.CompilerParams(vmem_limit_bytes=VMEM_LIMIT),
        cost_estimate=cost,
    )(ids, *args)


def update_body(planes, ids, rate, mine, other, flipped, norms, q, win, gates, out, grads):
    plane, side, core = ids[0], ids[1], ids[2]
    part = mine.shape[1]
    for m in range(planes):
        for far in range(2):
            base = ((side if far == 0 else 1 - side) * planes + (plane ^ m)) * part
            where = pl.ds(pl.multiple_of(base, part), part)
            grads[core, where, :] = mine[far * planes + m]
            grads[1 - core, where, :] = other[far * planes + m]
    width = flipped.shape[0] // 3
    half = width // 2
    turned = []
    for b in range(3):
        block = jnp.concatenate(
            [grads[0, b * half : (b + 1) * half, :], grads[1, b * half : (b + 1) * half, :]], 0
        ).astype(F32)
        length = jnp.sqrt(jnp.sum(block * block, keepdims=True))
        turned.append((block / (length + 1e-06)).astype(BF))
    for _ in range(3):
        grams = [dot_nt(y, y) for y in turned]
        lows = [a.astype(BF) for a in grams]
        squares = [dot_nn(a, a) for a in lows]
        mixers = [(B_COEF * a + C_COEF * s).astype(BF) for a, s in zip(grams, squares)]
        turned = [
            (A_COEF * y.astype(F32) + dot_nn(b, y)).astype(BF) for b, y in zip(mixers, turned)
        ]
    fresh = []
    for b in range(3):
        cols = slice(b * width, (b + 1) * width)
        moved = flipped[cols, :] - rate[0] * turned[b].astype(F32)
        length = jnp.sqrt(jnp.sum(moved * moved, 1, keepdims=True))
        fresh.append((moved * (norms[cols, :] / (length + 1e-06))).astype(BF))
    x = q[...]
    g = dot_nt(x, fresh[0])
    u = dot_nt(x, fresh[1])
    hidden = (silu(g) * u).astype(BF)
    fast = dot_nn(hidden, fresh[2])
    gate = gates[...].astype(F32)
    out[...] = ((win[...] + fast) * silu(gate)).astype(BF)


def norm_body(ids, own, got, gain, out):
    head = ids[3]
    rows, depth = own.shape
    a = own[...].astype(F32)
    b = got[...].astype(F32)
    low = jnp.where(head == 0, a, b)
    high = jnp.where(head == 0, b, a)
    square = jnp.sum(a * a, -1, keepdims=True) + jnp.sum(b * b, -1, keepdims=True)
    inv = lax.rsqrt(square / (2 * depth) + 1e-06)
    out[:, :depth] = (low * inv * gain[:, :depth]).astype(BF)
    out[:, depth:] = (high * inv * gain[:, depth:]).astype(BF)


def finished(ids, gated, norm_gain):
    heads = lax.axis_size("head")
    rows = gated.shape[0] // heads
    if heads == 2:
        own_head = lax.axis_index("head")
        low, high = gated[:rows], gated[rows:]
        own = jnp.where(own_head == 0, low, high)
        got = swapped(jnp.where(own_head == 0, high, low), 1, "head")
        return call(
            norm_body,
            (ids, own, got, norm_gain[None, :]),
            jax.ShapeDtypeStruct((rows, norm_gain.shape[0]), BF),
            cost=cost_of(0, 4 * rows * norm_gain.shape[0]),
        )
    wide = lax.all_to_all(gated, "head", split_axis=0, concat_axis=1, tiled=True).astype(F32)
    inv = lax.rsqrt(jnp.mean(wide * wide, -1, keepdims=True) + 1e-06)
    return (wide * inv * norm_gain).astype(BF)


def shards(queries, keys, values, gates, token_rates, fast_init, fast_rate, norm_gain):
    count = lax.axis_size("ctx")
    rows, depth = queries.shape[1], queries.shape[2]
    reach = (WIN - 1) // rows + 1
    planes = count // reach
    if reach != 4 or WIN % rows or planes * reach != count or planes & (planes - 1):
        raise ValueError("unsupported shapes")
    position = lax.axis_index("ctx")
    plane, side, core = position // 4, (position // 2) % 2, position % 2
    ids = jnp.stack([plane, side, core, lax.axis_index("head")]).astype(jnp.int32)
    width = fast_init.shape[2] // 3
    half = width // 2

    local = fast_init[0]
    fast_rows = local.shape[0]
    split = local.reshape(fast_rows, 3, 2, half)
    low, high = split[:, :, 0].reshape(fast_rows, -1), split[:, :, 1].reshape(fast_rows, -1)
    mine = jnp.where(core == 0, low, high)
    theirs = swapped(jnp.where(core == 0, high, low), 1)
    pair = jnp.concatenate(
        [jnp.where(core == 0, mine, theirs), jnp.where(core == 0, theirs, mine)], 0
    )
    target = (-token_rates * values[0].astype(F32)).astype(BF)
    grad_pair = jnp.stack([keys[0], target])
    grad_other = swapped(grad_pair, 1)
    mine_w = jnp.stack([pair] + [swapped(pair, 4 * m) for m in range(1, planes)])
    other_w = swapped(mine_w, 2)

    pieces = 2 * planes
    part = -(-3 * half // (16 * pieces)) * 16
    send, keep = call(
        functools.partial(gradient_body, planes),
        (ids, mine_w, other_w, grad_pair, grad_other),
        (
            jax.ShapeDtypeStruct((planes * part, depth), BF),
            jax.ShapeDtypeStruct((planes * part, depth), F32),
        ),
        scratch=(pltpu.VMEM((depth, 3 * half), BF), pltpu.VMEM((pieces * part, depth), F32)),
        cost=cost_of(2 * 2 * rows * depth * half * 6, 4 * rows * depth * 4),
    )
    got = swapped(send, 2)
    parts = call(
        functools.partial(side_sum_body, planes),
        (ids, keep, got),
        tuple(jax.ShapeDtypeStruct((part, depth), F32 if m == 0 else BF) for m in range(planes)),
        scratch=(pltpu.VMEM((planes * part, depth), F32),),
        cost=cost_of(0, planes * part * depth * 8),
    )
    arrived = [swapped(parts[m], 4 * m) for m in range(1, planes)]
    total = call(
        plane_sum_body,
        (ids, parts[0], *arrived),
        jax.ShapeDtypeStruct((part, depth), BF),
        cost=cost_of(0, planes * part * depth * 3),
    )
    stacked = jnp.stack([total] + [swapped(total, 4 * m) for m in range(1, planes)])
    side_grad = jnp.concatenate([stacked, swapped(stacked, 2)], 0)
    core_grad = swapped(side_grad, 1)

    last = plane == planes - 1
    windows = []
    for g in range(2):
        own = jnp.stack([keys[g], values[g]])
        if g == 0:
            pairs = [(i, i + reach) for i in range(count - reach)]
            far = lax.ppermute(own, "ctx", pairs)
        else:
            first = jnp.stack([keys[0], values[0]])
            pairs = [(i, (i + reach) % count) for i in range(count)]
            far = lax.ppermute(jnp.where(last, first, own), "ctx", pairs)
        near = swapped(jnp.where(side == 0, own, far), 2)
        beside = swapped(jnp.concatenate([jnp.where(core == 0, own, far), near], 0), 1)
        windows.append((far, near, beside))

    half_w = jnp.concatenate([mine_w, other_w], 0)
    beside_w = swapped(half_w, 1)
    whole, flipped, norms = call(
        functools.partial(weights_body, planes),
        (ids, mine_w, other_w, beside_w),
        (
            jax.ShapeDtypeStruct((depth, 3 * width), BF),
            jax.ShapeDtypeStruct((3 * width, depth), F32),
            jax.ShapeDtypeStruct((3 * width, 1), F32),
        ),
        cost=cost_of(0, depth * width * 3 * 8),
    )
    attn_flops = 4 * rows * depth * 5 * rows
    far, near, beside = windows[0]
    gated_first = group_call(
        first_group_body,
        0,
        ids,
        [(queries, True), (keys, True), (values, True)]
        + [(far, False), (near, False), (beside, False)]
        + [(gates, True)],
        [whole],
        jax.ShapeDtypeStruct((rows, depth), BF),
        cost_of(attn_flops * 2, rows * depth * 30),
    )
    far, near, beside = windows[1]
    window_second = group_call(
        second_group_body,
        1,
        ids,
        [(queries, True), (keys, True), (values, True)]
        + [(far, False), (near, False), (beside, False)],
        [],
        jax.ShapeDtypeStruct((rows, depth), F32),
        cost_of(attn_flops * 2, rows * depth * 30),
    )
    done_first = finished(ids, gated_first, norm_gain)

    gated_second = pl.pallas_call(
        functools.partial(update_body, planes),
        grid=(1,),
        out_shape=jax.ShapeDtypeStruct((rows, depth), BF),
        in_specs=[
            pl.BlockSpec(memory_space=pltpu.SMEM),
            pl.BlockSpec(memory_space=pltpu.SMEM),
            pl.BlockSpec(side_grad.shape, lambda i: (0, 0, 0)),
            pl.BlockSpec(core_grad.shape, lambda i: (0, 0, 0)),
            pl.BlockSpec(flipped.shape, lambda i: (0, 0)),
            pl.BlockSpec(norms.shape, lambda i: (0, 0)),
            pl.BlockSpec((None, rows, depth), lambda i: (1, 0, 0)),
            pl.BlockSpec((rows, depth), lambda i: (0, 0)),
            pl.BlockSpec((None, rows, depth), lambda i: (1, 0, 0)),
        ],
        out_specs=pl.BlockSpec((rows, depth), lambda i: (0, 0)),
        scratch_shapes=[pltpu.VMEM((2, pieces * part, depth), BF)],
        compiler_params=pltpu.CompilerParams(vmem_limit_bytes=VMEM_LIMIT),
        cost_estimate=cost_of(3e9, 4e6),
    )(ids, fast_rate, side_grad, core_grad, flipped, norms, queries, window_second, gates)
    done_second = finished(ids, gated_second, norm_gain)
    return jnp.stack([done_first, done_second])


def solution(mesh):
    placed = (
        P(None, "ctx", "head"),
        P(None, "ctx", "head"),
        P(None, "ctx", "head"),
        P(None, "ctx", "head"),
        P("ctx", "head"),
        P("head", "ctx", None),
        P("head"),
        P(),
    )
    return jax.shard_map(
        shards,
        mesh=mesh,
        in_specs=placed,
        out_specs=P(None, ("ctx", "head"), None),
        check_vma=False,
    )
```

```python
import functools

import jax
import jax.numpy as jnp
from jax import lax
from jax.experimental import pallas as pl
from jax.experimental.pallas import tpu as pltpu
from jax.sharding import PartitionSpec as P

WIN = 1024
A_COEF = 3.4445
B_COEF = -4.775
C_COEF = 2.0315
BF = jnp.bfloat16
F32 = jnp.float32
VMEM_LIMIT = 48 * 1024 * 1024


def dot_nn(a, b):
    return lax.dot_general(a, b, (((1,), (0,)), ((), ())), preferred_element_type=F32)


def dot_nt(a, b):
    return lax.dot_general(a, b, (((1,), (1,)), ((), ())), preferred_element_type=F32)


def dot_tn(a, b):
    return lax.dot_general(a, b, (((0,), (0,)), ((), ())), preferred_element_type=F32)


def swapped(value, mask, axis="ctx"):
    count = lax.axis_size(axis)
    return lax.ppermute(value, axis, [(i, i ^ mask) for i in range(count)])


def vmem_spec():
    return pl.BlockSpec(memory_space=pltpu.VMEM)


def call(body, args, outs, scratch=(), cost=None):
    return pl.pallas_call(
        body,
        out_shape=outs,
        in_specs=[pl.BlockSpec(memory_space=pltpu.SMEM)] + [vmem_spec()] * (len(args) - 1),
        out_specs=jax.tree.map(lambda _: vmem_spec(), outs),
        scratch_shapes=list(scratch),
        compiler_params=pltpu.CompilerParams(vmem_limit_bytes=VMEM_LIMIT),
        cost_estimate=cost,
    )(*args)


def cost_of(flops, moved):
    return pl.CostEstimate(flops=int(flops), bytes_accessed=int(moved), transcendentals=0)


def silu(v):
    return v / (1.0 + jnp.exp(-v))


def gradient_body(planes, ids, mine, other, beside, pair_a, pair_b, rate_a, rate_b, *refs):
    send, keep, whole, total = refs[:4]
    plane, side, core = ids[0], ids[1], ids[2]
    rows = mine.shape[1]
    target_ref = refs[4] if len(refs) > 4 else whole
    for m in range(planes):
        for far in range(2):
            block = ((plane ^ m) * 2 + (side if far == 0 else 1 - side)) * 2
            own_at = pl.multiple_of((block + core) * rows, rows)
            other_at = pl.multiple_of((block + 1 - core) * rows, rows)
            source = (mine, other)[far]
            target_ref[pl.ds(own_at, rows), :] = source[m].astype(target_ref.dtype)
            target_ref[pl.ds(other_at, rows), :] = beside[far * planes + m].astype(target_ref.dtype)
    if target_ref is not whole:
        whole[...] = target_ref[...].astype(BF)
    width = whole.shape[1] // 3
    half = width // 2
    parts = [
        whole[:, pl.ds(pl.multiple_of(b * width + core * half, half), half)] for b in range(3)
    ]
    gate_up_w = jnp.concatenate(parts[:2], 1)
    out_w = parts[2]
    first = None
    for pair, rate in ((pair_a, rate_a), (pair_b, rate_b)):
        key_rows = pair[0]
        target = (-rate[...] * pair[1].astype(F32)).astype(BF)
        gate_up = dot_nn(key_rows, gate_up_w)
        g, u = gate_up[:, :half], gate_up[:, half:]
        dh = dot_nn(target, out_w)
        s = 1.0 / (1.0 + jnp.exp(-g))
        gs = g * s
        hidden = (gs * u).astype(BF)
        dg = dh * u * s * (1.0 + g * (1.0 - s))
        du = dh * gs
        joined = jnp.concatenate([dg, du], 1).astype(BF)
        in_grad = dot_tn(joined, key_rows)
        out_grad = dot_tn(hidden, target)
        first = (in_grad, out_grad) if first is None else (first[0] + in_grad, first[1] + out_grad)
    total[: 2 * half, :] = first[0]
    total[2 * half : 3 * half, :] = first[1]
    if total.shape[0] > 3 * half:
        total[3 * half :, :] = jnp.zeros((total.shape[0] - 3 * half, total.shape[1]), F32)
    part = send.shape[0]
    send[...] = total[pl.ds(pl.multiple_of((1 - side) * part, part), part), :].astype(BF)
    keep[...] = total[pl.ds(pl.multiple_of(side * part, part), part), :]


def side_sum_body(planes, ids, keep, got, *refs):
    outs, total = refs[:planes], refs[planes]
    plane = ids[0]
    total[...] = keep[...] + got[...].astype(F32)
    part = outs[0].shape[0]
    for m in range(planes):
        rows = total[pl.ds(pl.multiple_of((plane ^ m) * part, part), part), :]
        outs[m][...] = rows.astype(outs[m].dtype)


def plane_sum_body(ids, own, *refs):
    total = own[...]
    for ref in refs[:-1]:
        total = total + ref[...].astype(F32)
    refs[-1][...] = total.astype(BF)


def weights_body(ids, whole, flipped, norms):
    width = whole.shape[1] // 3
    for b in range(3):
        cols = slice(b * width, (b + 1) * width)
        turned = whole[:, cols].astype(F32).T
        flipped[cols, :] = turned
        norms[cols, :] = jnp.sqrt(jnp.sum(turned * turned, 1, keepdims=True))


def fetch(slots, options):
    held, sems = slots
    for slot, choices in enumerate(options):
        for condition, source in choices:
            for which in range(2):
                part = source[which] if isinstance(source, tuple) else source.at[which]
                copy = pltpu.make_async_copy(part, held.at[slot, which], sems.at[slot, which])
                if condition is None:
                    copy.start()
                else:
                    pl.when(condition)(copy.start)

    def wait(slot, which):
        part = held.at[slot, which]
        pltpu.make_async_copy(part, part, sems.at[slot, which]).wait()

    return wait


def window(q, k_own, v_own, held, wait, lives):
    rows, depth = q.shape
    scale = depth**-0.5
    row = lax.broadcasted_iota(jnp.int32, (rows, rows), 0)
    col = lax.broadcasted_iota(jnp.int32, (rows, rows), 1)
    scores = [jnp.where(col <= row, dot_nt(q, k_own) * scale, -1e30)]
    for slot in range(4):
        wait(slot, 0)
        s = dot_nt(q, held[slot, 0]) * scale
        allowed = col > row if slot == 0 else None
        if lives is not None:
            alive = jnp.full((rows, rows), lives[slot], jnp.int32) != 0
            allowed = alive if allowed is None else allowed & alive
        scores.append(s if allowed is None else jnp.where(allowed, s, -1e30))
    top = jnp.max(scores[0], -1, keepdims=True)
    for s in scores[1:]:
        top = jnp.maximum(top, jnp.max(s, -1, keepdims=True))
    total = None
    out = None
    for slot, s in enumerate(scores):
        e = jnp.exp(s - top)
        t = jnp.sum(e, -1, keepdims=True)
        if slot:
            wait(slot - 1, 1)
        o = dot_nn(e.astype(BF), v_own if slot == 0 else held[slot - 1, 1])
        total = t if total is None else total + t
        out = o if out is None else out + o
    return out / total


def first_group_body(ids, q, k_own, v_own, gates, whole, *refs):
    far, near_k, near_v, near, own_beside, far_beside, diag_k, diag_v, diag = refs[:9]
    outs, (held, sems, gated) = refs[9:-3], refs[-3:]
    plane, side, core = ids[0], ids[1], ids[2]
    wait = fetch(
        (held, sems),
        [
            [(None, far)],
            [(side == 1, (near_k, near_v)), (side == 0, near)],
            [(core == 1, own_beside), (core == 0, far_beside)],
            [(side == 1, (diag_k, diag_v)), (side == 0, diag)],
        ],
    )
    later = (plane > 0).astype(jnp.int32)
    side_live = jnp.maximum(later, side)
    core_live = jnp.maximum(later, core)
    lives = [later, side_live, core_live, side_live]
    width = whole.shape[1] // 3
    gate_up = dot_nn(q[0], whole[:, : 2 * width])
    hidden = (silu(gate_up[:, :width]) * gate_up[:, width:]).astype(BF)
    fast = dot_nt(hidden, whole[:, 2 * width :])
    win = window(q[0], k_own[0], v_own[0], held, wait, lives)
    gate = gates[0].astype(F32)
    spread(ids, ((win + fast) * silu(gate)).astype(BF), outs, gated)


def spread(ids, value, outs, held):
    if len(outs) == 1:
        outs[0][...] = value
        return
    held[...] = value
    rows = outs[0].shape[0]
    outs[0][...] = held[pl.ds(pl.multiple_of(ids[3] * rows, rows), rows), :]
    outs[1][...] = held[pl.ds(pl.multiple_of((1 - ids[3]) * rows, rows), rows), :]


def second_group_body(ids, q, k_own, v_own, *refs):
    far_0, far_1, near_own, near_0, near_1, own_beside, far_beside_0, far_beside_1 = refs[:8]
    diag_own, diag_0, diag_1, out, held, sems = refs[8:]
    plane, side, core = ids[0], ids[1], ids[2]
    begin, after = plane == 0, plane > 0
    wait = fetch(
        (held, sems),
        [
            [(begin, far_0), (after, far_1)],
            [
                (side == 1, near_own),
                ((side == 0) & begin, near_0),
                ((side == 0) & after, near_1),
            ],
            [
                (core == 1, own_beside),
                ((core == 0) & begin, far_beside_0),
                ((core == 0) & after, far_beside_1),
            ],
            [
                (side == 1, diag_own),
                ((side == 0) & begin, diag_0),
                ((side == 0) & after, diag_1),
            ],
        ],
    )
    out[...] = window(q[0], k_own[0], v_own[0], held, wait, None)


def group_call(body, index, ids, grouped, whole, raw, outs, rows, depth, scratch, cost):
    def full(a):
        return pl.BlockSpec(a.shape, lambda i, nd=len(a.shape): (0,) * nd)

    specs = [pl.BlockSpec((1,) + a.shape[1:], lambda i: (index, 0, 0)) for a in grouped]
    specs += [full(a) for a in whole]
    specs += [pl.BlockSpec(memory_space=pl.ANY)] * len(raw)
    return pl.pallas_call(
        body,
        grid=(1,),
        out_shape=outs,
        in_specs=[pl.BlockSpec(memory_space=pltpu.SMEM)] + specs,
        out_specs=jax.tree.map(full, outs),
        scratch_shapes=[
            pltpu.VMEM((4, 2, rows, depth), BF),
            pltpu.SemaphoreType.DMA((4, 2)),
            *scratch,
        ],
        compiler_params=pltpu.CompilerParams(vmem_limit_bytes=VMEM_LIMIT),
        cost_estimate=cost,
    )(ids, *grouped, *whole, *raw)


def update_body(planes, ids, rate, mine, other, flipped, norms, q, win, gates, *refs):
    outs, (grads, gated) = refs[:-2], refs[-2:]
    plane, side, core = ids[0], ids[1], ids[2]
    part = mine.shape[1]
    for m in range(planes):
        for far in range(2):
            base = ((side if far == 0 else 1 - side) * planes + (plane ^ m)) * part
            where = pl.ds(pl.multiple_of(base, part), part)
            grads[core, where, :] = mine[far * planes + m]
            grads[1 - core, where, :] = other[far * planes + m]
    width = flipped.shape[0] // 3
    half = width // 2
    turned = []
    for b in range(3):
        block = jnp.concatenate(
            [grads[0, b * half : (b + 1) * half, :], grads[1, b * half : (b + 1) * half, :]], 0
        ).astype(F32)
        length = jnp.sqrt(jnp.sum(block * block, keepdims=True))
        turned.append((block / (length + 1e-06)).astype(BF))
    for _ in range(3):
        grams = [dot_nt(y, y) for y in turned]
        lows = [a.astype(BF) for a in grams]
        squares = [dot_nn(a, a) for a in lows]
        mixers = [(B_COEF * a + C_COEF * s).astype(BF) for a, s in zip(grams, squares)]
        turned = [
            (A_COEF * y.astype(F32) + dot_nn(b, y)).astype(BF) for b, y in zip(mixers, turned)
        ]
    fresh = []
    for b in range(3):
        cols = slice(b * width, (b + 1) * width)
        moved = flipped[cols, :] - rate[0] * turned[b].astype(F32)
        length = jnp.sqrt(jnp.sum(moved * moved, 1, keepdims=True))
        fresh.append((moved * (norms[cols, :] / (length + 1e-06))).astype(BF))
    x = q[...]
    g = dot_nt(x, fresh[0])
    u = dot_nt(x, fresh[1])
    hidden = (silu(g) * u).astype(BF)
    fast = dot_nn(hidden, fresh[2])
    gate = gates[...].astype(F32)
    spread(ids, ((win[...] + fast) * silu(gate)).astype(BF), outs, gated)


def norm_body(ids, own, got, gain, *refs):
    out = refs[-1]
    head = ids[3]
    rows, depth = own.shape
    a = own[...].astype(F32)
    b = got[...].astype(F32)
    low = jnp.where(head == 0, a, b)
    high = jnp.where(head == 0, b, a)
    square = jnp.sum(a * a, -1, keepdims=True) + jnp.sum(b * b, -1, keepdims=True)
    inv = lax.rsqrt(square / (2 * depth) + 1e-06)
    out[0, :, :depth] = (low * inv * gain[:, :depth]).astype(BF)
    out[0, :, depth:] = (high * inv * gain[:, depth:]).astype(BF)


def finished(ids, group, gated, norm_gain, before):
    total = norm_gain.shape[0]
    if len(gated) == 2:
        own, away = gated
        got = swapped(away, 1, "head")
        rows, depth = own.shape
        earlier = () if before is None else (before,)
        return pl.pallas_call(
            norm_body,
            grid=(1,),
            out_shape=jax.ShapeDtypeStruct((2, rows, total), BF),
            in_specs=[
                pl.BlockSpec(memory_space=pltpu.SMEM),
                pl.BlockSpec((rows, depth), lambda i: (0, 0)),
                pl.BlockSpec((rows, depth), lambda i: (0, 0)),
                pl.BlockSpec((1, total), lambda i: (0, 0)),
                *([pl.BlockSpec(memory_space=pl.ANY)] * len(earlier)),
            ],
            out_specs=pl.BlockSpec((1, rows, total), lambda i: (group, 0, 0)),
            input_output_aliases={4: 0} if earlier else {},
            compiler_params=pltpu.CompilerParams(vmem_limit_bytes=VMEM_LIMIT),
            cost_estimate=cost_of(0, 4 * rows * total),
        )(ids, own, got, norm_gain[None, :], *earlier)
    wide = lax.all_to_all(gated[0], "head", split_axis=0, concat_axis=1, tiled=True).astype(F32)
    inv = lax.rsqrt(jnp.mean(wide * wide, -1, keepdims=True) + 1e-06)
    done = (wide * inv * norm_gain).astype(BF)[None]
    return done if before is None else jnp.concatenate([before, done], 0)


def after(value, *needed):
    return lax.optimization_barrier((value,) + needed)[0]


def sent(value, pairs, axis="ctx"):
    return lax.ppermute(value, axis, pairs)


def shards(queries, keys, values, gates, token_rates, fast_init, fast_rate, norm_gain):
    count = lax.axis_size("ctx")
    heads = lax.axis_size("head")
    rows, depth = queries.shape[1], queries.shape[2]
    reach = (WIN - 1) // rows + 1
    planes = count // reach
    if reach != 4 or WIN % rows or planes * reach != count or planes & (planes - 1):
        raise ValueError("unsupported shapes")
    position = lax.axis_index("ctx")
    plane, side, core = position // 4, (position // 2) % 2, position % 2
    ids = jnp.stack([plane, side, core, lax.axis_index("head")]).astype(jnp.int32)
    width = fast_init.shape[2] // 3
    half = width // 2
    everyone = range(count)
    side_up = [(i, i ^ 2) for i in everyone if i & 2 == 0]
    side_down = [(i, i ^ 2) for i in everyone if i & 2]
    core_up = [(i, i ^ 1) for i in everyone if i & 1 == 0]
    core_down = [(i, i ^ 1) for i in everyone if i & 1]
    high_cores = [(i, i ^ 1) for i in everyone if i & 2]
    low_cores = [(i, i ^ 1) for i in everyone if i & 2 == 0]

    local = fast_init[0]
    arrived = [swapped(local, 4 * m) for m in range(1, planes)]
    mine_w = jnp.stack([local] + arrived)
    other_w = swapped(mine_w, 2)
    beside_w = swapped(jnp.concatenate([mine_w, other_w], 0), 1)

    pair_0 = jnp.stack([keys[0], values[0]])
    pair_1 = jnp.stack([keys[1], values[1]])
    beside_0 = swapped(pair_0, 1)
    beside_1 = sent(pair_1, core_up)
    rates_beside = swapped(token_rates, 1)
    near_k = sent(keys[0], side_up)
    near_v = sent(after(values[0], other_w), side_up)
    diag_k = sent(near_k, high_cores)
    diag_v = sent(near_v, high_cores)

    pieces = 2 * planes
    part = -(-3 * half // (16 * pieces)) * 16
    scratch = [pltpu.VMEM((pieces * part, depth), F32)]
    if local.shape[0] % 16:
        scratch.append(pltpu.VMEM((depth, 3 * width), F32))
    send, keep, whole = call(
        functools.partial(gradient_body, planes),
        (ids, mine_w, other_w, beside_w, pair_0, beside_0, token_rates, rates_beside),
        (
            jax.ShapeDtypeStruct((planes * part, depth), BF),
            jax.ShapeDtypeStruct((planes * part, depth), F32),
            jax.ShapeDtypeStruct((depth, 3 * width), BF),
        ),
        scratch=scratch,
        cost=cost_of(2 * 2 * rows * depth * half * 6, 4 * rows * depth * 4),
    )
    got = swapped(send, 2)
    parts = call(
        functools.partial(side_sum_body, planes),
        (ids, keep, got),
        tuple(jax.ShapeDtypeStruct((part, depth), F32 if m == 0 else BF) for m in range(planes)),
        scratch=(pltpu.VMEM((planes * part, depth), F32),),
        cost=cost_of(0, planes * part * depth * 8),
    )
    partial = [swapped(parts[m], 4 * m) for m in range(1, planes)]
    total = call(
        plane_sum_body,
        (ids, parts[0], *partial),
        jax.ShapeDtypeStruct((part, depth), BF),
        cost=cost_of(0, planes * part * depth * 3),
    )
    stacked = jnp.stack([total] + [swapped(total, 4 * m) for m in range(1, planes)])
    side_grad = jnp.concatenate([stacked, swapped(stacked, 2)], 0)
    core_grad = swapped(side_grad, 1)

    ring = [(i, (i + reach) % count) for i in everyone]
    line = [(i, i + reach) for i in range(count - reach)]
    far_0 = sent(after(pair_0, mine_w), ring)
    far_1 = sent(after(pair_1, send), line)
    far_beside_0 = sent(far_0, core_down)
    far_beside_1 = sent(far_1, core_down)
    near_0 = sent(after(far_0, got), side_down)
    diag_0 = sent(near_0, low_cores)
    near_own = sent(after(pair_1, got), side_up)
    diag_own = sent(near_own, high_cores)
    near_1 = sent(after(far_1, total), side_down)
    diag_1 = sent(near_1, low_cores)

    flipped, norms = call(
        weights_body,
        (ids, whole),
        (
            jax.ShapeDtypeStruct((3 * width, depth), F32),
            jax.ShapeDtypeStruct((3 * width, 1), F32),
        ),
        cost=cost_of(0, depth * width * 3 * 8),
    )
    attn_cost = cost_of(8 * rows * depth * 5 * rows, rows * depth * 30)
    if heads == 2:
        split = (jax.ShapeDtypeStruct((rows // 2, depth), BF),) * 2
    else:
        split = (jax.ShapeDtypeStruct((rows, depth), BF),)
    gated_first = group_call(
        first_group_body,
        0,
        ids,
        [queries, keys, values, gates],
        [whole],
        [far_0, near_k, near_v, near_0, beside_0, far_beside_0, diag_k, diag_v, diag_0],
        split,
        rows,
        depth,
        [pltpu.VMEM((rows, depth), BF)],
        attn_cost,
    )
    window_second = group_call(
        second_group_body,
        1,
        ids,
        [queries, keys, values],
        [],
        [far_0, far_1, near_own, near_0, near_1, beside_1, far_beside_0, far_beside_1]
        + [diag_own, diag_0, diag_1],
        jax.ShapeDtypeStruct((rows, depth), F32),
        rows,
        depth,
        [],
        attn_cost,
    )
    done = finished(ids, 0, gated_first, norm_gain, None)

    def full(shape):
        return pl.BlockSpec(shape, lambda i, nd=len(shape): (0,) * nd)

    gated_second = pl.pallas_call(
        functools.partial(update_body, planes),
        grid=(1,),
        out_shape=split,
        in_specs=[
            pl.BlockSpec(memory_space=pltpu.SMEM),
            pl.BlockSpec(memory_space=pltpu.SMEM),
            full(side_grad.shape),
            full(core_grad.shape),
            full(flipped.shape),
            full(norms.shape),
            pl.BlockSpec((None, rows, depth), lambda i: (1, 0, 0)),
            full((rows, depth)),
            pl.BlockSpec((None, rows, depth), lambda i: (1, 0, 0)),
        ],
        out_specs=tuple(full(s.shape) for s in split),
        scratch_shapes=[
            pltpu.VMEM((2, pieces * part, depth), BF),
            pltpu.VMEM((rows, depth), BF),
        ],
        compiler_params=pltpu.CompilerParams(vmem_limit_bytes=VMEM_LIMIT),
        cost_estimate=cost_of(3e9, 4e6),
    )(ids, fast_rate, side_grad, core_grad, flipped, norms, queries, window_second, gates)
    return finished(ids, 1, gated_second, norm_gain, done)


def solution(mesh):
    placed = (
        P(None, "ctx", "head"),
        P(None, "ctx", "head"),
        P(None, "ctx", "head"),
        P(None, "ctx", "head"),
        P("ctx", "head"),
        P("head", "ctx", None),
        P("head"),
        P(),
    )
    return jax.shard_map(
        shards,
        mesh=mesh,
        in_specs=placed,
        out_specs=P(None, ("ctx", "head"), None),
        check_vma=False,
    )
```

```python
import functools

import jax
import jax.numpy as jnp
from jax import lax
from jax.experimental import pallas as pl
from jax.experimental.pallas import tpu as pltpu
from jax.sharding import PartitionSpec as P

WIN = 1024
A_COEF = 3.4445
B_COEF = -4.775
C_COEF = 2.0315
BF = jnp.bfloat16
F32 = jnp.float32
VMEM_LIMIT = 48 * 1024 * 1024


def dot_nn(a, b):
    return lax.dot_general(a, b, (((1,), (0,)), ((), ())), preferred_element_type=F32)


def dot_nt(a, b):
    return lax.dot_general(a, b, (((1,), (1,)), ((), ())), preferred_element_type=F32)


def dot_tn(a, b):
    return lax.dot_general(a, b, (((0,), (0,)), ((), ())), preferred_element_type=F32)


def swapped(value, mask, axis="ctx"):
    count = lax.axis_size(axis)
    return lax.ppermute(value, axis, [(i, i ^ mask) for i in range(count)])


def vmem_spec():
    return pl.BlockSpec(memory_space=pltpu.VMEM)


def call(body, args, outs, scratch=(), cost=None):
    return pl.pallas_call(
        body,
        out_shape=outs,
        in_specs=[pl.BlockSpec(memory_space=pltpu.SMEM)] + [vmem_spec()] * (len(args) - 1),
        out_specs=jax.tree.map(lambda _: vmem_spec(), outs),
        scratch_shapes=list(scratch),
        compiler_params=pltpu.CompilerParams(vmem_limit_bytes=VMEM_LIMIT),
        cost_estimate=cost,
    )(*args)


def cost_of(flops, moved):
    return pl.CostEstimate(flops=int(flops), bytes_accessed=int(moved), transcendentals=0)


def silu(v):
    return v / (1.0 + jnp.exp(-v))


def prepare_body(keys, values, rates, pair_0, pair_1, target, held, sems, value_sem):
    load = pltpu.make_async_copy(values.at[0], held, value_sem)
    load.start()
    copies = []
    for g, pair in enumerate((pair_0, pair_1)):
        for which, source in enumerate((keys, values)):
            copies.append(
                pltpu.make_async_copy(source.at[g], pair.at[which], sems.at[2 * g + which])
            )
    for copy in copies:
        copy.start()
    load.wait()
    target[...] = (-rates[...] * held[...].astype(F32)).astype(BF)
    for copy in copies:
        copy.wait()


def prepared(keys, values, rates):
    rows, depth = keys.shape[1:]
    anywhere = pl.BlockSpec(memory_space=pl.ANY)
    pair = jax.ShapeDtypeStruct((2, rows, depth), BF)
    return pl.pallas_call(
        prepare_body,
        out_shape=(pair, pair, jax.ShapeDtypeStruct((rows, depth), BF)),
        in_specs=[anywhere, anywhere, vmem_spec()],
        out_specs=(anywhere, anywhere, vmem_spec()),
        scratch_shapes=[
            pltpu.VMEM((rows, depth), BF),
            pltpu.SemaphoreType.DMA((4,)),
            pltpu.SemaphoreType.DMA,
        ],
        cost_estimate=cost_of(0, rows * depth * 8),
    )(keys, values, rates)


def pick_body(ids, own, far, out, sems):
    side = ids[1]
    for condition, source in ((side == 0, own), (side == 1, far)):

        @pl.when(condition)
        def _():
            copies = [
                pltpu.make_async_copy(source.at[w], out.at[w], sems.at[w]) for w in range(2)
            ]
            for copy in copies:
                copy.start()
            for copy in copies:
                copy.wait()


def picked(ids, own, far):
    anywhere = pl.BlockSpec(memory_space=pl.ANY)
    return pl.pallas_call(
        pick_body,
        out_shape=jax.ShapeDtypeStruct(own.shape, own.dtype),
        in_specs=[pl.BlockSpec(memory_space=pltpu.SMEM), anywhere, anywhere],
        out_specs=anywhere,
        scratch_shapes=[pltpu.SemaphoreType.DMA((2,))],
        cost_estimate=cost_of(0, own.size * 4),
    )(ids, own, far)


def gradient_body(planes, ids, mine, other, beside, pair_a, pair_b, target_a, target_b, *refs):
    send, keep, whole, total = refs[:4]
    plane, side, core = ids[0], ids[1], ids[2]
    rows = mine.shape[1]
    target_ref = refs[4] if len(refs) > 4 else whole
    for m in range(planes):
        for far in range(2):
            block = ((plane ^ m) * 2 + (side if far == 0 else 1 - side)) * 2
            own_at = pl.multiple_of((block + core) * rows, rows)
            other_at = pl.multiple_of((block + 1 - core) * rows, rows)
            source = (mine, other)[far]
            target_ref[pl.ds(own_at, rows), :] = source[m].astype(target_ref.dtype)
            target_ref[pl.ds(other_at, rows), :] = beside[far * planes + m].astype(target_ref.dtype)
    if target_ref is not whole:
        whole[...] = target_ref[...].astype(BF)
    width = whole.shape[1] // 3
    half = width // 2
    parts = [
        whole[:, pl.ds(pl.multiple_of(b * width + core * half, half), half)] for b in range(3)
    ]
    gate_up_w = jnp.concatenate(parts[:2], 1)
    out_w = parts[2]
    first = None
    for pair, target_rows in ((pair_a, target_a), (pair_b, target_b)):
        key_rows, target = pair[0], target_rows[...]
        gate_up = dot_nn(key_rows, gate_up_w)
        g, u = gate_up[:, :half], gate_up[:, half:]
        dh = dot_nn(target, out_w)
        s = 1.0 / (1.0 + jnp.exp(-g))
        gs = g * s
        hidden = (gs * u).astype(BF)
        dg = dh * u * s * (1.0 + g * (1.0 - s))
        du = dh * gs
        joined = jnp.concatenate([dg, du], 1).astype(BF)
        in_grad = dot_tn(joined, key_rows)
        out_grad = dot_tn(hidden, target)
        first = (in_grad, out_grad) if first is None else (first[0] + in_grad, first[1] + out_grad)
    total[: 2 * half, :] = first[0]
    total[2 * half : 3 * half, :] = first[1]
    if total.shape[0] > 3 * half:
        total[3 * half :, :] = jnp.zeros((total.shape[0] - 3 * half, total.shape[1]), F32)
    part = send.shape[0]
    send[...] = total[pl.ds(pl.multiple_of((1 - side) * part, part), part), :].astype(BF)
    keep[...] = total[pl.ds(pl.multiple_of(side * part, part), part), :]


def side_sum_body(planes, ids, keep, got, *refs):
    outs, total = refs[:planes], refs[planes]
    plane = ids[0]
    total[...] = keep[...] + got[...].astype(F32)
    part = outs[0].shape[0]
    for m in range(planes):
        rows = total[pl.ds(pl.multiple_of((plane ^ m) * part, part), part), :]
        outs[m][...] = rows.astype(outs[m].dtype)


def plane_sum_body(ids, own, *refs):
    total = own[...]
    for ref in refs[:-1]:
        total = total + ref[...].astype(F32)
    refs[-1][...] = total.astype(BF)


def weights_body(ids, whole, flipped, norms):
    width = whole.shape[1] // 3
    for b in range(3):
        cols = slice(b * width, (b + 1) * width)
        turned = whole[:, cols].astype(F32).T
        flipped[cols, :] = turned
        norms[cols, :] = jnp.sqrt(jnp.sum(turned * turned, 1, keepdims=True))


def fetch(slots, options):
    held, sems = slots
    for slot, choices in enumerate(options):
        for condition, source in choices:
            for which in range(2):
                copy = pltpu.make_async_copy(
                    source.at[which], held.at[slot, which], sems.at[slot, which]
                )
                if condition is None:
                    copy.start()
                else:
                    pl.when(condition)(copy.start)

    def wait(slot, which):
        part = held.at[slot, which]
        pltpu.make_async_copy(part, part, sems.at[slot, which]).wait()

    return wait


def window(q, k_own, v_own, held, wait, lives):
    rows, depth = q.shape
    scale = depth**-0.5
    row = lax.broadcasted_iota(jnp.int32, (rows, rows), 0)
    col = lax.broadcasted_iota(jnp.int32, (rows, rows), 1)
    scores = [jnp.where(col <= row, dot_nt(q, k_own) * scale, -1e30)]
    for slot in range(4):
        wait(slot, 0)
        s = dot_nt(q, held[slot, 0]) * scale
        allowed = col > row if slot == 0 else None
        if lives is not None:
            alive = jnp.full((rows, rows), lives[slot], jnp.int32) != 0
            allowed = alive if allowed is None else allowed & alive
        scores.append(s if allowed is None else jnp.where(allowed, s, -1e30))
    top = jnp.max(scores[0], -1, keepdims=True)
    for s in scores[1:]:
        top = jnp.maximum(top, jnp.max(s, -1, keepdims=True))
    total = None
    out = None
    for slot, s in enumerate(scores):
        e = jnp.exp(s - top)
        t = jnp.sum(e, -1, keepdims=True)
        if slot:
            wait(slot - 1, 1)
        o = dot_nn(e.astype(BF), v_own if slot == 0 else held[slot - 1, 1])
        total = t if total is None else total + t
        out = o if out is None else out + o
    return out / total


def first_group_body(ids, q, k_own, v_own, gates, whole, *refs):
    far, near, own_beside, far_beside, diag = refs[:5]
    outs, (held, sems, gated) = refs[5:-3], refs[-3:]
    plane, side, core = ids[0], ids[1], ids[2]
    wait = fetch(
        (held, sems),
        [
            [(None, far)],
            [(None, near)],
            [(core == 1, own_beside), (core == 0, far_beside)],
            [(None, diag)],
        ],
    )
    later = (plane > 0).astype(jnp.int32)
    side_live = jnp.maximum(later, side)
    core_live = jnp.maximum(later, core)
    lives = [later, side_live, core_live, side_live]
    width = whole.shape[1] // 3
    gate_up = dot_nn(q[0], whole[:, : 2 * width])
    hidden = (silu(gate_up[:, :width]) * gate_up[:, width:]).astype(BF)
    fast = dot_nt(hidden, whole[:, 2 * width :])
    win = window(q[0], k_own[0], v_own[0], held, wait, lives)
    gate = gates[0].astype(F32)
    spread(ids, ((win + fast) * silu(gate)).astype(BF), outs, gated)


def spread(ids, value, outs, held):
    if len(outs) == 1:
        outs[0][...] = value
        return
    held[...] = value
    rows = outs[0].shape[0]
    outs[0][...] = held[pl.ds(pl.multiple_of(ids[3] * rows, rows), rows), :]
    outs[1][...] = held[pl.ds(pl.multiple_of((1 - ids[3]) * rows, rows), rows), :]


def second_group_body(ids, q, k_own, v_own, *refs):
    far_0, far_1, near_0, near_1, own_beside, far_beside_0, far_beside_1 = refs[:7]
    diag_0, diag_1, out, held, sems = refs[7:]
    plane, side, core = ids[0], ids[1], ids[2]
    begin = plane == 0
    wrapped = begin & (side == 0)
    wait = fetch(
        (held, sems),
        [
            [(begin, far_0), (plane > 0, far_1)],
            [(wrapped, near_0), (jnp.logical_not(wrapped), near_1)],
            [
                (core == 1, own_beside),
                ((core == 0) & begin, far_beside_0),
                ((core == 0) & (plane > 0), far_beside_1),
            ],
            [(wrapped, diag_0), (jnp.logical_not(wrapped), diag_1)],
        ],
    )
    out[...] = window(q[0], k_own[0], v_own[0], held, wait, None)


def group_call(body, index, ids, grouped, whole, raw, outs, rows, depth, scratch, cost):
    def full(a):
        return pl.BlockSpec(a.shape, lambda i, nd=len(a.shape): (0,) * nd)

    specs = [pl.BlockSpec((1,) + a.shape[1:], lambda i: (index, 0, 0)) for a in grouped]
    specs += [full(a) for a in whole]
    specs += [pl.BlockSpec(memory_space=pl.ANY)] * len(raw)
    return pl.pallas_call(
        body,
        grid=(1,),
        out_shape=outs,
        in_specs=[pl.BlockSpec(memory_space=pltpu.SMEM)] + specs,
        out_specs=jax.tree.map(full, outs),
        scratch_shapes=[
            pltpu.VMEM((4, 2, rows, depth), BF),
            pltpu.SemaphoreType.DMA((4, 2)),
            *scratch,
        ],
        compiler_params=pltpu.CompilerParams(vmem_limit_bytes=VMEM_LIMIT),
        cost_estimate=cost,
    )(ids, *grouped, *whole, *raw)


def update_body(planes, ids, rate, mine, other, flipped, norms, q, win, gates, *refs):
    outs, (grads, gated) = refs[:-2], refs[-2:]
    plane, side, core = ids[0], ids[1], ids[2]
    part = mine.shape[1]
    for m in range(planes):
        for far in range(2):
            base = ((side if far == 0 else 1 - side) * planes + (plane ^ m)) * part
            where = pl.ds(pl.multiple_of(base, part), part)
            grads[core, where, :] = mine[far * planes + m]
            grads[1 - core, where, :] = other[far * planes + m]
    width = flipped.shape[0] // 3
    half = width // 2
    turned = []
    for b in range(3):
        block = jnp.concatenate(
            [grads[0, b * half : (b + 1) * half, :], grads[1, b * half : (b + 1) * half, :]], 0
        ).astype(F32)
        length = jnp.sqrt(jnp.sum(block * block, keepdims=True))
        turned.append((block / (length + 1e-06)).astype(BF))
    for _ in range(3):
        grams = [dot_nt(y, y) for y in turned]
        lows = [a.astype(BF) for a in grams]
        squares = [dot_nn(a, a) for a in lows]
        mixers = [(B_COEF * a + C_COEF * s).astype(BF) for a, s in zip(grams, squares)]
        turned = [
            (A_COEF * y.astype(F32) + dot_nn(b, y)).astype(BF) for b, y in zip(mixers, turned)
        ]
    fresh = []
    for b in range(3):
        cols = slice(b * width, (b + 1) * width)
        moved = flipped[cols, :] - rate[0] * turned[b].astype(F32)
        length = jnp.sqrt(jnp.sum(moved * moved, 1, keepdims=True))
        fresh.append((moved * (norms[cols, :] / (length + 1e-06))).astype(BF))
    x = q[...]
    g = dot_nt(x, fresh[0])
    u = dot_nt(x, fresh[1])
    hidden = (silu(g) * u).astype(BF)
    fast = dot_nn(hidden, fresh[2])
    gate = gates[...].astype(F32)
    spread(ids, ((win[...] + fast) * silu(gate)).astype(BF), outs, gated)


def norm_body(group, ids, own, got, gain, *refs):
    out, held, sems = refs[-3:]
    head = ids[3]
    rows, depth = own.shape
    chunk = rows // 4
    copies = []
    for c in range(4):
        at = slice(c * chunk, (c + 1) * chunk)
        a = own[at, :].astype(F32)
        b = got[at, :].astype(F32)
        low = jnp.where(head == 0, a, b)
        high = jnp.where(head == 0, b, a)
        square = jnp.sum(a * a, -1, keepdims=True) + jnp.sum(b * b, -1, keepdims=True)
        inv = lax.rsqrt(square / (2 * depth) + 1e-06)
        held[at, :depth] = (low * inv * gain[:, :depth]).astype(BF)
        held[at, depth:] = (high * inv * gain[:, depth:]).astype(BF)
        copies.append(pltpu.make_async_copy(held.at[at], out.at[group, at], sems.at[c]))
        copies[-1].start()
    for copy in copies:
        copy.wait()


def finished(ids, group, gated, norm_gain, before):
    total = norm_gain.shape[0]
    if len(gated) == 2:
        own, away = gated
        got = swapped(away, 1, "head")
        rows, depth = own.shape
        earlier = () if before is None else (before,)
        return pl.pallas_call(
            functools.partial(norm_body, group),
            out_shape=jax.ShapeDtypeStruct((2, rows, total), BF),
            in_specs=[
                pl.BlockSpec(memory_space=pltpu.SMEM),
                vmem_spec(),
                vmem_spec(),
                vmem_spec(),
                *([pl.BlockSpec(memory_space=pl.ANY)] * len(earlier)),
            ],
            out_specs=pl.BlockSpec(memory_space=pl.ANY),
            scratch_shapes=[pltpu.VMEM((rows, total), BF), pltpu.SemaphoreType.DMA((4,))],
            input_output_aliases={4: 0} if earlier else {},
            compiler_params=pltpu.CompilerParams(vmem_limit_bytes=VMEM_LIMIT),
            cost_estimate=cost_of(0, 4 * rows * total),
        )(ids, own, got, norm_gain[None, :], *earlier)
    wide = lax.all_to_all(gated[0], "head", split_axis=0, concat_axis=1, tiled=True).astype(F32)
    inv = lax.rsqrt(jnp.mean(wide * wide, -1, keepdims=True) + 1e-06)
    done = (wide * inv * norm_gain).astype(BF)[None]
    return done if before is None else jnp.concatenate([before, done], 0)


def after(value, *needed):
    return lax.optimization_barrier((value,) + needed)[0]


def sent(value, pairs, axis="ctx"):
    return lax.ppermute(value, axis, pairs)


def shards(queries, keys, values, gates, token_rates, fast_init, fast_rate, norm_gain):
    count = lax.axis_size("ctx")
    heads = lax.axis_size("head")
    rows, depth = queries.shape[1], queries.shape[2]
    reach = (WIN - 1) // rows + 1
    planes = count // reach
    if reach != 4 or WIN % rows or planes * reach != count or planes & (planes - 1):
        raise ValueError("unsupported shapes")
    position = lax.axis_index("ctx")
    plane, side, core = position // 4, (position // 2) % 2, position % 2
    ids = jnp.stack([plane, side, core, lax.axis_index("head")]).astype(jnp.int32)
    width = fast_init.shape[2] // 3
    half = width // 2
    everyone = range(count)
    local = fast_init[0]
    arrived = [swapped(local, 4 * m) for m in range(1, planes)]
    pair_0, pair_1, target = prepared(keys, values, token_rates)
    beside_0 = swapped(pair_0, 1)
    target_beside = swapped(target, 1)
    mine_w = jnp.stack([local] + arrived)
    other_w = swapped(after(mine_w, beside_0, target_beside), 2)
    beside_w = swapped(jnp.concatenate([mine_w, other_w], 0), 1)

    pieces = 2 * planes
    part = -(-3 * half // (16 * pieces)) * 16
    scratch = [pltpu.VMEM((pieces * part, depth), F32)]
    if local.shape[0] % 16:
        scratch.append(pltpu.VMEM((depth, 3 * width), F32))
    send, keep, whole = call(
        functools.partial(gradient_body, planes),
        (ids, mine_w, other_w, beside_w, pair_0, beside_0, target, target_beside),
        (
            jax.ShapeDtypeStruct((planes * part, depth), BF),
            jax.ShapeDtypeStruct((planes * part, depth), F32),
            jax.ShapeDtypeStruct((depth, 3 * width), BF),
        ),
        scratch=scratch,
        cost=cost_of(2 * 2 * rows * depth * half * 6, 4 * rows * depth * 4),
    )
    got = swapped(send, 2)
    parts = call(
        functools.partial(side_sum_body, planes),
        (ids, keep, got),
        tuple(jax.ShapeDtypeStruct((part, depth), F32 if m == 0 else BF) for m in range(planes)),
        scratch=(pltpu.VMEM((planes * part, depth), F32),),
        cost=cost_of(0, planes * part * depth * 8),
    )
    partial = [swapped(parts[m], 4 * m) for m in range(1, planes)]
    total = call(
        plane_sum_body,
        (ids, parts[0], *partial),
        jax.ShapeDtypeStruct((part, depth), BF),
        cost=cost_of(0, planes * part * depth * 3),
    )
    stacked = jnp.stack([total] + [swapped(total, 4 * m) for m in range(1, planes)])
    side_grad = jnp.concatenate([stacked, swapped(stacked, 2)], 0)
    core_grad = swapped(side_grad, 1)

    ring = [(i, (i + reach) % count) for i in everyone]
    far_0 = sent(after(pair_0, mine_w), ring)
    pair_1, far_0, _ = lax.optimization_barrier((pair_1, far_0, send))
    far_1 = sent(pair_1, ring)
    near_0 = swapped(picked(ids, pair_0, far_0), 2)
    near_1 = swapped(picked(ids, pair_1, far_1), 2)
    beside_1, far_beside_0, far_beside_1 = (swapped(v, 1) for v in (pair_1, far_0, far_1))
    diag_0, diag_1 = (swapped(v, 1) for v in (near_0, near_1))

    flipped, norms = call(
        weights_body,
        (ids, whole),
        (
            jax.ShapeDtypeStruct((3 * width, depth), F32),
            jax.ShapeDtypeStruct((3 * width, 1), F32),
        ),
        cost=cost_of(0, depth * width * 3 * 8),
    )
    attn_cost = cost_of(8 * rows * depth * 5 * rows, rows * depth * 30)
    if heads == 2:
        split = (jax.ShapeDtypeStruct((rows // 2, depth), BF),) * 2
    else:
        split = (jax.ShapeDtypeStruct((rows, depth), BF),)
    gated_first = group_call(
        first_group_body,
        0,
        ids,
        [queries, keys, values, gates],
        [whole],
        [far_0, near_0, beside_0, far_beside_0, diag_0],
        split,
        rows,
        depth,
        [pltpu.VMEM((rows, depth), BF)],
        attn_cost,
    )
    window_second = group_call(
        second_group_body,
        1,
        ids,
        [queries, keys, values],
        [],
        [far_0, far_1, near_0, near_1, beside_1, far_beside_0, far_beside_1, diag_0, diag_1],
        jax.ShapeDtypeStruct((rows, depth), F32),
        rows,
        depth,
        [],
        attn_cost,
    )
    done = finished(ids, 0, gated_first, norm_gain, None)

    def full(shape):
        return pl.BlockSpec(shape, lambda i, nd=len(shape): (0,) * nd)

    gated_second = pl.pallas_call(
        functools.partial(update_body, planes),
        grid=(1,),
        out_shape=split,
        in_specs=[
            pl.BlockSpec(memory_space=pltpu.SMEM),
            pl.BlockSpec(memory_space=pltpu.SMEM),
            full(side_grad.shape),
            full(core_grad.shape),
            full(flipped.shape),
            full(norms.shape),
            pl.BlockSpec((None, rows, depth), lambda i: (1, 0, 0)),
            full((rows, depth)),
            pl.BlockSpec((None, rows, depth), lambda i: (1, 0, 0)),
        ],
        out_specs=tuple(full(s.shape) for s in split),
        scratch_shapes=[
            pltpu.VMEM((2, pieces * part, depth), BF),
            pltpu.VMEM((rows, depth), BF),
        ],
        compiler_params=pltpu.CompilerParams(vmem_limit_bytes=VMEM_LIMIT),
        cost_estimate=cost_of(3e9, 4e6),
    )(ids, fast_rate, side_grad, core_grad, flipped, norms, queries, window_second, gates)
    return finished(ids, 1, gated_second, norm_gain, done)


def solution(mesh):
    placed = (
        P(None, "ctx", "head"),
        P(None, "ctx", "head"),
        P(None, "ctx", "head"),
        P(None, "ctx", "head"),
        P("ctx", "head"),
        P("head", "ctx", None),
        P("head"),
        P(),
    )
    return jax.shard_map(
        shards,
        mesh=mesh,
        in_specs=placed,
        out_specs=P(None, ("ctx", "head"), None),
        check_vma=False,
    )
```

```python
import functools

import jax
import jax.numpy as jnp
from jax import lax
from jax.experimental import pallas as pl
from jax.experimental.pallas import tpu as pltpu
from jax.sharding import PartitionSpec as P

WIN = 1024
A_COEF = 3.4445
B_COEF = -4.775
C_COEF = 2.0315
BF = jnp.bfloat16
F32 = jnp.float32
VMEM_LIMIT = 48 * 1024 * 1024


def dot_nn(a, b):
    return lax.dot_general(a, b, (((1,), (0,)), ((), ())), preferred_element_type=F32)


def dot_nt(a, b):
    return lax.dot_general(a, b, (((1,), (1,)), ((), ())), preferred_element_type=F32)


def dot_tn(a, b):
    return lax.dot_general(a, b, (((0,), (0,)), ((), ())), preferred_element_type=F32)


def swapped(value, mask, axis="ctx"):
    count = lax.axis_size(axis)
    return lax.ppermute(value, axis, [(i, i ^ mask) for i in range(count)])


def vmem_spec():
    return pl.BlockSpec(memory_space=pltpu.VMEM)


def call(body, args, outs, scratch=(), cost=None):
    return pl.pallas_call(
        body,
        out_shape=outs,
        in_specs=[pl.BlockSpec(memory_space=pltpu.SMEM)] + [vmem_spec()] * (len(args) - 1),
        out_specs=jax.tree.map(lambda _: vmem_spec(), outs),
        scratch_shapes=list(scratch),
        compiler_params=pltpu.CompilerParams(vmem_limit_bytes=VMEM_LIMIT),
        cost_estimate=cost,
    )(*args)


def cost_of(flops, moved):
    return pl.CostEstimate(flops=int(flops), bytes_accessed=int(moved), transcendentals=0)


def silu(v):
    return v / (1.0 + jnp.exp(-v))


def prepare_body(keys, values, rates, pair_0, pair_1, target, held, sems_in, sems_out):
    loads = [
        pltpu.make_async_copy(source.at[g], held.at[2 * g + which], sems_in.at[2 * g + which])
        for g in range(2)
        for which, source in enumerate((keys, values))
    ]
    stores = [
        pltpu.make_async_copy(
            held.at[2 * g + which], pair.at[which], sems_out.at[2 * g + which]
        )
        for g, pair in enumerate((pair_0, pair_1))
        for which in range(2)
    ]
    for load in loads:
        load.start()
    rows = target.shape[0]
    column = jnp.broadcast_to(rates[...], (128, rows)).T[:, :1]
    for load, store in zip(loads, stores):
        load.wait()
        store.start()
    target[...] = (-column * held[1].astype(F32)).astype(BF)
    for store in stores:
        store.wait()


def prepared(keys, values, rates):
    rows, depth = keys.shape[1:]
    anywhere = pl.BlockSpec(memory_space=pl.ANY)
    pair = jax.ShapeDtypeStruct((2, rows, depth), BF)
    return pl.pallas_call(
        prepare_body,
        out_shape=(pair, pair, jax.ShapeDtypeStruct((rows, depth), BF)),
        in_specs=[anywhere, anywhere, vmem_spec()],
        out_specs=(anywhere, anywhere, vmem_spec()),
        scratch_shapes=[
            pltpu.VMEM((4, rows, depth), BF),
            pltpu.SemaphoreType.DMA((4,)),
            pltpu.SemaphoreType.DMA((4,)),
        ],
        compiler_params=pltpu.CompilerParams(vmem_limit_bytes=VMEM_LIMIT),
        cost_estimate=cost_of(0, rows * depth * 8),
    )(keys, values, rates.reshape(1, rows))


def pick_body(ids, own, far, out, held, sems_in, sems_out):
    side = ids[1]
    half = held.shape[1] // 2
    parts = [(w, pl.ds(h * half, half)) for w in range(2) for h in range(2)]
    for condition, source in ((side == 0, own), (side == 1, far)):

        @pl.when(condition)
        def _():
            loads = [
                pltpu.make_async_copy(source.at[w, at], held.at[w, at], sems_in.at[i])
                for i, (w, at) in enumerate(parts)
            ]
            stores = [
                pltpu.make_async_copy(held.at[w, at], out.at[w, at], sems_out.at[i])
                for i, (w, at) in enumerate(parts)
            ]
            for load in loads:
                load.start()
            for load, store in zip(loads, stores):
                load.wait()
                store.start()
            for store in stores:
                store.wait()


def picked(ids, own, far):
    anywhere = pl.BlockSpec(memory_space=pl.ANY)
    return pl.pallas_call(
        pick_body,
        out_shape=jax.ShapeDtypeStruct(own.shape, own.dtype),
        in_specs=[pl.BlockSpec(memory_space=pltpu.SMEM), anywhere, anywhere],
        out_specs=anywhere,
        scratch_shapes=[
            pltpu.VMEM(own.shape, own.dtype),
            pltpu.SemaphoreType.DMA((4,)),
            pltpu.SemaphoreType.DMA((4,)),
        ],
        compiler_params=pltpu.CompilerParams(vmem_limit_bytes=VMEM_LIMIT),
        cost_estimate=cost_of(0, own.size * 4),
    )(ids, own, far)


def pack_body(*refs):
    for m, ref in enumerate(refs[:-1]):
        refs[-1][m] = ref[...]


def packed(*pieces):
    return pl.pallas_call(
        pack_body,
        out_shape=jax.ShapeDtypeStruct((len(pieces),) + pieces[0].shape, pieces[0].dtype),
        in_specs=[vmem_spec()] * len(pieces),
        out_specs=vmem_spec(),
        compiler_params=pltpu.CompilerParams(vmem_limit_bytes=VMEM_LIMIT),
        cost_estimate=cost_of(0, 4 * len(pieces) * pieces[0].size),
    )(*pieces)


def gradient_body(planes, ids, mine, other, beside_mine, beside_other, pair_a, pair_b, target_a, target_b, *refs):
    send, keep, whole, total = refs[:4]
    plane, side, core = ids[0], ids[1], ids[2]
    rows = mine.shape[1]
    target_ref = refs[4] if len(refs) > 4 else whole
    for m in range(planes):
        for far in range(2):
            block = ((plane ^ m) * 2 + (side if far == 0 else 1 - side)) * 2
            own_at = pl.multiple_of((block + core) * rows, rows)
            other_at = pl.multiple_of((block + 1 - core) * rows, rows)
            source = (mine, other)[far]
            target_ref[pl.ds(own_at, rows), :] = source[m].astype(target_ref.dtype)
            source = (beside_mine, beside_other)[far]
            target_ref[pl.ds(other_at, rows), :] = source[m].astype(target_ref.dtype)
    if target_ref is not whole:
        whole[...] = target_ref[...].astype(BF)
    width = whole.shape[1] // 3
    half = width // 2
    parts = [
        whole[:, pl.ds(pl.multiple_of(b * width + core * half, half), half)] for b in range(3)
    ]
    gate_up_w = jnp.concatenate(parts[:2], 1)
    out_w = parts[2]
    first = None
    for pair, target_rows in ((pair_a, target_a), (pair_b, target_b)):
        key_rows, target = pair[0], target_rows[...]
        gate_up = dot_nn(key_rows, gate_up_w)
        g, u = gate_up[:, :half], gate_up[:, half:]
        dh = dot_nn(target, out_w)
        s = 1.0 / (1.0 + jnp.exp(-g))
        gs = g * s
        hidden = (gs * u).astype(BF)
        dg = dh * u * s * (1.0 + g * (1.0 - s))
        du = dh * gs
        joined = jnp.concatenate([dg, du], 1).astype(BF)
        in_grad = dot_tn(joined, key_rows)
        out_grad = dot_tn(hidden, target)
        first = (in_grad, out_grad) if first is None else (first[0] + in_grad, first[1] + out_grad)
    total[: 2 * half, :] = first[0]
    total[2 * half : 3 * half, :] = first[1]
    if total.shape[0] > 3 * half:
        total[3 * half :, :] = jnp.zeros((total.shape[0] - 3 * half, total.shape[1]), F32)
    part = send.shape[0]
    send[...] = total[pl.ds(pl.multiple_of((1 - side) * part, part), part), :].astype(BF)
    keep[...] = total[pl.ds(pl.multiple_of(side * part, part), part), :]


def side_sum_body(planes, ids, keep, got, *refs):
    outs, total = refs[:planes], refs[planes]
    plane = ids[0]
    total[...] = keep[...] + got[...].astype(F32)
    part = outs[0].shape[0]
    for m in range(planes):
        rows = total[pl.ds(pl.multiple_of((plane ^ m) * part, part), part), :]
        outs[m][...] = rows.astype(outs[m].dtype)


def plane_sum_body(ids, own, *refs):
    total = own[...]
    for ref in refs[:-1]:
        total = total + ref[...].astype(F32)
    refs[-1][...] = total.astype(BF)


def weights_body(ids, whole, flipped, norms):
    width = whole.shape[1] // 3
    for b in range(3):
        cols = slice(b * width, (b + 1) * width)
        turned = whole[:, cols].astype(F32).T
        flipped[cols, :] = turned
        norms[cols, :] = jnp.sqrt(jnp.sum(turned * turned, 1, keepdims=True))


def fetch(slots, options):
    held, sems = slots
    for slot, choices in enumerate(options):
        for condition, source in choices:
            for which in range(2):
                copy = pltpu.make_async_copy(
                    source.at[which], held.at[slot, which], sems.at[slot, which]
                )
                if condition is None:
                    copy.start()
                else:
                    pl.when(condition)(copy.start)

    def wait(slot, which):
        part = held.at[slot, which]
        pltpu.make_async_copy(part, part, sems.at[slot, which]).wait()

    return wait


def window(q, k_own, v_own, held, wait, lives):
    rows, depth = q.shape
    scale = depth**-0.5
    row = lax.broadcasted_iota(jnp.int32, (rows, rows), 0)
    col = lax.broadcasted_iota(jnp.int32, (rows, rows), 1)
    scores = [jnp.where(col <= row, dot_nt(q, k_own) * scale, -1e30)]
    for slot in range(4):
        wait(slot, 0)
        s = dot_nt(q, held[slot, 0]) * scale
        allowed = col > row if slot == 0 else None
        if lives is not None:
            alive = jnp.full((rows, rows), lives[slot], jnp.int32) != 0
            allowed = alive if allowed is None else allowed & alive
        scores.append(s if allowed is None else jnp.where(allowed, s, -1e30))
    top = jnp.max(scores[0], -1, keepdims=True)
    for s in scores[1:]:
        top = jnp.maximum(top, jnp.max(s, -1, keepdims=True))
    total = None
    out = None
    for slot, s in enumerate(scores):
        e = jnp.exp(s - top)
        t = jnp.sum(e, -1, keepdims=True)
        if slot:
            wait(slot - 1, 1)
        o = dot_nn(e.astype(BF), v_own if slot == 0 else held[slot - 1, 1])
        total = t if total is None else total + t
        out = o if out is None else out + o
    return out / total


def first_group_body(ids, q, k_own, v_own, gates, whole, *refs):
    far, near, own_beside, far_beside, diag = refs[:5]
    outs, (held, sems, gated) = refs[5:-3], refs[-3:]
    plane, side, core = ids[0], ids[1], ids[2]
    wait = fetch(
        (held, sems),
        [
            [(None, far)],
            [(None, near)],
            [(core == 1, own_beside), (core == 0, far_beside)],
            [(None, diag)],
        ],
    )
    later = (plane > 0).astype(jnp.int32)
    side_live = jnp.maximum(later, side)
    core_live = jnp.maximum(later, core)
    lives = [later, side_live, core_live, side_live]
    width = whole.shape[1] // 3
    gate_up = dot_nn(q[0], whole[:, : 2 * width])
    hidden = (silu(gate_up[:, :width]) * gate_up[:, width:]).astype(BF)
    fast = dot_nt(hidden, whole[:, 2 * width :])
    win = window(q[0], k_own[0], v_own[0], held, wait, lives)
    gate = gates[0].astype(F32)
    spread(ids, ((win + fast) * silu(gate)).astype(BF), outs, gated)


def spread(ids, value, outs, held):
    if len(outs) == 1:
        outs[0][...] = value
        return
    held[...] = value
    rows = outs[0].shape[0]
    outs[0][...] = held[pl.ds(pl.multiple_of(ids[3] * rows, rows), rows), :]
    outs[1][...] = held[pl.ds(pl.multiple_of((1 - ids[3]) * rows, rows), rows), :]


def second_group_body(ids, q, k_own, v_own, *refs):
    far_0, far_1, near_0, near_1, own_beside, far_beside_0, far_beside_1 = refs[:7]
    diag_0, diag_1, out, held, sems = refs[7:]
    plane, side, core = ids[0], ids[1], ids[2]
    begin = plane == 0
    wrapped = begin & (side == 0)
    wait = fetch(
        (held, sems),
        [
            [(begin, far_0), (plane > 0, far_1)],
            [(wrapped, near_0), (jnp.logical_not(wrapped), near_1)],
            [
                (core == 1, own_beside),
                ((core == 0) & begin, far_beside_0),
                ((core == 0) & (plane > 0), far_beside_1),
            ],
            [(wrapped, diag_0), (jnp.logical_not(wrapped), diag_1)],
        ],
    )
    out[...] = window(q[0], k_own[0], v_own[0], held, wait, None)


def group_call(body, index, ids, grouped, whole, raw, outs, rows, depth, scratch, cost):
    def full(a):
        return pl.BlockSpec(a.shape, lambda i, nd=len(a.shape): (0,) * nd)

    specs = [pl.BlockSpec((1,) + a.shape[1:], lambda i: (index, 0, 0)) for a in grouped]
    specs += [full(a) for a in whole]
    specs += [pl.BlockSpec(memory_space=pl.ANY)] * len(raw)
    return pl.pallas_call(
        body,
        grid=(1,),
        out_shape=outs,
        in_specs=[pl.BlockSpec(memory_space=pltpu.SMEM)] + specs,
        out_specs=jax.tree.map(full, outs),
        scratch_shapes=[
            pltpu.VMEM((4, 2, rows, depth), BF),
            pltpu.SemaphoreType.DMA((4, 2)),
            *scratch,
        ],
        compiler_params=pltpu.CompilerParams(vmem_limit_bytes=VMEM_LIMIT),
        cost_estimate=cost,
    )(ids, *grouped, *whole, *raw)


def update_body(planes, ids, rate, mine, side_in, core_in, diag_in, flipped, norms, q, win, gates, *refs):
    outs, (grads, gated) = refs[:-2], refs[-2:]
    plane, side, core = ids[0], ids[1], ids[2]
    part = mine.shape[1]
    for m in range(planes):
        for far in range(2):
            base = ((side if far == 0 else 1 - side) * planes + (plane ^ m)) * part
            where = pl.ds(pl.multiple_of(base, part), part)
            grads[core, where, :] = (mine, side_in)[far][m]
            grads[1 - core, where, :] = (core_in, diag_in)[far][m]
    width = flipped.shape[0] // 3
    half = width // 2
    turned = []
    for b in range(3):
        block = jnp.concatenate(
            [grads[0, b * half : (b + 1) * half, :], grads[1, b * half : (b + 1) * half, :]], 0
        ).astype(F32)
        length = jnp.sqrt(jnp.sum(block * block, keepdims=True))
        turned.append((block / (length + 1e-06)).astype(BF))
    for _ in range(3):
        grams = [dot_nt(y, y) for y in turned]
        lows = [a.astype(BF) for a in grams]
        squares = [dot_nn(a, a) for a in lows]
        mixers = [(B_COEF * a + C_COEF * s).astype(BF) for a, s in zip(grams, squares)]
        turned = [
            (A_COEF * y.astype(F32) + dot_nn(b, y)).astype(BF) for b, y in zip(mixers, turned)
        ]
    fresh = []
    for b in range(3):
        cols = slice(b * width, (b + 1) * width)
        moved = flipped[cols, :] - rate[0] * turned[b].astype(F32)
        length = jnp.sqrt(jnp.sum(moved * moved, 1, keepdims=True))
        fresh.append((moved * (norms[cols, :] / (length + 1e-06))).astype(BF))
    x = q[...]
    g = dot_nt(x, fresh[0])
    u = dot_nt(x, fresh[1])
    hidden = (silu(g) * u).astype(BF)
    fast = dot_nn(hidden, fresh[2])
    gate = gates[...].astype(F32)
    spread(ids, ((win[...] + fast) * silu(gate)).astype(BF), outs, gated)


def norm_body(group, ids, own, got, gain, *refs):
    out, held, sems = refs[-3:]
    head = ids[3]
    rows, depth = own.shape
    chunk = rows // 4
    copies = []
    for c in range(4):
        at = slice(c * chunk, (c + 1) * chunk)
        a = own[at, :].astype(F32)
        b = got[at, :].astype(F32)
        low = jnp.where(head == 0, a, b)
        high = jnp.where(head == 0, b, a)
        square = jnp.sum(a * a, -1, keepdims=True) + jnp.sum(b * b, -1, keepdims=True)
        inv = lax.rsqrt(square / (2 * depth) + 1e-06)
        held[at, :depth] = (low * inv * gain[:, :depth]).astype(BF)
        held[at, depth:] = (high * inv * gain[:, depth:]).astype(BF)
        copies.append(pltpu.make_async_copy(held.at[at], out.at[group, at], sems.at[c]))
        copies[-1].start()
    for copy in copies:
        copy.wait()


def finished(ids, group, gated, norm_gain, before):
    total = norm_gain.shape[0]
    if len(gated) == 2:
        own, away = gated
        got = swapped(away, 1, "head")
        rows, depth = own.shape
        earlier = () if before is None else (before,)
        return pl.pallas_call(
            functools.partial(norm_body, group),
            out_shape=jax.ShapeDtypeStruct((2, rows, total), BF),
            in_specs=[
                pl.BlockSpec(memory_space=pltpu.SMEM),
                vmem_spec(),
                vmem_spec(),
                vmem_spec(),
                *([pl.BlockSpec(memory_space=pl.ANY)] * len(earlier)),
            ],
            out_specs=pl.BlockSpec(memory_space=pl.ANY),
            scratch_shapes=[pltpu.VMEM((rows, total), BF), pltpu.SemaphoreType.DMA((4,))],
            input_output_aliases={4: 0} if earlier else {},
            compiler_params=pltpu.CompilerParams(vmem_limit_bytes=VMEM_LIMIT),
            cost_estimate=cost_of(0, 4 * rows * total),
        )(ids, own, got, norm_gain[None, :], *earlier)
    wide = lax.all_to_all(gated[0], "head", split_axis=0, concat_axis=1, tiled=True).astype(F32)
    inv = lax.rsqrt(jnp.mean(wide * wide, -1, keepdims=True) + 1e-06)
    done = (wide * inv * norm_gain).astype(BF)[None]
    return done if before is None else jnp.concatenate([before, done], 0)


def after(value, *needed):
    return lax.optimization_barrier((value,) + needed)[0]


def sent(value, pairs, axis="ctx"):
    return lax.ppermute(value, axis, pairs)


def shards(queries, keys, values, gates, token_rates, fast_init, fast_rate, norm_gain):
    count = lax.axis_size("ctx")
    heads = lax.axis_size("head")
    rows, depth = queries.shape[1], queries.shape[2]
    reach = (WIN - 1) // rows + 1
    planes = count // reach
    if reach != 4 or WIN % rows or planes * reach != count or planes & (planes - 1):
        raise ValueError("unsupported shapes")
    position = lax.axis_index("ctx")
    plane, side, core = position // 4, (position // 2) % 2, position % 2
    ids = jnp.stack([plane, side, core, lax.axis_index("head")]).astype(jnp.int32)
    width = fast_init.shape[2] // 3
    half = width // 2
    everyone = range(count)
    local = fast_init[0]
    arrived = [swapped(local, 4 * m) for m in range(1, planes)]
    pair_0, pair_1, target = prepared(keys, values, token_rates)
    beside_0 = swapped(pair_0, 1)
    target_beside = swapped(target, 1)
    mine_w = packed(local, *arrived)
    other_w = swapped(after(mine_w, beside_0, target_beside), 2)
    beside_w = [swapped(w, 1) for w in (mine_w, other_w)]

    pieces = 2 * planes
    part = -(-3 * half // (16 * pieces)) * 16
    scratch = [pltpu.VMEM((pieces * part, depth), F32)]
    if local.shape[0] % 16:
        scratch.append(pltpu.VMEM((depth, 3 * width), F32))
    send, keep, whole = call(
        functools.partial(gradient_body, planes),
        (ids, mine_w, other_w, *beside_w, pair_0, beside_0, target, target_beside),
        (
            jax.ShapeDtypeStruct((planes * part, depth), BF),
            jax.ShapeDtypeStruct((planes * part, depth), F32),
            jax.ShapeDtypeStruct((depth, 3 * width), BF),
        ),
        scratch=scratch,
        cost=cost_of(2 * 2 * rows * depth * half * 6, 4 * rows * depth * 4),
    )
    got = swapped(send, 2)
    parts = call(
        functools.partial(side_sum_body, planes),
        (ids, keep, got),
        tuple(jax.ShapeDtypeStruct((part, depth), F32 if m == 0 else BF) for m in range(planes)),
        scratch=(pltpu.VMEM((planes * part, depth), F32),),
        cost=cost_of(0, planes * part * depth * 8),
    )
    partial = [swapped(parts[m], 4 * m) for m in range(1, planes)]
    total = call(
        plane_sum_body,
        (ids, parts[0], *partial),
        jax.ShapeDtypeStruct((part, depth), BF),
        cost=cost_of(0, planes * part * depth * 3),
    )
    plane_grad = packed(total, *[swapped(total, 4 * m) for m in range(1, planes)])
    side_grad = swapped(plane_grad, 2)
    grads = [plane_grad, side_grad] + [swapped(v, 1) for v in (plane_grad, side_grad)]

    ring = [(i, (i + reach) % count) for i in everyone]
    far_0 = sent(pair_0, ring)
    far_1 = sent(after(pair_1, mine_w), ring)
    near_0 = swapped(picked(ids, pair_0, after(far_0, got)), 2)
    near_1 = swapped(picked(ids, pair_1, after(far_1, total)), 2)
    beside_1, far_beside_0, far_beside_1 = (swapped(v, 1) for v in (pair_1, far_0, far_1))
    diag_0, diag_1 = (swapped(v, 1) for v in (near_0, near_1))

    flipped, norms = call(
        weights_body,
        (ids, whole),
        (
            jax.ShapeDtypeStruct((3 * width, depth), F32),
            jax.ShapeDtypeStruct((3 * width, 1), F32),
        ),
        cost=cost_of(0, depth * width * 3 * 8),
    )
    attn_cost = cost_of(8 * rows * depth * 5 * rows, rows * depth * 30)
    if heads == 2:
        split = (jax.ShapeDtypeStruct((rows // 2, depth), BF),) * 2
    else:
        split = (jax.ShapeDtypeStruct((rows, depth), BF),)
    gated_first = group_call(
        first_group_body,
        0,
        ids,
        [queries, keys, values, gates],
        [whole],
        [far_0, near_0, beside_0, far_beside_0, diag_0],
        split,
        rows,
        depth,
        [pltpu.VMEM((rows, depth), BF)],
        attn_cost,
    )
    window_second = group_call(
        second_group_body,
        1,
        ids,
        [queries, keys, values],
        [],
        [far_0, far_1, near_0, near_1, beside_1, far_beside_0, far_beside_1, diag_0, diag_1],
        jax.ShapeDtypeStruct((rows, depth), F32),
        rows,
        depth,
        [],
        attn_cost,
    )
    done = finished(ids, 0, gated_first, norm_gain, None)

    def full(shape):
        return pl.BlockSpec(shape, lambda i, nd=len(shape): (0,) * nd)

    gated_second = pl.pallas_call(
        functools.partial(update_body, planes),
        grid=(1,),
        out_shape=split,
        in_specs=[
            pl.BlockSpec(memory_space=pltpu.SMEM),
            pl.BlockSpec(memory_space=pltpu.SMEM),
            *[full(v.shape) for v in grads],
            full(flipped.shape),
            full(norms.shape),
            pl.BlockSpec((None, rows, depth), lambda i: (1, 0, 0)),
            full((rows, depth)),
            pl.BlockSpec((None, rows, depth), lambda i: (1, 0, 0)),
        ],
        out_specs=tuple(full(s.shape) for s in split),
        scratch_shapes=[
            pltpu.VMEM((2, pieces * part, depth), BF),
            pltpu.VMEM((rows, depth), BF),
        ],
        compiler_params=pltpu.CompilerParams(vmem_limit_bytes=VMEM_LIMIT),
        cost_estimate=cost_of(3e9, 4e6),
    )(ids, fast_rate, *grads, flipped, norms, queries, window_second, gates)
    return finished(ids, 1, gated_second, norm_gain, done)


def solution(mesh):
    placed = (
        P(None, "ctx", "head"),
        P(None, "ctx", "head"),
        P(None, "ctx", "head"),
        P(None, "ctx", "head"),
        P("ctx", "head"),
        P("head", "ctx", None),
        P("head"),
        P(),
    )
    return jax.shard_map(
        shards,
        mesh=mesh,
        in_specs=placed,
        out_specs=P(None, ("ctx", "head"), None),
        check_vma=False,
    )
```

```python
import functools

import jax
import jax.numpy as jnp
from jax import lax
from jax.experimental import pallas as pl
from jax.experimental.pallas import tpu as pltpu
from jax.sharding import PartitionSpec as P

WIN = 1024
A_COEF = 3.4445
B_COEF = -4.775
C_COEF = 2.0315
BF = jnp.bfloat16
F32 = jnp.float32
VMEM_LIMIT = 32 * 1024 * 1024


def dot_nn(a, b):
    return lax.dot_general(a, b, (((1,), (0,)), ((), ())), preferred_element_type=F32)


def dot_nt(a, b):
    return lax.dot_general(a, b, (((1,), (1,)), ((), ())), preferred_element_type=F32)


def dot_tn(a, b):
    return lax.dot_general(a, b, (((0,), (0,)), ((), ())), preferred_element_type=F32)


def swapped(value, mask, axis="ctx"):
    count = lax.axis_size(axis)
    return lax.ppermute(value, axis, [(i, i ^ mask) for i in range(count)])


def vmem_spec():
    return pl.BlockSpec(memory_space=pltpu.VMEM)


def call(body, args, outs, scratch=(), cost=None):
    return pl.pallas_call(
        body,
        out_shape=outs,
        in_specs=[pl.BlockSpec(memory_space=pltpu.SMEM)] + [vmem_spec()] * (len(args) - 1),
        out_specs=jax.tree.map(lambda _: vmem_spec(), outs),
        scratch_shapes=list(scratch),
        compiler_params=pltpu.CompilerParams(vmem_limit_bytes=VMEM_LIMIT),
        cost_estimate=cost,
    )(*args)


def cost_of(flops, moved):
    return pl.CostEstimate(flops=int(flops), bytes_accessed=int(moved), transcendentals=0)


def silu(v):
    return v / (1.0 + jnp.exp(-v))


def hold_body(keys, values, rates, held_keys, held_values, held_rates):
    held_keys[...] = keys[...]
    held_values[...] = values[...]
    held_rates[...] = rates[...]


def held(keys, values, rates):
    def block(a):
        return pl.BlockSpec((1,) + a.shape[1:], lambda i: (i, 0, 0))

    specs = (block(keys), block(values), pl.BlockSpec(rates.shape, lambda i: (0, 0)))
    return pl.pallas_call(
        hold_body,
        grid=(2,),
        out_shape=tuple(jax.ShapeDtypeStruct(a.shape, a.dtype) for a in (keys, values, rates)),
        in_specs=list(specs),
        out_specs=specs,
        compiler_params=pltpu.CompilerParams(vmem_limit_bytes=VMEM_LIMIT),
        cost_estimate=cost_of(0, keys.size * 8),
    )(keys, values, rates)


def pick_body(ids, own, far, out):
    out[...] = jnp.where(ids[1] == 0, own[...], far[...])


def picked(ids, own, far):
    return call(
        pick_body,
        (ids, own, far),
        jax.ShapeDtypeStruct(own.shape, own.dtype),
        cost=cost_of(0, own.size * 4),
    )


def pack_body(*refs):
    for m, ref in enumerate(refs[:-1]):
        refs[-1][m] = ref[...]


def packed(*pieces):
    return pl.pallas_call(
        pack_body,
        out_shape=jax.ShapeDtypeStruct((len(pieces),) + pieces[0].shape, pieces[0].dtype),
        in_specs=[vmem_spec()] * len(pieces),
        out_specs=vmem_spec(),
        compiler_params=pltpu.CompilerParams(vmem_limit_bytes=VMEM_LIMIT),
        cost_estimate=cost_of(0, 4 * len(pieces) * pieces[0].size),
    )(*pieces)


def gradient_body(planes, ids, mine, other, beside_mine, beside_other, *refs):
    (keys, values, rates, keys_in, values_in, rates_in), refs = refs[:6], refs[6:]
    send, keep, whole, total = refs[:4]
    plane, side, core = ids[0], ids[1], ids[2]
    rows = mine.shape[1]
    target_ref = refs[4] if len(refs) > 4 else whole
    for m in range(planes):
        holder = 1 - core if m == 0 else core
        for far in range(2):
            block = ((plane ^ m) * 2 + (side if far == 0 else 1 - side)) * 2
            for source, at in (((mine, other)[far], holder), ((beside_mine, beside_other)[far], 1 - holder)):
                where = pl.ds(pl.multiple_of((block + at) * rows, rows), rows)
                target_ref[where, :] = source[m].astype(target_ref.dtype)
    if target_ref is not whole:
        whole[...] = target_ref[...].astype(BF)
    width = whole.shape[1] // 3
    half = width // 2
    parts = [
        whole[:, pl.ds(pl.multiple_of(b * width + core * half, half), half)] for b in range(3)
    ]
    gate_up_w = jnp.concatenate(parts[:2], 1)
    out_w = parts[2]
    first = None
    for key_ref, value_ref, rate in ((keys, values, rates), (keys_in, values_in, rates_in)):
        key_rows = key_ref[0]
        column = jnp.broadcast_to(rate[...], (128, rate.shape[1])).T[:, :1]
        target = (-column * value_ref[0].astype(F32)).astype(BF)
        gate_up = dot_nn(key_rows, gate_up_w)
        g, u = gate_up[:, :half], gate_up[:, half:]
        dh = dot_nn(target, out_w)
        s = 1.0 / (1.0 + jnp.exp(-g))
        gs = g * s
        hidden = (gs * u).astype(BF)
        dg = dh * u * s * (1.0 + g * (1.0 - s))
        du = dh * gs
        joined = jnp.concatenate([dg, du], 1).astype(BF)
        in_grad = dot_tn(joined, key_rows)
        out_grad = dot_tn(hidden, target)
        first = (in_grad, out_grad) if first is None else (first[0] + in_grad, first[1] + out_grad)
    total[: 2 * half, :] = first[0]
    total[2 * half : 3 * half, :] = first[1]
    if total.shape[0] > 3 * half:
        total[3 * half :, :] = jnp.zeros((total.shape[0] - 3 * half, total.shape[1]), F32)
    part = send.shape[0]
    send[...] = total[pl.ds(pl.multiple_of((1 - side) * part, part), part), :].astype(BF)
    keep[...] = total[pl.ds(pl.multiple_of(side * part, part), part), :]


def side_sum_body(planes, ids, keep, got, *refs):
    outs, total = refs[:planes], refs[planes]
    plane = ids[0]
    total[...] = keep[...] + got[...].astype(F32)
    part = outs[0].shape[0]
    for m in range(planes):
        rows = total[pl.ds(pl.multiple_of((plane ^ m) * part, part), part), :]
        outs[m][...] = rows.astype(outs[m].dtype)


def plane_sum_body(ids, own, *refs):
    total = own[...]
    for ref in refs[:-1]:
        total = total + ref[...].astype(F32)
    refs[-1][...] = total.astype(BF)


def weights_body(ids, whole, flipped, norms):
    width = whole.shape[1] // 3
    for b in range(3):
        cols = slice(b * width, (b + 1) * width)
        turned = whole[:, cols].astype(F32).T
        flipped[cols, :] = turned
        norms[cols, :] = jnp.sqrt(jnp.sum(turned * turned, 1, keepdims=True))


def blocks_of(ids, group, own, far, near, beside, far_beside, diag):
    plane, side, core = ids[0], ids[1], ids[2]
    moved = group if group == 0 else jnp.where(plane == 0, 0, group)
    crossed = group if group == 0 else jnp.where((plane == 0) & (side == 0), 0, group)
    return [
        own[group],
        far[moved],
        near[crossed],
        jnp.where(core == 1, beside[group], far_beside[moved]),
        diag[crossed],
    ]


def scores_body(ids, queries, *refs):
    key_refs, whole, (weights, totals, fast) = refs[:6], refs[6], refs[7:]
    plane, side, core = ids[0], ids[1], ids[2]
    later = (plane > 0).astype(jnp.int32)
    side_live, core_live = jnp.maximum(later, side), jnp.maximum(later, core)
    rows, depth = queries.shape[1:]
    scale = depth**-0.5
    row = lax.broadcasted_iota(jnp.int32, (rows, rows), 0)
    col = lax.broadcasted_iota(jnp.int32, (rows, rows), 1)
    for group in range(2):
        q = queries[group]
        scores = []
        lives = [None, later, side_live, core_live, side_live]
        for slot, keys in enumerate(blocks_of(ids, group, *key_refs)):
            s = dot_nt(q, keys) * scale
            allowed = {0: col <= row, 1: col > row}.get(slot)
            if group == 0 and slot:
                alive = jnp.full((rows, rows), lives[slot], jnp.int32) != 0
                allowed = alive if allowed is None else allowed & alive
            scores.append(s if allowed is None else jnp.where(allowed, s, -1e30))
        top = jnp.max(scores[0], -1, keepdims=True)
        for s in scores[1:]:
            top = jnp.maximum(top, jnp.max(s, -1, keepdims=True))
        total = None
        for slot, s in enumerate(scores):
            e = jnp.exp(s - top)
            t = jnp.sum(e, -1, keepdims=True)
            total = t if total is None else total + t
            weights[group, slot] = e.astype(BF)
        totals[group] = total
    width = whole.shape[1] // 3
    gate_up = dot_nn(queries[0], whole[:, : 2 * width])
    hidden = (silu(gate_up[:, :width]) * gate_up[:, width:]).astype(BF)
    fast[...] = dot_nt(hidden, whole[:, 2 * width :])


def mix_body(ids, *refs):
    value_refs, (weights, totals, fast, gates), refs = refs[:6], refs[6:10], refs[10:]
    win, outs, gated = refs[0], refs[1:-1], refs[-1]
    for group in range(2):
        out = None
        for slot, values in enumerate(blocks_of(ids, group, *value_refs)):
            o = dot_nn(weights[group, slot], values)
            out = o if out is None else out + o
        out = out / totals[group]
        if group == 0:
            gate = gates[0].astype(F32)
            spread(ids, ((out + fast[...]) * silu(gate)).astype(BF), outs, gated)
        else:
            win[...] = out


def spread(ids, value, outs, held):
    if len(outs) == 1:
        outs[0][...] = value
        return
    held[...] = value
    rows = outs[0].shape[0]
    outs[0][...] = held[pl.ds(pl.multiple_of(ids[3] * rows, rows), rows), :]
    outs[1][...] = held[pl.ds(pl.multiple_of((1 - ids[3]) * rows, rows), rows), :]


def update_body(planes, ids, rate, mine, side_in, core_in, diag_in, flipped, norms, q, win, gates, *refs):
    outs, (grads, gated) = refs[:-2], refs[-2:]
    plane, side, core = ids[0], ids[1], ids[2]
    part = mine.shape[1]
    for m in range(planes):
        for far in range(2):
            base = ((side if far == 0 else 1 - side) * planes + (plane ^ m)) * part
            where = pl.ds(pl.multiple_of(base, part), part)
            grads[core, where, :] = (mine, side_in)[far][m]
            grads[1 - core, where, :] = (core_in, diag_in)[far][m]
    width = flipped.shape[0] // 3
    half = width // 2
    turned = []
    for b in range(3):
        block = jnp.concatenate(
            [grads[0, b * half : (b + 1) * half, :], grads[1, b * half : (b + 1) * half, :]], 0
        ).astype(F32)
        length = jnp.sqrt(jnp.sum(block * block, keepdims=True))
        turned.append((block / (length + 1e-06)).astype(BF))
    for _ in range(3):
        grams = [dot_nt(y, y) for y in turned]
        lows = [a.astype(BF) for a in grams]
        squares = [dot_nn(a, a) for a in lows]
        mixers = [(B_COEF * a + C_COEF * s).astype(BF) for a, s in zip(grams, squares)]
        turned = [
            (A_COEF * y.astype(F32) + dot_nn(b, y)).astype(BF) for b, y in zip(mixers, turned)
        ]
    fresh = []
    for b in range(3):
        cols = slice(b * width, (b + 1) * width)
        moved = flipped[cols, :] - rate[0] * turned[b].astype(F32)
        length = jnp.sqrt(jnp.sum(moved * moved, 1, keepdims=True))
        fresh.append((moved * (norms[cols, :] / (length + 1e-06))).astype(BF))
    x = q[...]
    g = dot_nt(x, fresh[0])
    u = dot_nt(x, fresh[1])
    hidden = (silu(g) * u).astype(BF)
    fast = dot_nn(hidden, fresh[2])
    gate = gates[...].astype(F32)
    spread(ids, ((win[...] + fast) * silu(gate)).astype(BF), outs, gated)


def norm_body(group, ids, own, got, gain, *refs):
    out, held, sems = refs[-3:]
    head = ids[3]
    rows, depth = own.shape
    chunk = rows // 4
    copies = []
    for c in range(4):
        at = slice(c * chunk, (c + 1) * chunk)
        a = own[at, :].astype(F32)
        b = got[at, :].astype(F32)
        low = jnp.where(head == 0, a, b)
        high = jnp.where(head == 0, b, a)
        square = jnp.sum(a * a, -1, keepdims=True) + jnp.sum(b * b, -1, keepdims=True)
        inv = lax.rsqrt(square / (2 * depth) + 1e-06)
        held[at, :depth] = (low * inv * gain[:, :depth]).astype(BF)
        held[at, depth:] = (high * inv * gain[:, depth:]).astype(BF)
        copies.append(pltpu.make_async_copy(held.at[at], out.at[group, at], sems.at[c]))
        copies[-1].start()
    for copy in copies:
        copy.wait()


def finished(ids, group, gated, norm_gain, before):
    total = norm_gain.shape[0]
    if len(gated) == 2:
        own, away = gated
        got = swapped(away, 1, "head")
        rows, depth = own.shape
        earlier = () if before is None else (before,)
        return pl.pallas_call(
            functools.partial(norm_body, group),
            out_shape=jax.ShapeDtypeStruct((2, rows, total), BF),
            in_specs=[
                pl.BlockSpec(memory_space=pltpu.SMEM),
                vmem_spec(),
                vmem_spec(),
                vmem_spec(),
                *([pl.BlockSpec(memory_space=pl.ANY)] * len(earlier)),
            ],
            out_specs=pl.BlockSpec(memory_space=pl.ANY),
            scratch_shapes=[pltpu.VMEM((rows, total), BF), pltpu.SemaphoreType.DMA((4,))],
            input_output_aliases={4: 0} if earlier else {},
            compiler_params=pltpu.CompilerParams(vmem_limit_bytes=VMEM_LIMIT),
            cost_estimate=cost_of(0, 4 * rows * total),
        )(ids, own, got, norm_gain[None, :], *earlier)
    wide = lax.all_to_all(gated[0], "head", split_axis=0, concat_axis=1, tiled=True).astype(F32)
    inv = lax.rsqrt(jnp.mean(wide * wide, -1, keepdims=True) + 1e-06)
    done = (wide * inv * norm_gain).astype(BF)[None]
    return done if before is None else jnp.concatenate([before, done], 0)


def after(value, *needed):
    return lax.optimization_barrier((value,) + needed)[0]


def sent(value, pairs, axis="ctx"):
    return lax.ppermute(value, axis, pairs)


def shards(queries, keys, values, gates, token_rates, fast_init, fast_rate, norm_gain):
    count = lax.axis_size("ctx")
    heads = lax.axis_size("head")
    rows, depth = queries.shape[1], queries.shape[2]
    reach = (WIN - 1) // rows + 1
    planes = count // reach
    if reach != 4 or WIN % rows or planes * reach != count or planes & (planes - 1):
        raise ValueError("unsupported shapes")
    position = lax.axis_index("ctx")
    plane, side, core = position // 4, (position // 2) % 2, position % 2
    ids = jnp.stack([plane, side, core, lax.axis_index("head")]).astype(jnp.int32)
    width = fast_init.shape[2] // 3
    half = width // 2
    everyone = range(count)
    local = fast_init[0]
    local_in = swapped(local, 1)
    arrived = [swapped(after(local, local_in) if m == 1 else local, 4 * m) for m in range(1, planes)]
    rates = token_rates.reshape(1, rows)
    keys_in, values_in, rates_in = (swapped(v, 1) for v in (keys, values, rates))
    mine_w = packed(local_in, *arrived)
    other_w = swapped(mine_w, 2)
    own_keys, own_values, own_rates = held(keys, values, rates)
    beside_w = [swapped(mine_w, 1), swapped(after(other_w, own_keys), 1)]

    pieces = 2 * planes
    part = -(-3 * half // (16 * pieces)) * 16
    scratch = [pltpu.VMEM((pieces * part, depth), F32)]
    if local.shape[0] % 16:
        scratch.append(pltpu.VMEM((depth, 3 * width), F32))
    send, keep, whole = call(
        functools.partial(gradient_body, planes),
        (ids, mine_w, other_w, *beside_w)
        + (own_keys, own_values, own_rates, keys_in, values_in, rates_in),
        (
            jax.ShapeDtypeStruct((planes * part, depth), BF),
            jax.ShapeDtypeStruct((planes * part, depth), F32),
            jax.ShapeDtypeStruct((depth, 3 * width), BF),
        ),
        scratch=scratch,
        cost=cost_of(2 * 2 * rows * depth * half * 6, 4 * rows * depth * 4),
    )
    got = swapped(send, 2)

    flipped, norms = call(
        weights_body,
        (ids, whole),
        (
            jax.ShapeDtypeStruct((3 * width, depth), F32),
            jax.ShapeDtypeStruct((3 * width, 1), F32),
        ),
        cost=cost_of(0, depth * width * 3 * 8),
    )
    parts = call(
        functools.partial(side_sum_body, planes),
        (ids, after(keep, flipped), got),
        tuple(jax.ShapeDtypeStruct((part, depth), F32 if m == 0 else BF) for m in range(planes)),
        scratch=(pltpu.VMEM((planes * part, depth), F32),),
        cost=cost_of(0, planes * part * depth * 8),
    )
    partial = [swapped(parts[m], 4 * m) for m in range(1, planes)]
    ring = [(i, (i + reach) % count) for i in everyone]
    far_keys = sent(after(keys, *arrived), ring)
    far_values = sent(after(values, send), ring)
    near_keys = swapped(picked(ids, own_keys, after(far_keys, got)), 2)
    pick_values = picked(ids, own_values, after(far_values, parts[0]))
    near_values = swapped(after(pick_values, *partial), 2)

    total = call(
        plane_sum_body,
        (ids, after(parts[0], pick_values), *partial),
        jax.ShapeDtypeStruct((part, depth), BF),
        cost=cost_of(0, planes * part * depth * 3),
    )
    far_keys_in = swapped(after(far_keys, total), 1)
    near_keys_in = swapped(after(near_keys, total), 1)
    all_keys = [own_keys, far_keys, near_keys, keys_in, far_keys_in, near_keys_in]
    planes_grad = [
        swapped(total if m < planes - 1 else after(total, far_keys_in, near_keys_in), 4 * m)
        for m in range(1, planes)
    ]

    if heads == 2:
        split = (jax.ShapeDtypeStruct((rows // 2, depth), BF),) * 2
    else:
        split = (jax.ShapeDtypeStruct((rows, depth), BF),)
    attn_cost = cost_of(6 * rows * depth * 10 * rows, rows * depth * 40)
    weights, totals, fast_first = call(
        scores_body,
        (ids, queries, *all_keys, whole),
        (
            jax.ShapeDtypeStruct((2, reach + 1, rows, rows), BF),
            jax.ShapeDtypeStruct((2, rows, 1), F32),
            jax.ShapeDtypeStruct((rows, depth), F32),
        ),
        cost=attn_cost,
    )
    plane_grad = packed(after(total, totals), *planes_grad)
    far_values_in = swapped(after(far_values, plane_grad), 1)
    near_values_in = swapped(after(near_values, plane_grad), 1)
    all_values = [own_values, far_values, near_values, values_in, far_values_in, near_values_in]
    window_second, *gated_first = call(
        mix_body,
        (ids, *all_values, weights, totals, fast_first, gates),
        (jax.ShapeDtypeStruct((rows, depth), F32), *split),
        scratch=(pltpu.VMEM((rows, depth), BF),),
        cost=attn_cost,
    )
    side_grad = swapped(plane_grad, 2)
    beside_grad = [swapped(plane_grad, 1), swapped(after(side_grad, window_second), 1)]
    grads = [plane_grad, side_grad, *beside_grad]
    done = finished(ids, 0, gated_first, norm_gain, None)

    def full(shape):
        return pl.BlockSpec(shape, lambda i, nd=len(shape): (0,) * nd)

    gated_second = pl.pallas_call(
        functools.partial(update_body, planes),
        grid=(1,),
        out_shape=split,
        in_specs=[
            pl.BlockSpec(memory_space=pltpu.SMEM),
            pl.BlockSpec(memory_space=pltpu.SMEM),
            *[full(v.shape) for v in grads],
            full(flipped.shape),
            full(norms.shape),
            pl.BlockSpec((None, rows, depth), lambda i: (1, 0, 0)),
            full((rows, depth)),
            pl.BlockSpec((None, rows, depth), lambda i: (1, 0, 0)),
        ],
        out_specs=tuple(full(s.shape) for s in split),
        scratch_shapes=[
            pltpu.VMEM((2, pieces * part, depth), BF),
            pltpu.VMEM((rows, depth), BF),
        ],
        compiler_params=pltpu.CompilerParams(vmem_limit_bytes=VMEM_LIMIT),
        cost_estimate=cost_of(3e9, 4e6),
    )(ids, fast_rate, *grads, flipped, norms, queries, window_second, gates)
    return finished(ids, 1, gated_second, norm_gain, done)


def solution(mesh):
    placed = (
        P(None, "ctx", "head"),
        P(None, "ctx", "head"),
        P(None, "ctx", "head"),
        P(None, "ctx", "head"),
        P("ctx", "head"),
        P("head", "ctx", None),
        P("head"),
        P(),
    )
    return jax.shard_map(
        shards,
        mesh=mesh,
        in_specs=placed,
        out_specs=P(None, ("ctx", "head"), None),
        check_vma=False,
    )
```

```python
import functools

import jax
import jax.numpy as jnp
from jax import lax
from jax.experimental import pallas as pl
from jax.experimental.pallas import tpu as pltpu
from jax.sharding import PartitionSpec as P

WIN = 1024
A_COEF = 3.4445
B_COEF = -4.775
C_COEF = 2.0315
BF = jnp.bfloat16
F32 = jnp.float32
VMEM_LIMIT = 32 * 1024 * 1024


def dot_nn(a, b):
    return lax.dot_general(a, b, (((1,), (0,)), ((), ())), preferred_element_type=F32)


def dot_nt(a, b):
    return lax.dot_general(a, b, (((1,), (1,)), ((), ())), preferred_element_type=F32)


def dot_tn(a, b):
    return lax.dot_general(a, b, (((0,), (0,)), ((), ())), preferred_element_type=F32)


def swapped(value, mask, axis="ctx"):
    count = lax.axis_size(axis)
    return lax.ppermute(value, axis, [(i, i ^ mask) for i in range(count)])


def place():
    position = lax.axis_index("ctx")
    return position >> 2, (position >> 1) & 1, position & 1, lax.axis_index("head")


def vmem_spec():
    return pl.BlockSpec(memory_space=pltpu.VMEM)


def call(body, args, outs, scratch=(), cost=None):
    return pl.pallas_call(
        body,
        out_shape=outs,
        in_specs=[vmem_spec()] * len(args),
        out_specs=jax.tree.map(lambda _: vmem_spec(), outs),
        scratch_shapes=list(scratch),
        compiler_params=pltpu.CompilerParams(vmem_limit_bytes=VMEM_LIMIT),
        cost_estimate=cost,
    )(*args)


def cost_of(flops, moved):
    return pl.CostEstimate(flops=int(flops), bytes_accessed=int(moved), transcendentals=0)


def sigmoid(v):
    return 0.5 * jnp.tanh(0.5 * v) + 0.5


def silu(v):
    return v * sigmoid(v)


def hold_body(keys, values, rates, rate, held_keys, held_values, held_rates, held_rate):
    held_keys[...] = keys[...]
    held_values[...] = values[...]
    held_rates[...] = rates[...]
    held_rate[...] = jnp.broadcast_to(rate[...], held_rate.shape)


def held(keys, values, rates, rate):
    outs = tuple(jax.ShapeDtypeStruct(a.shape, a.dtype) for a in (keys, values, rates))
    outs += (jax.ShapeDtypeStruct((8, 128), rate.dtype),)
    return call(hold_body, (keys, values, rates, rate), outs)


def pick_body(own, far, out):
    out[...] = jnp.where(place()[1] == 0, own[...], far[...])


def picked(own, far):
    return call(
        pick_body,
        (own, far),
        jax.ShapeDtypeStruct(own.shape, own.dtype),
        cost=cost_of(0, own.size * 4),
    )


def pack_body(*refs):
    for m, ref in enumerate(refs[:-1]):
        refs[-1][m] = ref[...]


def packed(*pieces):
    return pl.pallas_call(
        pack_body,
        out_shape=jax.ShapeDtypeStruct((len(pieces),) + pieces[0].shape, pieces[0].dtype),
        in_specs=[vmem_spec()] * len(pieces),
        out_specs=vmem_spec(),
        compiler_params=pltpu.CompilerParams(vmem_limit_bytes=VMEM_LIMIT),
        cost_estimate=cost_of(0, 4 * len(pieces) * pieces[0].size),
    )(*pieces)


def gradient_body(planes, mine, other, beside_mine, beside_other, *refs):
    (keys, values, rates, keys_in, values_in, rates_in), refs = refs[:6], refs[6:]
    send, keep, whole, total = refs[:4]
    plane, side, core, _ = place()
    rows = mine.shape[1]
    target_ref = refs[4] if len(refs) > 4 else whole
    for m in range(planes):
        holder = 1 - core if m == 0 else core
        for far in range(2):
            block = ((plane ^ m) * 2 + (side if far == 0 else 1 - side)) * 2
            for source, at in (((mine, other)[far], holder), ((beside_mine, beside_other)[far], 1 - holder)):
                where = pl.ds(pl.multiple_of((block + at) * rows, rows), rows)
                target_ref[where, :] = source[m].astype(target_ref.dtype)
    if target_ref is not whole:
        whole[...] = target_ref[...].astype(BF)
    width = whole.shape[1] // 3
    half = width // 2
    parts = [
        whole[:, pl.ds(pl.multiple_of(b * width + core * half, half), half)] for b in range(3)
    ]
    gate_up_w = jnp.concatenate(parts[:2], 1)
    out_w = parts[2]
    first = None
    for key_ref, value_ref, rate in ((keys, values, rates), (keys_in, values_in, rates_in)):
        key_rows = key_ref[0]
        column = jnp.broadcast_to(rate[...], (128, rate.shape[1])).T[:, :1]
        target = (-column * value_ref[0].astype(F32)).astype(BF)
        gate_up = dot_nn(key_rows, gate_up_w)
        g, u = gate_up[:, :half], gate_up[:, half:]
        dh = dot_nn(target, out_w)
        s = sigmoid(g)
        gs = g * s
        hidden = (gs * u).astype(BF)
        dg = dh * u * s * (1.0 + g * (1.0 - s))
        du = dh * gs
        joined = jnp.concatenate([dg, du], 1).astype(BF)
        in_grad = dot_tn(joined, key_rows)
        out_grad = dot_tn(hidden, target)
        first = (in_grad, out_grad) if first is None else (first[0] + in_grad, first[1] + out_grad)
    total[: 2 * half, :] = first[0]
    total[2 * half : 3 * half, :] = first[1]
    if total.shape[0] > 3 * half:
        total[3 * half :, :] = jnp.zeros((total.shape[0] - 3 * half, total.shape[1]), F32)
    part = send.shape[0]
    send[...] = total[pl.ds(pl.multiple_of((1 - side) * part, part), part), :].astype(BF)
    keep[...] = total[pl.ds(pl.multiple_of(side * part, part), part), :]


def side_sum_body(planes, keep, got, *refs):
    outs, total = refs[:planes], refs[planes]
    plane = place()[0]
    total[...] = keep[...] + got[...].astype(F32)
    part = outs[0].shape[0]
    for m in range(planes):
        rows = total[pl.ds(pl.multiple_of((plane ^ m) * part, part), part), :]
        outs[m][...] = rows.astype(outs[m].dtype)


def plane_sum_body(own, *refs):
    total = own[...]
    for ref in refs[:-1]:
        total = total + ref[...].astype(F32)
    refs[-1][...] = total.astype(BF)


def weights_body(whole, flipped, norms):
    width = whole.shape[1] // 3
    for b in range(3):
        cols = slice(b * width, (b + 1) * width)
        turned = whole[:, cols].astype(F32).T
        flipped[cols, :] = turned
        norms[cols, :] = jnp.sqrt(jnp.sum(turned * turned, 1, keepdims=True))


def blocks_of(group, own, far, near, beside, far_beside, diag):
    plane, side, core, _ = place()
    moved = group if group == 0 else jnp.where(plane == 0, 0, group)
    crossed = group if group == 0 else jnp.where((plane == 0) & (side == 0), 0, group)
    return [
        own[group],
        far[moved],
        near[crossed],
        jnp.where(core == 1, beside[group], far_beside[moved]),
        diag[crossed],
    ]


def scores_body(queries, *refs):
    key_refs, whole, (weights, inverses, fast) = refs[:6], refs[6], refs[7:]
    plane, side, core, _ = place()
    later = (plane > 0).astype(jnp.int32)
    side_live, core_live = jnp.maximum(later, side), jnp.maximum(later, core)
    rows, depth = queries.shape[1:]
    scale = depth**-0.5
    row = lax.broadcasted_iota(jnp.int32, (rows, rows), 0)
    col = lax.broadcasted_iota(jnp.int32, (rows, rows), 1)
    for group in range(2):
        q = queries[group]
        scores = []
        lives = [None, later, side_live, core_live, side_live]
        for slot, keys in enumerate(blocks_of(group, *key_refs)):
            s = dot_nt(q, keys) * scale
            allowed = {0: col <= row, 1: col > row}.get(slot)
            if group == 0 and slot:
                alive = jnp.full((rows, rows), lives[slot], jnp.int32) != 0
                allowed = alive if allowed is None else allowed & alive
            scores.append(s if allowed is None else jnp.where(allowed, s, -1e30))
        top = jnp.max(scores[0], -1, keepdims=True)
        for s in scores[1:]:
            top = jnp.maximum(top, jnp.max(s, -1, keepdims=True))
        total = None
        for slot, s in enumerate(scores):
            e = jnp.exp(s - top)
            t = jnp.sum(e, -1, keepdims=True)
            total = t if total is None else total + t
            weights[group, slot] = e.astype(BF)
        inverses[group] = 1.0 / total
    width = whole.shape[1] // 3
    gate_up = dot_nn(queries[0], whole[:, : 2 * width])
    hidden = (silu(gate_up[:, :width]) * gate_up[:, width:]).astype(BF)
    fast[...] = dot_nt(hidden, whole[:, 2 * width :])


def mixed(group, value_refs, weights, inverses):
    out = None
    for slot, values in enumerate(blocks_of(group, *value_refs)):
        o = dot_nn(weights[group, slot], values)
        out = o if out is None else out + o
    return out * inverses[group]


def mix_body(*refs):
    value_refs, (weights, inverses, fast, gates), refs = refs[:6], refs[6:10], refs[10:]
    outs, gated = refs[:-1], refs[-1]
    win = mixed(0, value_refs, weights, inverses)
    gate = gates[0].astype(F32)
    spread(((win + fast[...]) * silu(gate)).astype(BF), outs, gated)


def spread(value, outs, held):
    if len(outs) == 1:
        outs[0][...] = value
        return
    held[...] = value
    rows, head = outs[0].shape[0], place()[3]
    outs[0][...] = held[pl.ds(pl.multiple_of(head * rows, rows), rows), :]
    outs[1][...] = held[pl.ds(pl.multiple_of((1 - head) * rows, rows), rows), :]


def update_body(planes, rate, mine, side_in, core_in, diag_in, flipped, norms, *refs):
    (queries, gates, weights, inverses), refs = refs[:4], refs[4:]
    value_refs, outs, (grads, gated) = refs[:6], refs[6:-2], refs[-2:]
    plane, side, core, _ = place()
    part = mine.shape[1]
    for m in range(planes):
        for far in range(2):
            base = ((side if far == 0 else 1 - side) * planes + (plane ^ m)) * part
            where = pl.ds(pl.multiple_of(base, part), part)
            grads[core, where, :] = (mine, side_in)[far][m]
            grads[1 - core, where, :] = (core_in, diag_in)[far][m]
    width = flipped.shape[0] // 3
    half = width // 2
    turned = []
    for b in range(3):
        block = jnp.concatenate(
            [grads[0, b * half : (b + 1) * half, :], grads[1, b * half : (b + 1) * half, :]], 0
        ).astype(F32)
        length = jnp.sqrt(jnp.sum(block * block, keepdims=True))
        turned.append((block * (1.0 / (length + 1e-06))).astype(BF))
    for _ in range(3):
        grams = [dot_nt(y, y) for y in turned]
        lows = [a.astype(BF) for a in grams]
        squares = [dot_nn(a, a) for a in lows]
        mixers = [(B_COEF * a + C_COEF * s).astype(BF) for a, s in zip(grams, squares)]
        turned = [
            (A_COEF * y.astype(F32) + dot_nn(b, y)).astype(BF) for b, y in zip(mixers, turned)
        ]
    fresh = []
    for b in range(3):
        cols = slice(b * width, (b + 1) * width)
        moved = flipped[cols, :] - rate[:1, :1] * turned[b].astype(F32)
        length = jnp.sqrt(jnp.sum(moved * moved, 1, keepdims=True))
        fresh.append((moved * (norms[cols, :] / (length + 1e-06))).astype(BF))
    win = mixed(1, value_refs, weights, inverses)
    x = queries[1]
    g = dot_nt(x, fresh[0])
    u = dot_nt(x, fresh[1])
    hidden = (silu(g) * u).astype(BF)
    fast = dot_nn(hidden, fresh[2])
    gate = gates[1].astype(F32)
    spread(((win + fast) * silu(gate)).astype(BF), outs, gated)


def norm_body(group, own, got, gain, *refs):
    out, held, sems = refs[-3:]
    head = place()[3]
    rows, depth = own.shape
    chunk = rows // 4
    copies = []
    for c in range(4):
        at = slice(c * chunk, (c + 1) * chunk)
        a = own[at, :].astype(F32)
        b = got[at, :].astype(F32)
        low = jnp.where(head == 0, a, b)
        high = jnp.where(head == 0, b, a)
        square = jnp.sum(a * a, -1, keepdims=True) + jnp.sum(b * b, -1, keepdims=True)
        inv = lax.rsqrt(square / (2 * depth) + 1e-06)
        held[at, :depth] = (low * inv * gain[:, :depth]).astype(BF)
        held[at, depth:] = (high * inv * gain[:, depth:]).astype(BF)
        copies.append(pltpu.make_async_copy(held.at[at], out.at[group, at], sems.at[c]))
        copies[-1].start()
    for copy in copies:
        copy.wait()


def finished(group, gated, norm_gain, before):
    total = norm_gain.shape[0]
    if len(gated) == 2:
        own, away = gated
        got = swapped(away, 1, "head")
        rows, depth = own.shape
        earlier = () if before is None else (before,)
        return pl.pallas_call(
            functools.partial(norm_body, group),
            out_shape=jax.ShapeDtypeStruct((2, rows, total), BF),
            in_specs=[
                vmem_spec(),
                vmem_spec(),
                vmem_spec(),
                *([pl.BlockSpec(memory_space=pl.ANY)] * len(earlier)),
            ],
            out_specs=pl.BlockSpec(memory_space=pl.ANY),
            scratch_shapes=[pltpu.VMEM((rows, total), BF), pltpu.SemaphoreType.DMA((4,))],
            input_output_aliases={3: 0} if earlier else {},
            compiler_params=pltpu.CompilerParams(vmem_limit_bytes=VMEM_LIMIT),
            cost_estimate=cost_of(0, 4 * rows * total),
        )(own, got, norm_gain[None, :], *earlier)
    wide = lax.all_to_all(gated[0], "head", split_axis=0, concat_axis=1, tiled=True).astype(F32)
    inv = lax.rsqrt(jnp.mean(wide * wide, -1, keepdims=True) + 1e-06)
    done = (wide * inv * norm_gain).astype(BF)[None]
    return done if before is None else jnp.concatenate([before, done], 0)


def after(value, *needed):
    return lax.optimization_barrier((value,) + needed)[0]


def sent(value, pairs, axis="ctx"):
    return lax.ppermute(value, axis, pairs)


def shards(queries, keys, values, gates, token_rates, fast_init, fast_rate, norm_gain):
    count = lax.axis_size("ctx")
    heads = lax.axis_size("head")
    rows, depth = queries.shape[1], queries.shape[2]
    reach = (WIN - 1) // rows + 1
    planes = count // reach
    if reach != 4 or WIN % rows or planes * reach != count or planes & (planes - 1):
        raise ValueError("unsupported shapes")
    width = fast_init.shape[2] // 3
    half = width // 2
    everyone = range(count)
    local = fast_init[0]
    local_in = swapped(local, 1)
    arrived = [swapped(after(local, local_in) if m == 1 else local, 4 * m) for m in range(1, planes)]
    rates = token_rates.reshape(1, rows)
    keys_in, values_in, rates_in = (swapped(v, 1) for v in (keys, values, rates))
    mine_w = packed(local_in, *arrived)
    other_w = swapped(mine_w, 2)
    own_keys, own_values, own_rates, own_rate = held(keys, values, rates, fast_rate.reshape(1, 1))
    beside_w = [swapped(mine_w, 1), swapped(after(other_w, own_keys), 1)]

    pieces = 2 * planes
    part = -(-3 * half // (16 * pieces)) * 16
    scratch = [pltpu.VMEM((pieces * part, depth), F32)]
    if local.shape[0] % 16:
        scratch.append(pltpu.VMEM((depth, 3 * width), F32))
    send, keep, whole = call(
        functools.partial(gradient_body, planes),
        (mine_w, other_w, *beside_w)
        + (own_keys, own_values, own_rates, keys_in, values_in, rates_in),
        (
            jax.ShapeDtypeStruct((planes * part, depth), BF),
            jax.ShapeDtypeStruct((planes * part, depth), F32),
            jax.ShapeDtypeStruct((depth, 3 * width), BF),
        ),
        scratch=scratch,
        cost=cost_of(2 * 2 * rows * depth * half * 6, 4 * rows * depth * 4),
    )
    got = swapped(send, 2)

    flipped, norms = call(
        weights_body,
        (whole,),
        (
            jax.ShapeDtypeStruct((3 * width, depth), F32),
            jax.ShapeDtypeStruct((3 * width, 1), F32),
        ),
        cost=cost_of(0, depth * width * 3 * 8),
    )
    parts = call(
        functools.partial(side_sum_body, planes),
        (keep, got),
        tuple(jax.ShapeDtypeStruct((part, depth), F32 if m == 0 else BF) for m in range(planes)),
        scratch=(pltpu.VMEM((planes * part, depth), F32),),
        cost=cost_of(0, planes * part * depth * 8),
    )
    partial = [swapped(parts[m], 4 * m) for m in range(1, planes)]
    ring = [(i, (i + reach) % count) for i in everyone]
    far_keys = sent(after(keys, *arrived), ring)
    far_values = sent(after(values, send), ring)
    near_keys = swapped(picked(own_keys, after(far_keys, got)), 2)
    pick_values = picked(own_values, after(far_values, parts[0]))
    near_values = swapped(pick_values, 2)

    total = call(
        plane_sum_body,
        (after(parts[0], pick_values, flipped), *partial),
        jax.ShapeDtypeStruct((part, depth), BF),
        cost=cost_of(0, planes * part * depth * 3),
    )
    far_keys_in = swapped(after(far_keys, total), 1)
    near_keys_in = swapped(after(near_keys, total), 1)
    all_keys = [own_keys, far_keys, near_keys, keys_in, far_keys_in, near_keys_in]
    planes_grad = [
        swapped(total if m < planes - 1 else after(total, far_keys_in, near_keys_in), 4 * m)
        for m in range(1, planes)
    ]

    if heads == 2:
        split = (jax.ShapeDtypeStruct((rows // 2, depth), BF),) * 2
    else:
        split = (jax.ShapeDtypeStruct((rows, depth), BF),)
    attn_cost = cost_of(1000, 1000)
    weights, inverses, fast_first = call(
        scores_body,
        (queries, *all_keys, whole),
        (
            jax.ShapeDtypeStruct((2, reach + 1, rows, rows), BF),
            jax.ShapeDtypeStruct((2, rows, 1), F32),
            jax.ShapeDtypeStruct((rows, depth), F32),
        ),
        cost=attn_cost,
    )
    plane_grad = packed(after(total, inverses), *planes_grad)
    side_grad = swapped(plane_grad, 2)
    far_values_in = swapped(after(far_values, plane_grad), 1)
    near_values_in = swapped(after(near_values, side_grad), 1)
    all_values = [own_values, far_values, near_values, values_in, far_values_in, near_values_in]
    gated_first = call(
        mix_body,
        (*all_values, weights, inverses, fast_first, gates),
        split,
        scratch=(pltpu.VMEM((rows, depth), BF),),
        cost=attn_cost,
    )
    beside_grad = [swapped(plane_grad, 1), swapped(side_grad, 1)]
    grads = [plane_grad, side_grad, *beside_grad]
    done = finished(0, gated_first, norm_gain, None)

    gated_second = call(
        functools.partial(update_body, planes),
        (own_rate, *grads, flipped, norms, queries, gates, weights, inverses, *all_values),
        split,
        scratch=(pltpu.VMEM((2, pieces * part, depth), BF), pltpu.VMEM((rows, depth), BF)),
        cost=cost_of(3e9, 4e6),
    )
    return finished(1, gated_second, norm_gain, done)


def solution(mesh):
    placed = (
        P(None, "ctx", "head"),
        P(None, "ctx", "head"),
        P(None, "ctx", "head"),
        P(None, "ctx", "head"),
        P("ctx", "head"),
        P("head", "ctx", None),
        P("head"),
        P(),
    )
    return jax.shard_map(
        shards,
        mesh=mesh,
        in_specs=placed,
        out_specs=P(None, ("ctx", "head"), None),
        check_vma=False,
    )
```

```python
import functools

import jax
import jax.numpy as jnp
from jax import lax
from jax.experimental import pallas as pl
from jax.experimental.pallas import tpu as pltpu
from jax.sharding import PartitionSpec as P

WIN = 1024
A_COEF = 3.4445
B_COEF = -4.775
C_COEF = 2.0315
BF = jnp.bfloat16
F32 = jnp.float32
VMEM_LIMIT = 32 * 1024 * 1024


def dot_nn(a, b):
    return lax.dot_general(a, b, (((1,), (0,)), ((), ())), preferred_element_type=F32)


def dot_nt(a, b):
    return lax.dot_general(a, b, (((1,), (1,)), ((), ())), preferred_element_type=F32)


def dot_tn(a, b):
    return lax.dot_general(a, b, (((0,), (0,)), ((), ())), preferred_element_type=F32)


def swapped(value, mask, axis="ctx"):
    count = lax.axis_size(axis)
    return lax.ppermute(value, axis, [(i, i ^ mask) for i in range(count)])


def place():
    position = lax.axis_index("ctx")
    return position >> 2, (position >> 1) & 1, position & 1, lax.axis_index("head")


def vmem_spec():
    return pl.BlockSpec(memory_space=pltpu.VMEM)


def call(body, args, outs, scratch=(), cost=None):
    return pl.pallas_call(
        body,
        out_shape=outs,
        in_specs=[vmem_spec()] * len(args),
        out_specs=jax.tree.map(lambda _: vmem_spec(), outs),
        scratch_shapes=list(scratch),
        compiler_params=pltpu.CompilerParams(vmem_limit_bytes=VMEM_LIMIT),
        cost_estimate=cost,
    )(*args)


def cost_of(flops, moved):
    return pl.CostEstimate(flops=int(flops), bytes_accessed=int(moved), transcendentals=0)


def sigmoid(v):
    return 0.5 * jnp.tanh(0.5 * v) + 0.5


def silu(v):
    return v * sigmoid(v)


def hold_body(keys, values, rates, rate, held_keys, held_values, held_rates, held_rate):
    held_keys[...] = keys[...]
    held_values[...] = values[...]
    held_rates[...] = rates[...]
    held_rate[...] = jnp.broadcast_to(rate[...], held_rate.shape)


def held(keys, values, rates, rate):
    outs = tuple(jax.ShapeDtypeStruct(a.shape, a.dtype) for a in (keys, values, rates))
    outs += (jax.ShapeDtypeStruct((8, 128), rate.dtype),)
    return call(hold_body, (keys, values, rates, rate), outs)


def pick_body(own, far, out):
    out[...] = jnp.where(place()[1] == 0, own[...], far[...])


def picked(own, far):
    return call(
        pick_body,
        (own, far),
        jax.ShapeDtypeStruct(own.shape, own.dtype),
        cost=cost_of(0, own.size * 4),
    )


def pack_body(*refs):
    first, *others, second = refs[:-1]
    for m, ref in enumerate((first, second, *others)):
        refs[-1][m] = ref[...]


def packed(first, second, *others):
    pieces = (first, *others, second)
    return pl.pallas_call(
        pack_body,
        out_shape=jax.ShapeDtypeStruct((len(pieces),) + pieces[0].shape, pieces[0].dtype),
        in_specs=[vmem_spec()] * len(pieces),
        out_specs=vmem_spec(),
        compiler_params=pltpu.CompilerParams(vmem_limit_bytes=VMEM_LIMIT),
        cost_estimate=cost_of(0, 4 * len(pieces) * pieces[0].size),
    )(*pieces)


def gradient_body(planes, mine, other, beside_mine, beside_other, *refs):
    (keys, values, rates, keys_in, values_in, rates_in), refs = refs[:6], refs[6:]
    send, keep, whole, total = refs[:4]
    plane, side, core, _ = place()
    rows = mine.shape[1]
    target_ref = refs[4] if len(refs) > 4 else whole
    for m in range(planes):
        holder = 1 - core if m == 0 else core
        for far in range(2):
            block = ((plane ^ m) * 2 + (side if far == 0 else 1 - side)) * 2
            for source, at in (((mine, other)[far], holder), ((beside_mine, beside_other)[far], 1 - holder)):
                where = pl.ds(pl.multiple_of((block + at) * rows, rows), rows)
                target_ref[where, :] = source[m].astype(target_ref.dtype)
    if target_ref is not whole:
        whole[...] = target_ref[...].astype(BF)
    width = whole.shape[1] // 3
    half = width // 2
    parts = [
        whole[:, pl.ds(pl.multiple_of(b * width + core * half, half), half)] for b in range(3)
    ]
    gate_up_w = jnp.concatenate(parts[:2], 1)
    out_w = parts[2]
    first = None
    for key_ref, value_ref, rate in ((keys, values, rates), (keys_in, values_in, rates_in)):
        key_rows = key_ref[0]
        column = jnp.broadcast_to(rate[...], (128, rate.shape[1])).T[:, :1]
        target = (-column * value_ref[0].astype(F32)).astype(BF)
        gate_up = dot_nn(key_rows, gate_up_w)
        g, u = gate_up[:, :half], gate_up[:, half:]
        dh = dot_nn(target, out_w)
        s = sigmoid(g)
        gs = g * s
        hidden = (gs * u).astype(BF)
        dg = dh * u * s * (1.0 + g * (1.0 - s))
        du = dh * gs
        joined = jnp.concatenate([dg, du], 1).astype(BF)
        in_grad = dot_tn(joined, key_rows)
        out_grad = dot_tn(hidden, target)
        first = (in_grad, out_grad) if first is None else (first[0] + in_grad, first[1] + out_grad)
    total[: 2 * half, :] = first[0]
    total[2 * half : 3 * half, :] = first[1]
    if total.shape[0] > 3 * half:
        total[3 * half :, :] = jnp.zeros((total.shape[0] - 3 * half, total.shape[1]), F32)
    part = send.shape[0]
    send[...] = total[pl.ds(pl.multiple_of((1 - side) * part, part), part), :].astype(BF)
    keep[...] = total[pl.ds(pl.multiple_of(side * part, part), part), :]


def side_sum_body(planes, keep, got, *refs):
    outs, total = refs[:planes], refs[planes]
    plane = place()[0]
    total[...] = keep[...] + got[...].astype(F32)
    part = outs[0].shape[0]
    for m in range(planes):
        rows = total[pl.ds(pl.multiple_of((plane ^ m) * part, part), part), :]
        outs[m][...] = rows.astype(outs[m].dtype)


def plane_sum_body(own, *refs):
    total = own[...]
    for ref in refs[:-1]:
        total = total + ref[...].astype(F32)
    refs[-1][...] = total.astype(BF)


def weights_body(whole, flipped, norms):
    width = whole.shape[1] // 3
    for b in range(3):
        cols = slice(b * width, (b + 1) * width)
        turned = whole[:, cols].astype(F32).T
        flipped[cols, :] = turned
        norms[cols, :] = jnp.sqrt(jnp.sum(turned * turned, 1, keepdims=True))


def blocks_of(group, own, far, near, beside, far_beside, diag):
    plane, side, core, _ = place()
    moved = group if group == 0 else jnp.where(plane == 0, 0, group)
    crossed = group if group == 0 else jnp.where((plane == 0) & (side == 0), 0, group)
    return [
        own[group],
        far[moved],
        near[crossed],
        jnp.where(core == 1, beside[group], far_beside[moved]),
        diag[crossed],
    ]


def scores_body(queries, *refs):
    key_refs, whole, (weights, inverses, fast) = refs[:6], refs[6], refs[7:]
    plane, side, core, _ = place()
    later = (plane > 0).astype(jnp.int32)
    side_live, core_live = jnp.maximum(later, side), jnp.maximum(later, core)
    rows, depth = queries.shape[1:]
    scale = depth**-0.5
    row = lax.broadcasted_iota(jnp.int32, (rows, rows), 0)
    col = lax.broadcasted_iota(jnp.int32, (rows, rows), 1)
    for group in range(2):
        q = queries[group]
        scores = []
        lives = [None, later, side_live, core_live, side_live]
        for slot, keys in enumerate(blocks_of(group, *key_refs)):
            s = dot_nt(q, keys) * scale
            allowed = {0: col <= row, 1: col > row}.get(slot)
            if group == 0 and slot:
                alive = jnp.full((rows, rows), lives[slot], jnp.int32) != 0
                allowed = alive if allowed is None else allowed & alive
            scores.append(s if allowed is None else jnp.where(allowed, s, -1e30))
        top = jnp.max(scores[0], -1, keepdims=True)
        for s in scores[1:]:
            top = jnp.maximum(top, jnp.max(s, -1, keepdims=True))
        total = None
        for slot, s in enumerate(scores):
            e = jnp.exp(s - top)
            t = jnp.sum(e, -1, keepdims=True)
            total = t if total is None else total + t
            weights[group, slot] = e.astype(BF)
        inverses[group] = 1.0 / total
    width = whole.shape[1] // 3
    gate_up = dot_nn(queries[0], whole[:, : 2 * width])
    hidden = (silu(gate_up[:, :width]) * gate_up[:, width:]).astype(BF)
    fast[...] = dot_nt(hidden, whole[:, 2 * width :])


def mixed(group, value_refs, weights, inverses):
    out = None
    for slot, values in enumerate(blocks_of(group, *value_refs)):
        o = dot_nn(weights[group, slot], values)
        out = o if out is None else out + o
    return out * inverses[group]


def mix_body(*refs):
    value_refs, (weights, inverses, fast, gates), refs = refs[:6], refs[6:10], refs[10:]
    outs, gated = refs[:-1], refs[-1]
    win = mixed(0, value_refs, weights, inverses)
    gate = gates[0].astype(F32)
    spread(((win + fast[...]) * silu(gate)).astype(BF), outs, gated)


def spread(value, outs, held):
    if len(outs) == 1:
        outs[0][...] = value
        return
    held[...] = value
    rows, head = outs[0].shape[0], place()[3]
    outs[0][...] = held[pl.ds(pl.multiple_of(head * rows, rows), rows), :]
    outs[1][...] = held[pl.ds(pl.multiple_of((1 - head) * rows, rows), rows), :]


def update_body(planes, rate, mine, side_in, core_in, diag_in, flipped, norms, *refs):
    (queries, gates, weights, inverses), refs = refs[:4], refs[4:]
    value_refs, outs, (grads, gated) = refs[:6], refs[6:-2], refs[-2:]
    plane, side, core, _ = place()
    part = mine.shape[1]
    for m in range(planes):
        for far in range(2):
            base = ((side if far == 0 else 1 - side) * planes + (plane ^ m)) * part
            where = pl.ds(pl.multiple_of(base, part), part)
            grads[core, where, :] = (mine, side_in)[far][m]
            grads[1 - core, where, :] = (core_in, diag_in)[far][m]
    width = flipped.shape[0] // 3
    half = width // 2
    turned = []
    for b in range(3):
        block = jnp.concatenate(
            [grads[0, b * half : (b + 1) * half, :], grads[1, b * half : (b + 1) * half, :]], 0
        ).astype(F32)
        length = jnp.sqrt(jnp.sum(block * block, keepdims=True))
        turned.append((block * (1.0 / (length + 1e-06))).astype(BF))
    for _ in range(3):
        grams = [dot_nt(y, y) for y in turned]
        lows = [a.astype(BF) for a in grams]
        squares = [dot_nn(a, a) for a in lows]
        mixers = [(B_COEF * a + C_COEF * s).astype(BF) for a, s in zip(grams, squares)]
        turned = [
            (A_COEF * y.astype(F32) + dot_nn(b, y)).astype(BF) for b, y in zip(mixers, turned)
        ]
    fresh = []
    for b in range(3):
        cols = slice(b * width, (b + 1) * width)
        moved = flipped[cols, :] - rate[:1, :1] * turned[b].astype(F32)
        length = jnp.sqrt(jnp.sum(moved * moved, 1, keepdims=True))
        fresh.append((moved * (norms[cols, :] / (length + 1e-06))).astype(BF))
    win = mixed(1, value_refs, weights, inverses)
    x = queries[1]
    g = dot_nt(x, fresh[0])
    u = dot_nt(x, fresh[1])
    hidden = (silu(g) * u).astype(BF)
    fast = dot_nn(hidden, fresh[2])
    gate = gates[1].astype(F32)
    spread(((win + fast) * silu(gate)).astype(BF), outs, gated)


def norm_body(group, own, got, gain, *refs):
    out, held, sems = refs[-3:]
    head = place()[3]
    rows, depth = own.shape
    chunk = rows // 4
    copies = []
    for c in range(4):
        at = slice(c * chunk, (c + 1) * chunk)
        a = own[at, :].astype(F32)
        b = got[at, :].astype(F32)
        low = jnp.where(head == 0, a, b)
        high = jnp.where(head == 0, b, a)
        square = jnp.sum(a * a, -1, keepdims=True) + jnp.sum(b * b, -1, keepdims=True)
        inv = lax.rsqrt(square / (2 * depth) + 1e-06)
        held[at, :depth] = (low * inv * gain[:, :depth]).astype(BF)
        held[at, depth:] = (high * inv * gain[:, depth:]).astype(BF)
        copies.append(pltpu.make_async_copy(held.at[at], out.at[group, at], sems.at[c]))
        copies[-1].start()
    for copy in copies:
        copy.wait()


def finished(group, gated, norm_gain, before):
    total = norm_gain.shape[0]
    if len(gated) == 2:
        own, away = gated
        got = swapped(away, 1, "head")
        rows, depth = own.shape
        earlier = () if before is None else (before,)
        return pl.pallas_call(
            functools.partial(norm_body, group),
            out_shape=jax.ShapeDtypeStruct((2, rows, total), BF),
            in_specs=[
                vmem_spec(),
                vmem_spec(),
                vmem_spec(),
                *([pl.BlockSpec(memory_space=pl.ANY)] * len(earlier)),
            ],
            out_specs=pl.BlockSpec(memory_space=pl.ANY),
            scratch_shapes=[pltpu.VMEM((rows, total), BF), pltpu.SemaphoreType.DMA((4,))],
            input_output_aliases={3: 0} if earlier else {},
            compiler_params=pltpu.CompilerParams(vmem_limit_bytes=VMEM_LIMIT),
            cost_estimate=cost_of(0, 4 * rows * total),
        )(own, got, norm_gain[None, :], *earlier)
    wide = lax.all_to_all(gated[0], "head", split_axis=0, concat_axis=1, tiled=True).astype(F32)
    inv = lax.rsqrt(jnp.mean(wide * wide, -1, keepdims=True) + 1e-06)
    done = (wide * inv * norm_gain).astype(BF)[None]
    return done if before is None else jnp.concatenate([before, done], 0)


def after(value, *needed):
    return lax.optimization_barrier((value,) + needed)[0]


def sent(value, pairs, axis="ctx"):
    return lax.ppermute(value, axis, pairs)


def shards(queries, keys, values, gates, token_rates, fast_init, fast_rate, norm_gain):
    count = lax.axis_size("ctx")
    heads = lax.axis_size("head")
    rows, depth = queries.shape[1], queries.shape[2]
    reach = (WIN - 1) // rows + 1
    planes = count // reach
    if reach != 4 or WIN % rows or planes * reach != count or planes & (planes - 1):
        raise ValueError("unsupported shapes")
    width = fast_init.shape[2] // 3
    half = width // 2
    everyone = range(count)
    local = fast_init[0]
    local_in = swapped(local, 1)
    arrived = [swapped(after(local, local_in) if m == 1 else local, 4 * m) for m in range(1, planes)]
    rates = token_rates.reshape(1, rows)
    keys_in, values_in, rates_in = (swapped(v, 1) for v in (keys, values, rates))
    mine_w = packed(local_in, *arrived)
    other_w = swapped(mine_w, 2)
    own_keys, own_values, own_rates, own_rate = held(keys, values, rates, fast_rate.reshape(1, 1))
    beside_w = [swapped(mine_w, 1), swapped(after(other_w, own_keys), 1)]

    pieces = 2 * planes
    part = -(-3 * half // (16 * pieces)) * 16
    scratch = [pltpu.VMEM((pieces * part, depth), F32)]
    if local.shape[0] % 16:
        scratch.append(pltpu.VMEM((depth, 3 * width), F32))
    send, keep, whole = call(
        functools.partial(gradient_body, planes),
        (mine_w, other_w, *beside_w)
        + (own_keys, own_values, own_rates, keys_in, values_in, rates_in),
        (
            jax.ShapeDtypeStruct((planes * part, depth), BF),
            jax.ShapeDtypeStruct((planes * part, depth), F32),
            jax.ShapeDtypeStruct((depth, 3 * width), BF),
        ),
        scratch=scratch,
        cost=cost_of(2 * 2 * rows * depth * half * 6, 4 * rows * depth * 4),
    )
    got = swapped(send, 2)

    flipped, norms = call(
        weights_body,
        (whole,),
        (
            jax.ShapeDtypeStruct((3 * width, depth), F32),
            jax.ShapeDtypeStruct((3 * width, 1), F32),
        ),
        cost=cost_of(0, depth * width * 3 * 8),
    )
    parts = call(
        functools.partial(side_sum_body, planes),
        (keep, got),
        tuple(jax.ShapeDtypeStruct((part, depth), F32 if m == 0 else BF) for m in range(planes)),
        scratch=(pltpu.VMEM((planes * part, depth), F32),),
        cost=cost_of(0, planes * part * depth * 8),
    )
    partial = [swapped(parts[m], 4 * m) for m in range(1, planes)]
    ring = [(i, (i + reach) % count) for i in everyone]
    far_keys = sent(after(keys, *arrived), ring)
    far_values = sent(after(values, send), ring)
    near_keys = swapped(picked(own_keys, after(far_keys, got)), 2)
    pick_values = picked(own_values, after(far_values, parts[0]))
    near_values = swapped(pick_values, 2)

    total = call(
        plane_sum_body,
        (after(parts[0], pick_values, flipped), *partial[1:], partial[0]),
        jax.ShapeDtypeStruct((part, depth), BF),
        cost=cost_of(0, planes * part * depth * 3),
    )
    far_keys_in = swapped(after(far_keys, total), 1)
    near_keys_in = swapped(after(near_keys, total), 1)
    all_keys = [own_keys, far_keys, near_keys, keys_in, far_keys_in, near_keys_in]
    planes_grad = [
        swapped(total, 4 * m)
        for m in range(1, planes)
    ]

    if heads == 2:
        split = (jax.ShapeDtypeStruct((rows // 2, depth), BF),) * 2
    else:
        split = (jax.ShapeDtypeStruct((rows, depth), BF),)
    attn_cost = cost_of(1000, 1000)
    weights, inverses, fast_first = call(
        scores_body,
        (queries, *all_keys, whole),
        (
            jax.ShapeDtypeStruct((2, reach + 1, rows, rows), BF),
            jax.ShapeDtypeStruct((2, rows, 1), F32),
            jax.ShapeDtypeStruct((rows, depth), F32),
        ),
        cost=attn_cost,
    )
    plane_grad = packed(after(total, inverses), *planes_grad)
    side_grad = swapped(plane_grad, 2)
    far_values_in = swapped(after(far_values, plane_grad), 1)
    near_values_in = swapped(after(near_values, side_grad), 1)
    all_values = [own_values, far_values, near_values, values_in, far_values_in, near_values_in]
    gated_first = call(
        mix_body,
        (*all_values, weights, inverses, fast_first, gates),
        split,
        scratch=(pltpu.VMEM((rows, depth), BF),),
        cost=attn_cost,
    )
    beside_grad = [swapped(plane_grad, 1), swapped(side_grad, 1)]
    grads = [plane_grad, side_grad, *beside_grad]
    done = finished(0, gated_first, norm_gain, None)

    gated_second = call(
        functools.partial(update_body, planes),
        (own_rate, *grads, flipped, norms, queries, gates, weights, inverses, *all_values),
        split,
        scratch=(pltpu.VMEM((2, pieces * part, depth), BF), pltpu.VMEM((rows, depth), BF)),
        cost=cost_of(3e9, 4e6),
    )
    return finished(1, gated_second, norm_gain, done)


def solution(mesh):
    placed = (
        P(None, "ctx", "head"),
        P(None, "ctx", "head"),
        P(None, "ctx", "head"),
        P(None, "ctx", "head"),
        P("ctx", "head"),
        P("head", "ctx", None),
        P("head"),
        P(),
    )
    return jax.shard_map(
        shards,
        mesh=mesh,
        in_specs=placed,
        out_specs=P(None, ("ctx", "head"), None),
        check_vma=False,
    )
```

```python
import functools

import jax
import jax.numpy as jnp
from jax import lax
from jax.experimental import pallas as pl
from jax.experimental.pallas import tpu as pltpu
from jax.sharding import PartitionSpec as P

WIN = 1024
A_COEF = 3.4445
B_COEF = -4.775
C_COEF = 2.0315
BF = jnp.bfloat16
F32 = jnp.float32
VMEM_LIMIT = 32 * 1024 * 1024


def dot_nn(a, b):
    return lax.dot_general(a, b, (((1,), (0,)), ((), ())), preferred_element_type=F32)


def dot_nt(a, b):
    return lax.dot_general(a, b, (((1,), (1,)), ((), ())), preferred_element_type=F32)


def dot_tn(a, b):
    return lax.dot_general(a, b, (((0,), (0,)), ((), ())), preferred_element_type=F32)


def swapped(value, mask, axis="ctx"):
    count = lax.axis_size(axis)
    return lax.ppermute(value, axis, [(i, i ^ mask) for i in range(count)])


def place():
    position = lax.axis_index("ctx")
    return position >> 2, (position >> 1) & 1, position & 1, lax.axis_index("head")


def vmem_spec():
    return pl.BlockSpec(memory_space=pltpu.VMEM)


def call(body, args, outs, scratch=(), cost=None):
    return pl.pallas_call(
        body,
        out_shape=outs,
        in_specs=[vmem_spec()] * len(args),
        out_specs=jax.tree.map(lambda _: vmem_spec(), outs),
        scratch_shapes=list(scratch),
        compiler_params=pltpu.CompilerParams(vmem_limit_bytes=VMEM_LIMIT),
        cost_estimate=cost,
    )(*args)


def cost_of(flops, moved):
    return pl.CostEstimate(flops=int(flops), bytes_accessed=int(moved), transcendentals=0)


def sigmoid(v):
    return 0.5 * jnp.tanh(0.5 * v) + 0.5


def silu(v):
    return v * sigmoid(v)


def hold_body(keys, values, rates, rate, held_keys, held_values, held_rates, held_rate):
    held_keys[...] = keys[...]
    held_values[...] = values[...]
    held_rates[...] = rates[...]
    held_rate[...] = jnp.broadcast_to(rate[...], held_rate.shape)


def held(keys, values, rates, rate):
    outs = tuple(jax.ShapeDtypeStruct(a.shape, a.dtype) for a in (keys, values, rates))
    outs += (jax.ShapeDtypeStruct((8, 128), rate.dtype),)
    return call(hold_body, (keys, values, rates, rate), outs)


def pick_body(own, far, out):
    out[...] = jnp.where(place()[1] == 0, own[...], far[...])


def picked(own, far):
    return call(
        pick_body,
        (own, far),
        jax.ShapeDtypeStruct(own.shape, own.dtype),
        cost=cost_of(0, own.size * 4),
    )


def pack_body(*refs):
    first, *others, second = refs[:-1]
    for m, ref in enumerate((first, second, *others)):
        refs[-1][m] = ref[...]


def packed(first, second, *others):
    pieces = (first, *others, second)
    return pl.pallas_call(
        pack_body,
        out_shape=jax.ShapeDtypeStruct((len(pieces),) + pieces[0].shape, pieces[0].dtype),
        in_specs=[vmem_spec()] * len(pieces),
        out_specs=vmem_spec(),
        compiler_params=pltpu.CompilerParams(vmem_limit_bytes=VMEM_LIMIT),
        cost_estimate=cost_of(0, 4 * len(pieces) * pieces[0].size),
    )(*pieces)


def gradient_body(planes, mine, other, beside_mine, beside_other, *refs):
    (keys, values, rates, keys_in, values_in, rates_in), refs = refs[:6], refs[6:]
    send, keep, whole, total = refs[:4]
    plane, side, core, _ = place()
    rows = mine.shape[1]
    target_ref = refs[4] if len(refs) > 4 else whole
    for m in range(planes):
        holder = 1 - core if m == 0 else core
        for far in range(2):
            block = ((plane ^ m) * 2 + (side if far == 0 else 1 - side)) * 2
            for source, at in (((mine, other)[far], holder), ((beside_mine, beside_other)[far], 1 - holder)):
                where = pl.ds(pl.multiple_of((block + at) * rows, rows), rows)
                target_ref[where, :] = source[m].astype(target_ref.dtype)
    if target_ref is not whole:
        whole[...] = target_ref[...].astype(BF)
    width = whole.shape[1] // 3
    half = width // 2
    parts = [
        whole[:, pl.ds(pl.multiple_of(b * width + core * half, half), half)] for b in range(3)
    ]
    gate_up_w = jnp.concatenate(parts[:2], 1)
    out_w = parts[2]
    first = None
    for key_ref, value_ref, rate in ((keys, values, rates), (keys_in, values_in, rates_in)):
        key_rows = key_ref[0]
        column = jnp.broadcast_to(rate[...], (128, rate.shape[1])).T[:, :1]
        target = (-column * value_ref[0].astype(F32)).astype(BF)
        gate_up = dot_nn(key_rows, gate_up_w)
        g, u = gate_up[:, :half], gate_up[:, half:]
        dh = dot_nn(target, out_w)
        s = sigmoid(g)
        gs = g * s
        hidden = (gs * u).astype(BF)
        dg = dh * u * s * (1.0 + g * (1.0 - s))
        du = dh * gs
        joined = jnp.concatenate([dg, du], 1).astype(BF)
        in_grad = dot_tn(joined, key_rows)
        out_grad = dot_tn(hidden, target)
        first = (in_grad, out_grad) if first is None else (first[0] + in_grad, first[1] + out_grad)
    total[: 2 * half, :] = first[0]
    total[2 * half : 3 * half, :] = first[1]
    if total.shape[0] > 3 * half:
        total[3 * half :, :] = jnp.zeros((total.shape[0] - 3 * half, total.shape[1]), F32)
    part = send.shape[0]
    send[...] = total[pl.ds(pl.multiple_of((1 - side) * part, part), part), :].astype(BF)
    keep[...] = total[pl.ds(pl.multiple_of(side * part, part), part), :]


def side_sum_body(planes, keep, got, *refs):
    outs, total = refs[:planes], refs[planes]
    plane = place()[0]
    total[...] = keep[...] + got[...].astype(F32)
    part = outs[0].shape[0]
    for m in range(planes):
        rows = total[pl.ds(pl.multiple_of((plane ^ m) * part, part), part), :]
        outs[m][...] = rows.astype(outs[m].dtype)


def plane_sum_body(own, *refs):
    total = own[...]
    for ref in refs[:-1]:
        total = total + ref[...].astype(F32)
    refs[-1][...] = total.astype(BF)


def weights_body(whole, flipped, norms):
    width = whole.shape[1] // 3
    for b in range(3):
        cols = slice(b * width, (b + 1) * width)
        turned = whole[:, cols].astype(F32).T
        flipped[cols, :] = turned
        norms[cols, :] = jnp.sqrt(jnp.sum(turned * turned, 1, keepdims=True))


def blocks_of(group, own, far, near, beside, far_beside, diag):
    plane, side, core, _ = place()
    moved = group if group == 0 else jnp.where(plane == 0, 0, group)
    crossed = group if group == 0 else jnp.where((plane == 0) & (side == 0), 0, group)
    return [
        own[group],
        far[moved],
        near[crossed],
        jnp.where(core == 1, beside[group], far_beside[moved]),
        diag[crossed],
    ]


def scores_body(queries, *refs):
    key_refs, whole, (weights, inverses, fast) = refs[:6], refs[6], refs[7:]
    plane, side, core, _ = place()
    later = (plane > 0).astype(jnp.int32)
    side_live, core_live = jnp.maximum(later, side), jnp.maximum(later, core)
    rows, depth = queries.shape[1:]
    scale = depth**-0.5
    row = lax.broadcasted_iota(jnp.int32, (rows, rows), 0)
    col = lax.broadcasted_iota(jnp.int32, (rows, rows), 1)
    for group in range(2):
        q = queries[group]
        scores = []
        lives = [None, later, side_live, core_live, side_live]
        for slot, keys in enumerate(blocks_of(group, *key_refs)):
            s = dot_nt(q, keys) * scale
            allowed = {0: col <= row, 1: col > row}.get(slot)
            if group == 0 and slot:
                alive = jnp.full((rows, rows), lives[slot], jnp.int32) != 0
                allowed = alive if allowed is None else allowed & alive
            scores.append(s if allowed is None else jnp.where(allowed, s, -1e30))
        top = jnp.max(scores[0], -1, keepdims=True)
        for s in scores[1:]:
            top = jnp.maximum(top, jnp.max(s, -1, keepdims=True))
        total = None
        for slot, s in enumerate(scores):
            e = jnp.exp(s - top)
            t = jnp.sum(e, -1, keepdims=True)
            total = t if total is None else total + t
            weights[group, slot] = e.astype(BF)
        inverses[group] = 1.0 / total
    width = whole.shape[1] // 3
    gate_up = dot_nn(queries[0], whole[:, : 2 * width])
    hidden = (silu(gate_up[:, :width]) * gate_up[:, width:]).astype(BF)
    fast[...] = dot_nt(hidden, whole[:, 2 * width :])


def mixed(group, value_refs, weights, inverses):
    out = None
    for slot, values in enumerate(blocks_of(group, *value_refs)):
        o = dot_nn(weights[group, slot], values)
        out = o if out is None else out + o
    return out * inverses[group]


def mix_body(*refs):
    value_refs, (weights, inverses, fast, gates), refs = refs[:6], refs[6:10], refs[10:]
    outs, gated = refs[:-1], refs[-1]
    win = mixed(0, value_refs, weights, inverses)
    gate = gates[0].astype(F32)
    spread(((win + fast[...]) * silu(gate)).astype(BF), outs, gated)


def spread(value, outs, held):
    if len(outs) == 1:
        outs[0][...] = value
        return
    held[...] = value
    rows, head = outs[0].shape[0], place()[3]
    outs[0][...] = held[pl.ds(pl.multiple_of(head * rows, rows), rows), :]
    outs[1][...] = held[pl.ds(pl.multiple_of((1 - head) * rows, rows), rows), :]


def update_body(planes, rate, mine, side_in, core_in, diag_in, flipped, norms, *refs):
    (queries, gates, weights, inverses), refs = refs[:4], refs[4:]
    value_refs, outs, (grads, gated) = refs[:6], refs[6:-2], refs[-2:]
    plane, side, core, _ = place()
    part = mine.shape[1]
    for m in range(planes):
        for far in range(2):
            base = ((side if far == 0 else 1 - side) * planes + (plane ^ m)) * part
            where = pl.ds(pl.multiple_of(base, part), part)
            grads[core, where, :] = (mine, side_in)[far][m]
            grads[1 - core, where, :] = (core_in, diag_in)[far][m]
    width = flipped.shape[0] // 3
    half = width // 2
    turned = []
    for b in range(3):
        block = jnp.concatenate(
            [grads[0, b * half : (b + 1) * half, :], grads[1, b * half : (b + 1) * half, :]], 0
        ).astype(F32)
        length = jnp.sqrt(jnp.sum(block * block, keepdims=True))
        turned.append((block * (1.0 / (length + 1e-06))).astype(BF))
    def step(ys):
        grams = [dot_nt(y, y) for y in ys]
        lows = [a.astype(BF) for a in grams]
        squares = [dot_nn(a, a) for a in lows]
        mixers = [(B_COEF * a + C_COEF * s).astype(BF) for a, s in zip(grams, squares)]
        return [(A_COEF * y.astype(F32) + dot_nn(b, y)).astype(BF) for b, y in zip(mixers, ys)]

    def renewed(b, y):
        cols = slice(b * width, (b + 1) * width)
        moved = flipped[cols, :] - rate[:1, :1] * y.astype(F32)
        length = jnp.sqrt(jnp.sum(moved * moved, 1, keepdims=True))
        return (moved * (norms[cols, :] / (length + 1e-06))).astype(BF)

    gate_up, last = step(turned[:2]), turned[2:]
    for _ in range(2):
        *gate_up, behind = step(gate_up + last)
        last = [behind]
    gate_w, up_w = renewed(0, gate_up[0]), renewed(1, gate_up[1])
    x = queries[1]
    g = dot_nt(x, gate_w)
    u = dot_nt(x, up_w)
    out_w = renewed(2, step(last)[0])
    win = mixed(1, value_refs, weights, inverses)
    hidden = (silu(g) * u).astype(BF)
    fast = dot_nn(hidden, out_w)
    gate = gates[1].astype(F32)
    spread(((win + fast) * silu(gate)).astype(BF), outs, gated)


def norm_body(group, own, got, gain, *refs):
    out, held, sems = refs[-3:]
    head = place()[3]
    rows, depth = own.shape
    chunk = rows // 4
    copies = []
    for c in range(4):
        at = slice(c * chunk, (c + 1) * chunk)
        a = own[at, :].astype(F32)
        b = got[at, :].astype(F32)
        low = jnp.where(head == 0, a, b)
        high = jnp.where(head == 0, b, a)
        square = jnp.sum(a * a, -1, keepdims=True) + jnp.sum(b * b, -1, keepdims=True)
        inv = lax.rsqrt(square / (2 * depth) + 1e-06)
        held[at, :depth] = (low * inv * gain[:, :depth]).astype(BF)
        held[at, depth:] = (high * inv * gain[:, depth:]).astype(BF)
        copies.append(pltpu.make_async_copy(held.at[at], out.at[group, at], sems.at[c]))
        copies[-1].start()
    for copy in copies:
        copy.wait()


def finished(group, gated, norm_gain, before):
    total = norm_gain.shape[0]
    if len(gated) == 2:
        own, away = gated
        got = swapped(away, 1, "head")
        rows, depth = own.shape
        earlier = () if before is None else (before,)
        return pl.pallas_call(
            functools.partial(norm_body, group),
            out_shape=jax.ShapeDtypeStruct((2, rows, total), BF),
            in_specs=[
                vmem_spec(),
                vmem_spec(),
                vmem_spec(),
                *([pl.BlockSpec(memory_space=pl.ANY)] * len(earlier)),
            ],
            out_specs=pl.BlockSpec(memory_space=pl.ANY),
            scratch_shapes=[pltpu.VMEM((rows, total), BF), pltpu.SemaphoreType.DMA((4,))],
            input_output_aliases={3: 0} if earlier else {},
            compiler_params=pltpu.CompilerParams(vmem_limit_bytes=VMEM_LIMIT),
            cost_estimate=cost_of(0, 4 * rows * total),
        )(own, got, norm_gain[None, :], *earlier)
    wide = lax.all_to_all(gated[0], "head", split_axis=0, concat_axis=1, tiled=True).astype(F32)
    inv = lax.rsqrt(jnp.mean(wide * wide, -1, keepdims=True) + 1e-06)
    done = (wide * inv * norm_gain).astype(BF)[None]
    return done if before is None else jnp.concatenate([before, done], 0)


def after(value, *needed):
    return lax.optimization_barrier((value,) + needed)[0]


def sent(value, pairs, axis="ctx"):
    return lax.ppermute(value, axis, pairs)


def shards(queries, keys, values, gates, token_rates, fast_init, fast_rate, norm_gain):
    count = lax.axis_size("ctx")
    heads = lax.axis_size("head")
    rows, depth = queries.shape[1], queries.shape[2]
    reach = (WIN - 1) // rows + 1
    planes = count // reach
    if reach != 4 or WIN % rows or planes * reach != count or planes & (planes - 1):
        raise ValueError("unsupported shapes")
    width = fast_init.shape[2] // 3
    half = width // 2
    everyone = range(count)
    local = fast_init[0]
    local_in = swapped(local, 1)
    arrived = [swapped(after(local, local_in) if m == 1 else local, 4 * m) for m in range(1, planes)]
    rates = token_rates.reshape(1, rows)
    keys_in, values_in, rates_in = (swapped(v, 1) for v in (keys, values, rates))
    mine_w = packed(local_in, *arrived)
    other_w = swapped(mine_w, 2)
    own_keys, own_values, own_rates, own_rate = held(keys, values, rates, fast_rate.reshape(1, 1))
    beside_w = [swapped(mine_w, 1), swapped(after(other_w, own_keys), 1)]

    pieces = 2 * planes
    part = -(-3 * half // (16 * pieces)) * 16
    scratch = [pltpu.VMEM((pieces * part, depth), F32)]
    if local.shape[0] % 16:
        scratch.append(pltpu.VMEM((depth, 3 * width), F32))
    send, keep, whole = call(
        functools.partial(gradient_body, planes),
        (mine_w, other_w, *beside_w)
        + (own_keys, own_values, own_rates, keys_in, values_in, rates_in),
        (
            jax.ShapeDtypeStruct((planes * part, depth), BF),
            jax.ShapeDtypeStruct((planes * part, depth), F32),
            jax.ShapeDtypeStruct((depth, 3 * width), BF),
        ),
        scratch=scratch,
        cost=cost_of(2 * 2 * rows * depth * half * 6, 4 * rows * depth * 4),
    )
    got = swapped(send, 2)

    flipped, norms = call(
        weights_body,
        (whole,),
        (
            jax.ShapeDtypeStruct((3 * width, depth), F32),
            jax.ShapeDtypeStruct((3 * width, 1), F32),
        ),
        cost=cost_of(0, depth * width * 3 * 8),
    )
    parts = call(
        functools.partial(side_sum_body, planes),
        (keep, got),
        tuple(jax.ShapeDtypeStruct((part, depth), F32 if m == 0 else BF) for m in range(planes)),
        scratch=(pltpu.VMEM((planes * part, depth), F32),),
        cost=cost_of(0, planes * part * depth * 8),
    )
    partial = [swapped(parts[m], 4 * m) for m in range(1, planes)]
    ring = [(i, (i + reach) % count) for i in everyone]
    far_keys = sent(after(keys, *arrived), ring)
    far_values = sent(after(values, send), ring)
    near_keys = swapped(picked(own_keys, after(far_keys, got)), 2)
    pick_values = picked(own_values, after(far_values, parts[0]))
    near_values = swapped(pick_values, 2)

    total = call(
        plane_sum_body,
        (after(parts[0], pick_values, flipped), *partial[1:], partial[0]),
        jax.ShapeDtypeStruct((part, depth), BF),
        cost=cost_of(0, planes * part * depth * 3),
    )
    far_keys_in = swapped(after(far_keys, total), 1)
    near_keys_in = swapped(after(near_keys, total), 1)
    all_keys = [own_keys, far_keys, near_keys, keys_in, far_keys_in, near_keys_in]
    planes_grad = [
        swapped(total, 4 * m)
        for m in range(1, planes)
    ]

    if heads == 2:
        split = (jax.ShapeDtypeStruct((rows // 2, depth), BF),) * 2
    else:
        split = (jax.ShapeDtypeStruct((rows, depth), BF),)
    attn_cost = cost_of(1000, 1000)
    weights, inverses, fast_first = call(
        scores_body,
        (queries, *all_keys, whole),
        (
            jax.ShapeDtypeStruct((2, reach + 1, rows, rows), BF),
            jax.ShapeDtypeStruct((2, rows, 1), F32),
            jax.ShapeDtypeStruct((rows, depth), F32),
        ),
        cost=attn_cost,
    )
    plane_grad = packed(after(total, inverses), *planes_grad)
    side_grad = swapped(plane_grad, 2)
    far_values_in = swapped(after(far_values, plane_grad), 1)
    near_values_in = swapped(after(near_values, side_grad), 1)
    all_values = [own_values, far_values, near_values, values_in, far_values_in, near_values_in]
    gated_first = call(
        mix_body,
        (*all_values, weights, inverses, fast_first, gates),
        split,
        scratch=(pltpu.VMEM((rows, depth), BF),),
        cost=attn_cost,
    )
    beside_grad = [swapped(plane_grad, 1), swapped(side_grad, 1)]
    grads = [plane_grad, side_grad, *beside_grad]
    done = finished(0, gated_first, norm_gain, None)

    gated_second = call(
        functools.partial(update_body, planes),
        (own_rate, *grads, flipped, norms, queries, gates, weights, inverses, *all_values),
        split,
        scratch=(pltpu.VMEM((2, pieces * part, depth), BF), pltpu.VMEM((rows, depth), BF)),
        cost=cost_of(3e9, 4e6),
    )
    return finished(1, gated_second, norm_gain, done)


def solution(mesh):
    placed = (
        P(None, "ctx", "head"),
        P(None, "ctx", "head"),
        P(None, "ctx", "head"),
        P(None, "ctx", "head"),
        P("ctx", "head"),
        P("head", "ctx", None),
        P("head"),
        P(),
    )
    return jax.shard_map(
        shards,
        mesh=mesh,
        in_specs=placed,
        out_specs=P(None, ("ctx", "head"), None),
        check_vma=False,
    )
```

```python
import functools

import jax
import jax.numpy as jnp
from jax import lax
from jax.experimental import pallas as pl
from jax.experimental.pallas import tpu as pltpu
from jax.sharding import PartitionSpec as P

WIN = 1024
A_COEF = 3.4445
B_COEF = -4.775
C_COEF = 2.0315
BF = jnp.bfloat16
F32 = jnp.float32
VMEM_LIMIT = 32 * 1024 * 1024


def dot_nn(a, b):
    return lax.dot_general(a, b, (((1,), (0,)), ((), ())), preferred_element_type=F32)


def dot_nt(a, b):
    return lax.dot_general(a, b, (((1,), (1,)), ((), ())), preferred_element_type=F32)


def dot_tn(a, b):
    return lax.dot_general(a, b, (((0,), (0,)), ((), ())), preferred_element_type=F32)


def swapped(value, mask, axis="ctx"):
    count = lax.axis_size(axis)
    return lax.ppermute(value, axis, [(i, i ^ mask) for i in range(count)])


def place():
    position = lax.axis_index("ctx")
    return position >> 2, (position >> 1) & 1, position & 1, lax.axis_index("head")


def vmem_spec():
    return pl.BlockSpec(memory_space=pltpu.VMEM)


def call(body, args, outs, scratch=(), cost=None):
    return pl.pallas_call(
        body,
        out_shape=outs,
        in_specs=[vmem_spec()] * len(args),
        out_specs=jax.tree.map(lambda _: vmem_spec(), outs),
        scratch_shapes=list(scratch),
        compiler_params=pltpu.CompilerParams(vmem_limit_bytes=VMEM_LIMIT),
        cost_estimate=cost,
    )(*args)


def cost_of(flops, moved):
    return pl.CostEstimate(flops=int(flops), bytes_accessed=int(moved), transcendentals=0)


def sigmoid(v):
    return 0.5 * jnp.tanh(0.5 * v) + 0.5


def silu(v):
    return v * sigmoid(v)


def hold_body(keys, values, rates, rate, held_keys, held_values, held_rates, held_rate):
    held_keys[...] = keys[...]
    held_values[...] = values[...]
    held_rates[...] = rates[...]
    held_rate[...] = jnp.broadcast_to(rate[...], held_rate.shape)


def held(keys, values, rates, rate):
    outs = tuple(jax.ShapeDtypeStruct(a.shape, a.dtype) for a in (keys, values, rates))
    outs += (jax.ShapeDtypeStruct((8, 128), rate.dtype),)
    return call(hold_body, (keys, values, rates, rate), outs)


def pick_body(own, far, out):
    out[...] = jnp.where(place()[1] == 0, own[...], far[...])


def picked(own, far):
    return call(
        pick_body,
        (own, far),
        jax.ShapeDtypeStruct(own.shape, own.dtype),
        cost=cost_of(0, own.size * 4),
    )


def pack_body(*refs):
    first, *others, second = refs[:-1]
    for m, ref in enumerate((first, second, *others)):
        refs[-1][m] = ref[...]


def packed(first, second, *others):
    pieces = (first, *others, second)
    return pl.pallas_call(
        pack_body,
        out_shape=jax.ShapeDtypeStruct((len(pieces),) + pieces[0].shape, pieces[0].dtype),
        in_specs=[vmem_spec()] * len(pieces),
        out_specs=vmem_spec(),
        compiler_params=pltpu.CompilerParams(vmem_limit_bytes=VMEM_LIMIT),
        cost_estimate=cost_of(0, 4 * len(pieces) * pieces[0].size),
    )(*pieces)


def gradient_body(planes, mine, other, beside_mine, beside_other, *refs):
    (keys, values, rates, keys_in, values_in, rates_in), refs = refs[:6], refs[6:]
    send, keep, whole, total = refs[:4]
    plane, side, core, _ = place()
    rows = mine.shape[1]
    target_ref = refs[4] if len(refs) > 4 else whole
    for m in range(planes):
        holder = 1 - core if m == 0 else core
        for far in range(2):
            block = ((plane ^ m) * 2 + (side if far == 0 else 1 - side)) * 2
            for source, at in (((mine, other)[far], holder), ((beside_mine, beside_other)[far], 1 - holder)):
                where = pl.ds(pl.multiple_of((block + at) * rows, rows), rows)
                target_ref[where, :] = source[m].astype(target_ref.dtype)
    if target_ref is not whole:
        whole[...] = target_ref[...].astype(BF)
    width = whole.shape[1] // 3
    half = width // 2
    parts = [
        whole[:, pl.ds(pl.multiple_of(b * width + core * half, half), half)] for b in range(3)
    ]
    gate_up_w = jnp.concatenate(parts[:2], 1)
    out_w = parts[2]
    first = None
    for key_ref, value_ref, rate in ((keys, values, rates), (keys_in, values_in, rates_in)):
        key_rows = key_ref[0]
        column = jnp.broadcast_to(rate[...], (128, rate.shape[1])).T[:, :1]
        target = (-column * value_ref[0].astype(F32)).astype(BF)
        gate_up = dot_nn(key_rows, gate_up_w)
        g, u = gate_up[:, :half], gate_up[:, half:]
        dh = dot_nn(target, out_w)
        s = sigmoid(g)
        gs = g * s
        hidden = (gs * u).astype(BF)
        dg = dh * u * s * (1.0 + g * (1.0 - s))
        du = dh * gs
        joined = jnp.concatenate([dg, du], 1).astype(BF)
        in_grad = dot_tn(joined, key_rows)
        out_grad = dot_tn(hidden, target)
        first = (in_grad, out_grad) if first is None else (first[0] + in_grad, first[1] + out_grad)
    total[: 2 * half, :] = first[0]
    total[2 * half : 3 * half, :] = first[1]
    if total.shape[0] > 3 * half:
        total[3 * half :, :] = jnp.zeros((total.shape[0] - 3 * half, total.shape[1]), F32)
    part = send.shape[0]
    send[...] = total[pl.ds(pl.multiple_of((1 - side) * part, part), part), :].astype(BF)
    keep[...] = total[pl.ds(pl.multiple_of(side * part, part), part), :]


def side_sum_body(planes, keep, got, *refs):
    outs, total = refs[:planes], refs[planes]
    plane = place()[0]
    total[...] = keep[...] + got[...].astype(F32)
    part = outs[0].shape[0]
    for m in range(planes):
        rows = total[pl.ds(pl.multiple_of((plane ^ m) * part, part), part), :]
        outs[m][...] = rows.astype(outs[m].dtype)


def plane_sum_body(own, *refs):
    total = own[...]
    for ref in refs[:-1]:
        total = total + ref[...].astype(F32)
    refs[-1][...] = total.astype(BF)


def weights_body(whole, flipped, norms):
    width = whole.shape[1] // 3
    for b in range(3):
        cols = slice(b * width, (b + 1) * width)
        turned = whole[:, cols].astype(F32).T
        flipped[cols, :] = turned
        norms[cols, :] = jnp.sqrt(jnp.sum(turned * turned, 1, keepdims=True))


def blocks_of(group, own, far, near, beside, far_beside, diag):
    plane, side, core, _ = place()
    moved = group if group == 0 else jnp.where(plane == 0, 0, group)
    crossed = group if group == 0 else jnp.where((plane == 0) & (side == 0), 0, group)
    return [
        own[group],
        far[moved],
        near[crossed],
        jnp.where(core == 1, beside[group], far_beside[moved]),
        diag[crossed],
    ]


def scores_body(queries, *refs):
    key_refs, whole, (weights, inverses, fast) = refs[:6], refs[6], refs[7:]
    plane, side, core, _ = place()
    later = (plane > 0).astype(jnp.int32)
    side_live, core_live = jnp.maximum(later, side), jnp.maximum(later, core)
    rows, depth = queries.shape[1:]
    scale = depth**-0.5
    row = lax.broadcasted_iota(jnp.int32, (rows, rows), 0)
    col = lax.broadcasted_iota(jnp.int32, (rows, rows), 1)
    for group in range(2):
        q = queries[group]
        scores = []
        lives = [None, later, side_live, core_live, side_live]
        for slot, keys in enumerate(blocks_of(group, *key_refs)):
            s = dot_nt(q, keys) * scale
            allowed = {0: col <= row, 1: col > row}.get(slot)
            if group == 0 and slot:
                alive = jnp.full((rows, rows), lives[slot], jnp.int32) != 0
                allowed = alive if allowed is None else allowed & alive
            scores.append(s if allowed is None else jnp.where(allowed, s, -1e30))
        top = jnp.max(scores[0], -1, keepdims=True)
        for s in scores[1:]:
            top = jnp.maximum(top, jnp.max(s, -1, keepdims=True))
        total = None
        for slot, s in enumerate(scores):
            e = jnp.exp(s - top)
            t = jnp.sum(e, -1, keepdims=True)
            total = t if total is None else total + t
            weights[group, slot] = e.astype(BF)
        inverses[group] = 1.0 / total
    width = whole.shape[1] // 3
    gate_up = dot_nn(queries[0], whole[:, : 2 * width])
    hidden = (silu(gate_up[:, :width]) * gate_up[:, width:]).astype(BF)
    fast[...] = dot_nt(hidden, whole[:, 2 * width :])


def mixed(group, value_refs, weights, inverses):
    out = None
    for slot, values in enumerate(blocks_of(group, *value_refs)):
        o = dot_nn(weights[group, slot], values)
        out = o if out is None else out + o
    return out * inverses[group]


def mix_body(*refs):
    value_refs, (weights, inverses, fast, gates), refs = refs[:6], refs[6:10], refs[10:]
    outs, gated = refs[:-1], refs[-1]
    win = mixed(0, value_refs, weights, inverses)
    gate = gates[0].astype(F32)
    spread(((win + fast[...]) * silu(gate)).astype(BF), outs, gated)


def spread(value, outs, held):
    if len(outs) == 1:
        outs[0][...] = value
        return
    held[...] = value
    rows, head = outs[0].shape[0], place()[3]
    outs[0][...] = held[pl.ds(pl.multiple_of(head * rows, rows), rows), :]
    outs[1][...] = held[pl.ds(pl.multiple_of((1 - head) * rows, rows), rows), :]


def update_body(planes, rate, mine, side_in, core_in, diag_in, flipped, norms, *refs):
    (queries, gates, weights, inverses), refs = refs[:4], refs[4:]
    value_refs, outs, (grads, gated) = refs[:6], refs[6:-2], refs[-2:]
    plane, side, core, _ = place()
    part = mine.shape[1]
    for m in range(planes):
        for far in range(2):
            base = ((side if far == 0 else 1 - side) * planes + (plane ^ m)) * part
            where = pl.ds(pl.multiple_of(base, part), part)
            grads[core, where, :] = (mine, side_in)[far][m]
            grads[1 - core, where, :] = (core_in, diag_in)[far][m]
    width = flipped.shape[0] // 3
    half = width // 2
    turned = []
    for b in range(3):
        block = jnp.concatenate(
            [grads[0, b * half : (b + 1) * half, :], grads[1, b * half : (b + 1) * half, :]], 0
        ).astype(F32)
        length = jnp.sqrt(jnp.sum(block * block, keepdims=True))
        turned.append((block * (1.0 / (length + 1e-06))).astype(BF))
    for _ in range(3):
        grams = [dot_nt(y, y) for y in turned]
        lows = [a.astype(BF) for a in grams]
        squares = [dot_nn(a, a) for a in lows]
        mixers = [(B_COEF * a + C_COEF * s).astype(BF) for a, s in zip(grams, squares)]
        turned = [
            (A_COEF * y.astype(F32) + dot_nn(b, y)).astype(BF) for b, y in zip(mixers, turned)
        ]
    fresh = []
    for b in range(3):
        cols = slice(b * width, (b + 1) * width)
        moved = flipped[cols, :] - rate[:1, :1] * turned[b].astype(F32)
        length = jnp.sqrt(jnp.sum(moved * moved, 1, keepdims=True))
        fresh.append((moved * (norms[cols, :] / (length + 1e-06))).astype(BF))
    win = mixed(1, value_refs, weights, inverses)
    x = queries[1]
    g = dot_nt(x, fresh[0])
    u = dot_nt(x, fresh[1])
    hidden = (silu(g) * u).astype(BF)
    fast = dot_nn(hidden, fresh[2])
    gate = gates[1].astype(F32)
    spread(((win + fast) * silu(gate)).astype(BF), outs, gated)


def norm_body(group, own, got, gain, *refs):
    out, held, sems = refs[-3:]
    head = place()[3]
    rows, depth = own.shape
    chunk = rows // 4
    copies = []
    for c in range(4):
        at = slice(c * chunk, (c + 1) * chunk)
        a = own[at, :].astype(F32)
        b = got[at, :].astype(F32)
        low = jnp.where(head == 0, a, b)
        high = jnp.where(head == 0, b, a)
        square = jnp.sum(a * a, -1, keepdims=True) + jnp.sum(b * b, -1, keepdims=True)
        inv = lax.rsqrt(square / (2 * depth) + 1e-06)
        held[at, :depth] = (low * inv * gain[:, :depth]).astype(BF)
        held[at, depth:] = (high * inv * gain[:, depth:]).astype(BF)
        copies.append(pltpu.make_async_copy(held.at[at], out.at[group, at], sems.at[c]))
        copies[-1].start()
    for copy in copies:
        copy.wait()


def finished(group, gated, norm_gain, before):
    total = norm_gain.shape[0]
    if len(gated) == 2:
        own, away = gated
        got = swapped(away, 1, "head")
        rows, depth = own.shape
        earlier = () if before is None else (before,)
        return pl.pallas_call(
            functools.partial(norm_body, group),
            out_shape=jax.ShapeDtypeStruct((2, rows, total), BF),
            in_specs=[
                vmem_spec(),
                vmem_spec(),
                vmem_spec(),
                *([pl.BlockSpec(memory_space=pl.ANY)] * len(earlier)),
            ],
            out_specs=pl.BlockSpec(memory_space=pl.ANY),
            scratch_shapes=[pltpu.VMEM((rows, total), BF), pltpu.SemaphoreType.DMA((4,))],
            input_output_aliases={3: 0} if earlier else {},
            compiler_params=pltpu.CompilerParams(vmem_limit_bytes=VMEM_LIMIT),
            cost_estimate=cost_of(0, 4 * rows * total),
        )(own, got, norm_gain[None, :], *earlier)
    wide = lax.all_to_all(gated[0], "head", split_axis=0, concat_axis=1, tiled=True).astype(F32)
    inv = lax.rsqrt(jnp.mean(wide * wide, -1, keepdims=True) + 1e-06)
    done = (wide * inv * norm_gain).astype(BF)[None]
    return done if before is None else jnp.concatenate([before, done], 0)


def after(value, *needed):
    return lax.optimization_barrier((value,) + needed)[0]


def sent(value, pairs, axis="ctx"):
    return lax.ppermute(value, axis, pairs)


def shards(queries, keys, values, gates, token_rates, fast_init, fast_rate, norm_gain):
    count = lax.axis_size("ctx")
    heads = lax.axis_size("head")
    rows, depth = queries.shape[1], queries.shape[2]
    reach = (WIN - 1) // rows + 1
    planes = count // reach
    if reach != 4 or WIN % rows or planes * reach != count or planes & (planes - 1):
        raise ValueError("unsupported shapes")
    width = fast_init.shape[2] // 3
    half = width // 2
    everyone = range(count)
    local = fast_init[0]
    local_in = swapped(local, 1)
    arrived = [swapped(after(local, local_in) if m == 1 else local, 4 * m) for m in range(1, planes)]
    rates = token_rates.reshape(1, rows)
    keys_in, values_in, rates_in = (swapped(v, 1) for v in (keys, values, rates))
    mine_w = packed(local_in, *arrived)
    other_w = swapped(mine_w, 2)
    own_keys, own_values, own_rates, own_rate = held(keys, values, rates, fast_rate.reshape(1, 1))
    beside_w = [swapped(mine_w, 1), swapped(after(other_w, own_keys), 1)]

    pieces = 2 * planes
    part = -(-3 * half // (16 * pieces)) * 16
    scratch = [pltpu.VMEM((pieces * part, depth), F32)]
    if local.shape[0] % 16:
        scratch.append(pltpu.VMEM((depth, 3 * width), F32))
    send, keep, whole = call(
        functools.partial(gradient_body, planes),
        (mine_w, other_w, *beside_w)
        + (own_keys, own_values, own_rates, keys_in, values_in, rates_in),
        (
            jax.ShapeDtypeStruct((planes * part, depth), BF),
            jax.ShapeDtypeStruct((planes * part, depth), F32),
            jax.ShapeDtypeStruct((depth, 3 * width), BF),
        ),
        scratch=scratch,
        cost=cost_of(2 * 2 * rows * depth * half * 6, 4 * rows * depth * 4),
    )
    got = swapped(send, 2)

    flipped, norms = call(
        weights_body,
        (whole,),
        (
            jax.ShapeDtypeStruct((3 * width, depth), F32),
            jax.ShapeDtypeStruct((3 * width, 1), F32),
        ),
        cost=cost_of(0, depth * width * 3 * 8),
    )
    parts = call(
        functools.partial(side_sum_body, planes),
        (keep, got),
        tuple(jax.ShapeDtypeStruct((part, depth), F32 if m == 0 else BF) for m in range(planes)),
        scratch=(pltpu.VMEM((planes * part, depth), F32),),
        cost=cost_of(0, planes * part * depth * 8),
    )
    partial = [swapped(parts[m], 4 * m) for m in range(1, planes)]
    ring = [(i, (i + reach) % count) for i in everyone]
    far_keys = sent(after(keys, *arrived), ring)
    far_values = sent(after(values, other_w), ring)
    near_keys = swapped(picked(own_keys, after(far_keys, got)), 2)
    pick_values = picked(own_values, after(far_values, parts[0]))
    near_values = swapped(pick_values, 2)

    total = call(
        plane_sum_body,
        (after(parts[0], pick_values, flipped), *partial[1:], partial[0]),
        jax.ShapeDtypeStruct((part, depth), BF),
        cost=cost_of(0, planes * part * depth * 3),
    )
    far_keys_in = swapped(after(far_keys, total), 1)
    near_keys_in = swapped(after(near_keys, total), 1)
    all_keys = [own_keys, far_keys, near_keys, keys_in, far_keys_in, near_keys_in]
    planes_grad = [
        swapped(total, 4 * m)
        for m in range(1, planes)
    ]

    if heads == 2:
        split = (jax.ShapeDtypeStruct((rows // 2, depth), BF),) * 2
    else:
        split = (jax.ShapeDtypeStruct((rows, depth), BF),)
    attn_cost = cost_of(1000, 1000)
    weights, inverses, fast_first = call(
        scores_body,
        (queries, *all_keys, whole),
        (
            jax.ShapeDtypeStruct((2, reach + 1, rows, rows), BF),
            jax.ShapeDtypeStruct((2, rows, 1), F32),
            jax.ShapeDtypeStruct((rows, depth), F32),
        ),
        cost=attn_cost,
    )
    plane_grad = packed(after(total, inverses), *planes_grad)
    side_grad = swapped(plane_grad, 2)
    far_values_in = swapped(after(far_values, plane_grad), 1)
    near_values_in = swapped(after(near_values, side_grad), 1)
    all_values = [own_values, far_values, near_values, values_in, far_values_in, near_values_in]
    gated_first = call(
        mix_body,
        (*all_values, weights, inverses, fast_first, gates),
        split,
        scratch=(pltpu.VMEM((rows, depth), BF),),
        cost=attn_cost,
    )
    beside_grad = [swapped(plane_grad, 1), swapped(side_grad, 1)]
    grads = [plane_grad, side_grad, *beside_grad]
    done = finished(0, gated_first, norm_gain, None)

    gated_second = call(
        functools.partial(update_body, planes),
        (own_rate, *grads, flipped, norms, queries, gates, weights, inverses, *all_values),
        split,
        scratch=(pltpu.VMEM((2, pieces * part, depth), BF), pltpu.VMEM((rows, depth), BF)),
        cost=cost_of(3e9, 4e6),
    )
    return finished(1, gated_second, norm_gain, done)


def solution(mesh):
    placed = (
        P(None, "ctx", "head"),
        P(None, "ctx", "head"),
        P(None, "ctx", "head"),
        P(None, "ctx", "head"),
        P("ctx", "head"),
        P("head", "ctx", None),
        P("head"),
        P(),
    )
    return jax.shard_map(
        shards,
        mesh=mesh,
        in_specs=placed,
        out_specs=P(None, ("ctx", "head"), None),
        check_vma=False,
    )
```
